128 devices in a mesh: wrap: 8 (over z_lo, y), span: 16 (over x, z_hi, core).
Axes of the slice: x: 4, y: 4, z: 4 (z_hi: 2, z_lo: 2; z = z_hi * 2 + z_lo), core: 2. Of those that a mesh axis runs over, the one named last changes fastest.
Arguments:
- cgrid_state: float32 [5, 256, 256, 256], P(None, 'span', 'wrap'), as said below
- cgrid_metric: float32 [3, 256, 256, 256], P(None, 'span', 'wrap'), may hold values from 0.5 to 2
- flap_state: float32 [5, 256, 96, 512], P(None, 'span', 'wrap'), as said below
- flap_metric: float32 [3, 256, 96, 512], P(None, 'span', 'wrap'), may hold values from 0.5 to 2
- iblank: int32 [256, 96, 512], P('span', 'wrap'), may hold values from 0 to 1
- fringe_from: int32 [256, 96, 512], P('span', 'wrap'), may hold values from 0 to 8191
- donor_cell: int32 [128, 8, 1024], P(('wrap', 'span')), may hold values from 0 to 118574
- donor_frac: float32 [128, 8, 3, 1024], P(('wrap', 'span')), may hold values from 0 to 1
Outputs:
- cgrid_rate: float32 [5, 256, 256, 256], P(None, 'span', 'wrap')
- flap_rate: float32 [5, 256, 96, 512], P(None, 'span', 'wrap')
The draws below stay inside these ranges and needn't reach their ends.
Inputs may be any that keep to these rules, and one draw needn't show every extreme that they name: `cgrid_state`: component 0 (density) lies between 0.5 and 2. `flap_state`: component 0 (density) lies between 0.5 and 2.
All inputs are finite; a program needn't handle non-finite values.
Results may differ from the reference program's by a relative error of at most 0.0003.
Values sent between devices are 32-bit elements; how exact they have to be, the bound alone decides.
No kernel may reach another device: no remote copies, remote signals or barrier semaphores. Data moves between devices by JAX's collectives and lax.ppermute only.
A program may use at most 256 MiB of HBM per device.

```python
import math
import jax
import jax.numpy as jnp
from jax import lax

CI = 32
CK = 16
NJ = 256
FI = 512
FJD = 12
SLOTS = 1024
NI = 256
NK = 256
FJ = 96
N_WRAP = 8
N_SPAN = 16
DEVICES = 128


def fluid_state(key, span_len, first_len, second_len):
    dens_key, moment_key, energy_key = jax.random.split(key, 3)
    extent = (span_len, first_len, second_len)
    density = jnp.exp(jax.random.uniform(dens_key, extent, jnp.float32, math.log(0.5), math.log(2.0)))
    momentum = 0.6 * jax.random.truncated_normal(moment_key, -4.0, 4.0, (3,) + extent, jnp.float32)
    energy = jax.random.uniform(energy_key, extent, jnp.float32, 1.5, 3.0)
    return jnp.concatenate([density[None], momentum, energy[None]], axis=0)


def draw_cgrid_state(key, part):
    return fluid_state(key, NK, NI, NJ)


def draw_flap_state(key, part):
    return fluid_state(key, NK, FJ, FI)


def draw_iblank(key, part):
    levels = 8 + 48 * jnp.arange(FJ, dtype=jnp.int32) // FJ
    picks = jax.random.randint(key, (NK, FJ, FI), 0, 64, dtype=jnp.int32)
    return (picks >= levels[None, :, None]).astype(jnp.int32)


def place_ends(values, key, smallest, top_value):
    shape = values.shape
    place = [jax.random.randint(jax.random.fold_in(key, axis), (), 0, shape[axis]) for axis in range(len(shape))]
    values = values.at[tuple(place)].set(smallest)
    longest = shape.index(max(shape))
    place[longest] = (place[longest] + 1) % shape[longest]
    return values.at[tuple(place)].set(top_value)


def block_levels(own_key, dims, shards, least, high):
    def one(axis_at, shards_of):
        heights = jax.random.uniform(jax.random.fold_in(jax.random.fold_in(own_key, 6), axis_at), (shards_of,), jnp.float32, least / len(shards), high / len(shards))
        return jnp.repeat(jnp.exp(heights), dims[axis_at] // shards_of).reshape((-1,) + (1,) * (len(dims) - axis_at - 1))

    factor_of = one(*shards[0])
    for cut in shards[1:]:
        factor_of = factor_of * one(*cut)
    return factor_of


def setup_inputs(seed: int = 0) -> dict:
    arg_keys = jax.random.split(jax.random.key(seed), 9)
    return {
        "cgrid_state": draw_cgrid_state(jax.random.fold_in(arg_keys[8], 71), 0),
        "cgrid_metric": jnp.clip(jnp.exp(math.log(2.0) - 1.3862944 * jax.random.uniform(arg_keys[1], (3, NK, NI, NJ), jnp.float32) ** block_levels(arg_keys[1], (3, NK, NI, NJ), ((1, 16), (2, 8)), -0.2, 0.2)), 0.5, 2.0),
        "flap_state": draw_flap_state(jax.random.fold_in(arg_keys[8], 71), 0),
        "flap_metric": jnp.clip(jnp.exp(math.log(2.0) - 1.3862944 * jax.random.uniform(arg_keys[3], (3, NK, FJ, FI), jnp.float32) ** block_levels(arg_keys[3], (3, NK, FJ, FI), ((1, 16), (2, 8)), -0.2, 0.2)), 0.5, 2.0),
        "iblank": draw_iblank(jax.random.fold_in(arg_keys[8], 71), 0),
        "fringe_from": place_ends(jax.random.randint(arg_keys[5], (NK, FJ, FI), 0, N_WRAP * SLOTS), jax.random.fold_in(arg_keys[5], 1), 0, (N_WRAP * SLOTS) - 1).astype(jnp.int32),
        "donor_cell": place_ends(jax.random.randint(arg_keys[6], (DEVICES, N_WRAP, SLOTS), 0, (CK - 1) * (CI - 1) * (NJ - 1)), jax.random.fold_in(arg_keys[6], 1), 0, ((CK - 1) * (CI - 1) * (NJ - 1)) - 1).astype(jnp.int32),
        "donor_frac": jnp.clip(1.0 * jax.random.uniform(arg_keys[7], (DEVICES, N_WRAP, 3, SLOTS), jnp.float32) ** block_levels(arg_keys[7], (DEVICES, N_WRAP, 3, SLOTS), ((0, 128),), -0.2, 0.2), 0.0, 1.0),
    }


heat_ratio = 1.4
viscosity = 0.05
conduction = 0.07
damping = 1.0 / 32.0


def primitives(state):
    density = state[0]
    velocity = state[1:4] / density
    kinetic = 0.5 * jnp.sum(velocity * velocity, axis=0)
    pressure = (heat_ratio - 1.0) * (state[4] - density * kinetic)
    return velocity, kinetic, pressure, pressure / density


def flux_along(state, prims, component):
    velocity, kinetic, pressure, heat = prims
    normal_speed = velocity[component - 1]
    pieces = [state[0] * normal_speed]
    for member in range(1, 4):
        flowing = state[member] * normal_speed
        if member == component:
            flowing = flowing + pressure
        pieces.append(flowing)
    pieces.append((state[4] + pressure) * normal_speed)
    return jnp.stack(pieces)


def smooth_terms(prior_one, center_prims, next_one, factor, component):
    prior_prims = primitives(prior_one)
    next_prims = primitives(next_one)
    inviscid = -0.5 * factor * (flux_along(next_one, next_prims, component) - flux_along(prior_one, prior_prims, component))
    square = factor * factor
    bend_velocity = next_prims[0] - 2.0 * center_prims[0] + prior_prims[0]
    bend_kinetic = next_prims[1] - 2.0 * center_prims[1] + prior_prims[1]
    bend_heat = next_prims[3] - 2.0 * center_prims[3] + prior_prims[3]
    viscous = jnp.concatenate([jnp.zeros_like(factor)[None], viscosity * square * bend_velocity, (square * (viscosity * bend_kinetic + conduction * bend_heat))[None]], axis=0)
    return inviscid + viscous


def fourth_difference(prior_two, prior_one, center, next_one, next_two, factor):
    return -damping * factor * (next_two - 4.0 * next_one + 6.0 * center - 4.0 * prior_one + prior_two)


def rate_of(state, metric, neighbours, components):
    center_prims = primitives(state)
    total = jnp.zeros_like(state)
    for direction in range(3):
        prior_two, prior_one, next_one, next_two = neighbours[direction]
        factor = metric[direction]
        total = total + (smooth_terms(prior_one, center_prims, next_one, factor, components[direction]) + fourth_difference(prior_two, prior_one, state, next_one, next_two, factor))
    return total


def periodic_set(source, axis, count):
    extended = jnp.concatenate([lax.slice_in_dim(source, count - 2, count, axis=axis), source, lax.slice_in_dim(source, 0, 2, axis=axis)], axis=axis)
    return (lax.slice_in_dim(extended, 0, count, axis=axis), lax.slice_in_dim(extended, 1, count + 1, axis=axis), lax.slice_in_dim(extended, 3, count + 3, axis=axis), lax.slice_in_dim(extended, 4, count + 4, axis=axis))


def reference(cgrid_state, cgrid_metric, flap_state, flap_metric, iblank, fringe_from, donor_cell, donor_frac):
    sign = jnp.array([1.0, -1.0, -1.0, -1.0, 1.0], jnp.float32).reshape(5, 1, 1, 1)
    span_set = periodic_set(cgrid_state, 1, NK)
    first = cgrid_state[:, :, :1]
    last = cgrid_state[:, :, -1:]
    wrap_set = (jnp.concatenate([first, first, cgrid_state[:, :, :-2]], axis=2), jnp.concatenate([first, cgrid_state[:, :, :-1]], axis=2), jnp.concatenate([cgrid_state[:, :, 1:], last], axis=2), jnp.concatenate([cgrid_state[:, :, 2:], last, last], axis=2))
    wall = cgrid_state[:, :, :, 1::-1] * sign
    partner = cgrid_state[:, :, ::-1, 1::-1]
    wrap_cell = jnp.arange(NI, dtype=jnp.int32)
    in_wake = (wrap_cell < NI // 4) | (wrap_cell >= NI - NI // 4)
    lower = jnp.where(in_wake[None, None, :, None], partner, wall)
    top = cgrid_state[:, :, :, -1:]
    normal_set = (jnp.concatenate([lower, cgrid_state[:, :, :, :-2]], axis=3), jnp.concatenate([lower[:, :, :, 1:], cgrid_state[:, :, :, :-1]], axis=3), jnp.concatenate([cgrid_state[:, :, :, 1:], top], axis=3), jnp.concatenate([cgrid_state[:, :, :, 2:], top, top], axis=3))
    cgrid_rate = rate_of(cgrid_state, cgrid_metric, (span_set, wrap_set, normal_set), (3, 1, 2))

    device_ids = jnp.arange(DEVICES, dtype=jnp.int32).reshape(DEVICES, 1, 1)
    normal_pos = donor_cell % (NJ - 1)
    remainder = donor_cell // (NJ - 1)
    wrap_local = remainder % (CI - 1)
    span_local = remainder // (CI - 1)
    span_base = (device_ids % N_SPAN) * CK + span_local
    wrap_base = (device_ids // N_SPAN) * CI + wrap_local
    donor_values = jnp.zeros((5, DEVICES, N_WRAP, SLOTS), jnp.float32)
    for span_step in (0, 1):
        span_weight = donor_frac[:, :, 0] if span_step else 1.0 - donor_frac[:, :, 0]
        for wrap_step in (0, 1):
            wrap_weight = donor_frac[:, :, 1] if wrap_step else 1.0 - donor_frac[:, :, 1]
            for normal_step in (0, 1):
                normal_weight = donor_frac[:, :, 2] if normal_step else 1.0 - donor_frac[:, :, 2]
                weight = span_weight * wrap_weight * normal_weight
                donor_values = donor_values + cgrid_state[:, span_base + span_step, wrap_base + wrap_step, normal_pos + normal_step] * weight
    span_cell = jnp.arange(NK, dtype=jnp.int32).reshape(NK, 1, 1)
    normal_cell = jnp.arange(FJ, dtype=jnp.int32).reshape(1, FJ, 1)
    receiver_wrap = jnp.broadcast_to(normal_cell // FJD, (NK, FJ, FI)).astype(jnp.int32)
    sender = ((fringe_from // SLOTS) * N_SPAN + span_cell // CK).astype(jnp.int32)
    fringe_values = donor_values[:, sender, receiver_wrap, fringe_from % SLOTS]
    filled = jnp.where(iblank[None] == 1, flap_state, fringe_values)

    flap_span = periodic_set(filled, 1, NK)
    flap_wall = filled[:, :, 1::-1] * sign
    flap_top = filled[:, :, -1:]
    flap_normal = (jnp.concatenate([flap_wall, filled[:, :, :-2]], axis=2), jnp.concatenate([flap_wall[:, :, 1:], filled[:, :, :-1]], axis=2), jnp.concatenate([filled[:, :, 1:], flap_top], axis=2), jnp.concatenate([filled[:, :, 2:], flap_top, flap_top], axis=2))
    flap_around = (jnp.roll(filled, 2, axis=3), jnp.roll(filled, 1, axis=3), jnp.roll(filled, -1, axis=3), jnp.roll(filled, -2, axis=3))
    flap_rate = rate_of(filled, flap_metric, (flap_span, flap_normal, flap_around), (3, 2, 1))
    flap_rate = jnp.where(iblank[None] == 1, flap_rate, jnp.zeros_like(flap_rate))
    return cgrid_rate, flap_rate
```

```python
import functools

import jax
import jax.numpy as jnp
from jax import lax
from jax.experimental import pallas as pl
from jax.experimental.pallas import tpu as pltpu
from jax.sharding import PartitionSpec as P

viscosity = 0.05
conduction = 0.07
damping = 1.0 / 32.0
VMEM_LIMIT = 56 * 1024 * 1024

f32, bf16, i32 = jnp.float32, jnp.bfloat16, jnp.int32


def whole(shape):
    return pl.BlockSpec(shape, lambda *_: (0,) * len(shape))


def params():
    return pltpu.CompilerParams(vmem_limit_bytes=VMEM_LIMIT)


def primitives(q):
    inverse = 1.0 / q[0]
    v = [q[m] * inverse for m in (1, 2, 3)]
    kinetic = 0.5 * (v[0] * v[0] + v[1] * v[1] + v[2] * v[2])
    pressure = 0.4 * (q[4] - q[0] * kinetic)
    return v + [pressure, viscosity * kinetic + conduction * (pressure * inverse)]


def flux(q, prims, m):
    u = prims[m - 1]
    f = [q[0] * u]
    for c in (1, 2, 3):
        f.append(q[c] * u + prims[3] if c == m else q[c] * u)
    f.append((q[4] + prims[3]) * u)
    return f


def pack_kernel(q_ref, wrap_lo, wrap_hi, span_lo, span_hi, wall):
    spans, rows = q_ref.shape[1], q_ref.shape[2]
    lane = lax.broadcasted_iota(i32, (rows, 128), 1)
    for c in range(5):
        for l in range(2):
            span_lo[c, l] = q_ref[c, l]
            span_hi[c, l] = q_ref[c, spans - 2 + l]
        cells = jnp.zeros((rows, 128), f32)
        for k in range(spans):
            for l in range(2):
                wrap_lo[c, l, k : k + 1, :] = q_ref[c, k, l : l + 1, :]
                wrap_hi[c, l, k : k + 1, :] = q_ref[c, k, rows - 2 + l : rows - 1 + l, :]
            near = q_ref[c, k, :, 0:128]
            if k:
                near = pltpu.roll(near, 2 * k, 1)
            cells = jnp.where(lane // 2 == k, near, cells)
        wall[c] = cells


def pack(state):
    _, spans, rows, lanes = state.shape
    shapes = [(5, 2, spans, lanes)] * 2 + [(5, 2, rows, lanes)] * 2 + [(5, rows, 128)]
    return pl.pallas_call(
        pack_kernel,
        in_specs=[whole(state.shape)],
        out_specs=[whole(s) for s in shapes],
        out_shape=[jax.ShapeDtypeStruct(s, f32) for s in shapes],
        grid=(1,),
        compiler_params=params(),
        name="cgrid_pack",
    )(state)


def rate_kernel(
    place_ref,
    q_hbm,
    major_lo,
    major_hi,
    sub_lo,
    sub_hi,
    own_lo,
    own_hi,
    wall_own,
    wall_far,
    metric_ref,
    mask_ref,
    out_ref,
    qe,
    prim,
    sub_edge,
    lane_edge,
    sems,
    *,
    cgrid,
    step_planes,
    components,
    metric_rows,
):
    planes, rows, lanes = qe.shape[1] - 4, qe.shape[2], qe.shape[3]
    step = pl.program_id(0)
    at_start = place_ref[0] == 0
    at_end = place_ref[0] == place_ref[1] - 1
    major_m, sub_m, lane_m = components

    def edge_fields(q1, q2, m, side):
        prims = primitives(q1)
        fl = flux(q1, prims, m)
        lead = [(-0.5 * side) * fl[c] + 0.125 * q1[c] - damping * q2[c] for c in range(5)]
        return lead + q1 + prims[:3] + prims[4:]

    def store_prims(k, slot):
        for i, x in enumerate(primitives([qe[c, k] for c in range(5)])):
            prim[slot, i] = x

    @pl.when(step == 0)
    def _():
        copies = [
            pltpu.make_async_copy(q_hbm, qe.at[:, pl.ds(2, planes)], sems.at[0]),
            pltpu.make_async_copy(major_lo, qe.at[:, pl.ds(0, 2)], sems.at[1]),
            pltpu.make_async_copy(major_hi, qe.at[:, pl.ds(planes + 2, 2)], sems.at[2]),
        ]
        for copy in copies:
            copy.start()
        for side, ref, own in ((-1, sub_lo, own_lo), (1, sub_hi, own_hi)):
            near, far = (1, 0) if side < 0 else (0, 1)
            q1 = [ref[c, near] for c in range(5)]
            q2 = [ref[c, far] for c in range(5)]
            if cgrid:
                edge = at_start if side < 0 else at_end
                clamp = 0 if side < 0 else 1
                q1 = [jnp.where(edge, own[c, clamp], q1[c]) for c in range(5)]
                q2 = [jnp.where(edge, own[c, clamp], q2[c]) for c in range(5)]
            for i, x in enumerate(edge_fields(q1, q2, sub_m, side)):
                sub_edge[(side + 1) // 2, i] = x
        if cgrid:
            place, count = place_ref[0], place_ref[1]
            in_wake = (place < count // 4) | (place >= count - count // 4)
            turn = 7 - lax.broadcasted_iota(i32, (8, 128), 0)
            ghosts = []
            for c in range(5):
                sign = -1.0 if c in (1, 2, 3) else 1.0
                parts = []
                for r in range(rows // 8):
                    far = wall_far[c, rows - 8 - 8 * r : rows - 8 * r, :]
                    far = jnp.take_along_axis(far, turn, axis=0, mode="promise_in_bounds")
                    parts.append(jnp.where(in_wake, far, sign * wall_own[c, 8 * r : 8 * r + 8, :]))
                ghosts.append(jnp.concatenate(parts, axis=0))
            second = [pltpu.roll(x, 127, 1) for x in ghosts]
            for i, x in enumerate(edge_fields(ghosts, second, lane_m, -1)):
                lane_edge[i] = x
        for copy in copies:
            copy.wait()
        if not cgrid:

            @pl.when(at_start)
            def _():
                for c in range(5):
                    sign = -1.0 if c in (1, 2, 3) else 1.0
                    qe[c, 1] = sign * qe[c, 2]
                    qe[c, 0] = sign * qe[c, 3]

            @pl.when(at_end)
            def _():
                for c in range(5):
                    qe[c, planes + 2] = qe[c, planes + 1]
                    qe[c, planes + 3] = qe[c, planes + 1]

        store_prims(1, 0)
        store_prims(2, 1)

    row_at = lax.broadcasted_iota(i32, (rows, lanes), 0)
    lane_at = lax.broadcasted_iota(i32, (rows, lanes), 1)
    row_first, row_last = row_at == 0, row_at == rows - 1
    lane_first, lane_last = lane_at == 0, lane_at == lanes - 1

    def one(b, _):
        k = step * step_planes + b
        here, below, above = lax.rem(k + 1, 3), lax.rem(k, 3), lax.rem(k + 2, 3)
        store_prims(k + 3, above)

        def sub_next(x, i):
            return jnp.where(row_last, sub_edge[1, i, pl.ds(k, 1), :], pltpu.roll(x, rows - 1, 0))

        def sub_prior(x, i):
            return jnp.where(row_first, sub_edge[0, i, pl.ds(k, 1), :], pltpu.roll(x, 1, 0))

        def lane_next(x):
            moved = pltpu.roll(x, lanes - 1, 1)
            return jnp.where(lane_last, x, moved) if cgrid else moved

        def lane_prior(x, i):
            moved = pltpu.roll(x, 1, 1)
            if not cgrid:
                return moved
            ghost = pltpu.roll(lane_edge[i], lax.rem(128 - 2 * k, 128), 1)
            ghost = jnp.concatenate([ghost] * (lanes // 128), axis=1)
            return jnp.where(lane_first, ghost, moved)

        gm = metric_ref[metric_rows[0], b]
        gs = metric_ref[metric_rows[1], b]
        gl = metric_ref[metric_rows[2], b]
        gm2, gs2, gl2 = gm * gm, gs * gs, gl * gl
        mine = [prim[here, i] for i in range(5)]
        viscous = {}
        for i, field, c, e in ((0, 0, 1, 10), (1, 1, 2, 11), (2, 2, 3, 12), (4, 4, 4, 13)):
            x = mine[field]
            twice = 2.0 * x
            total = gm2 * (prim[above, i] + prim[below, i] - twice)
            total += gs2 * (sub_next(x, e) + sub_prior(x, e) - twice)
            total += gl2 * (lane_next(x) + lane_prior(x, e) - twice)
            viscous[c] = total if c == 4 else viscosity * total
        q = [qe[c, k + 2] for c in range(5)]
        sub_flux = flux(q, mine, sub_m)
        lane_flux = flux(q, mine, lane_m)
        next_flux = flux([qe[c, k + 3] for c in range(5)], [prim[above, i] for i in range(5)], major_m)
        prior_flux = flux([qe[c, k + 1] for c in range(5)], [prim[below, i] for i in range(5)], major_m)
        for c in range(5):
            x = q[c]
            middle = (6.0 * damping) * x
            eighth = 0.125 * x
            bend = (
                0.125 * (qe[c, k + 3] + qe[c, k + 1])
                - damping * (qe[c, k + 4] + qe[c, k])
                - 0.5 * (next_flux[c] - prior_flux[c])
                - middle
            )
            total = gm * bend
            half = 0.5 * sub_flux[c]
            up = eighth - half - damping * sub_next(x, 5 + c)
            down = eighth + half - damping * sub_prior(x, 5 + c)
            total += gs * (sub_next(up, c) + sub_prior(down, c) - middle)
            half = 0.5 * lane_flux[c]
            up = eighth - half - damping * lane_next(x)
            down = eighth + half - damping * lane_prior(x, 5 + c)
            total += gl * (lane_next(up) + lane_prior(down, c) - middle)
            if c:
                total += viscous[c]
            if not cgrid:
                total = jnp.where(mask_ref[b] == 1, total, 0.0)
            out_ref[c, b] = total
        return 0

    lax.fori_loop(0, step_planes, one, 0)


def rate(place, q, majors, subs, owns, walls, metric, mask, *, cgrid, step_planes, components, metric_rows):
    _, planes, rows, lanes = q.shape
    anywhere = pl.BlockSpec(memory_space=pl.ANY)
    block = lambda n: pl.BlockSpec((n, step_planes, rows, lanes), lambda i: (0, i, 0, 0))
    if mask is None:
        mask = jnp.zeros((1, 8, 128), i32)
        mask_spec = whole(mask.shape)
    else:
        mask_spec = pl.BlockSpec((step_planes, rows, lanes), lambda i: (i, 0, 0))
    return pl.pallas_call(
        functools.partial(
            rate_kernel,
            cgrid=cgrid,
            step_planes=step_planes,
            components=components,
            metric_rows=metric_rows,
        ),
        grid=(planes // step_planes,),
        in_specs=[pl.BlockSpec(memory_space=pltpu.SMEM), anywhere, anywhere, anywhere]
        + [whole(x.shape) for x in (*subs, *owns, *walls)]
        + [block(3), mask_spec],
        out_specs=block(5),
        out_shape=jax.ShapeDtypeStruct(q.shape, f32),
        scratch_shapes=[
            pltpu.VMEM((5, planes + 4, rows, lanes), f32),
            pltpu.VMEM((3, 5, rows, lanes), f32),
            pltpu.VMEM((2, 14, planes, lanes), f32),
            pltpu.VMEM((14, rows, 128), f32),
            pltpu.SemaphoreType.DMA((3,)),
        ],
        compiler_params=params(),
        cost_estimate=pl.CostEstimate(
            flops=300 * planes * rows * lanes, bytes_accessed=60 * planes * rows * lanes, transcendentals=0
        ),
        name="cgrid_rate" if cgrid else "flap_rate",
    )(place, q, *majors, *subs, *owns, *walls, metric, mask)


def split_two(x):
    high = x.astype(bf16)
    return high, (x - high.astype(f32)).astype(bf16)


def donor_kernel(cell_ref, frac_ref, q_ref, out_ref, table, *, tile):
    spans, rows, lanes = q_ref.shape[1:]
    slots = cell_ref.shape[1]

    @pl.when(pl.program_id(0) == 0)
    def _():
        def prepare(k, _):
            for c in range(5):
                high, low = split_two(q_ref[c, k])
                here = slice(c * rows, (c + 1) * rows)
                table[k, here, 0:lanes] = high
                table[k, here, lanes : 2 * lanes] = low
                table[k, here, 2 * lanes : 3 * lanes] = high
            return 0

        lax.fori_loop(0, spans, prepare, 0)

    part = pl.program_id(0)
    per = slots // tile
    w = part // per
    t0 = pl.multiple_of((part % per) * tile, 128)
    cell = cell_ref[pl.ds(w, 1), pl.ds(t0, tile)]
    f0, f1, f2 = [frac_ref[d, pl.ds(w, 1), pl.ds(t0, tile)] for d in range(3)]
    upper = jnp.floor((cell.astype(f32) + 0.5) * (1.0 / (lanes - 1)))
    span = jnp.floor((upper + 0.5) * (1.0 / (rows - 1)))
    wrap = (upper - span * (rows - 1)).astype(i32)
    normal = cell - upper.astype(i32) * (lanes - 1)
    span = span.astype(i32)

    def weights(count, at, frac):
        cells = lax.broadcasted_iota(i32, (count, tile), 0)
        return jnp.where(cells == at, 1.0 - frac, jnp.where(cells == at + 1, frac, 0.0))

    high, low = split_two(weights(lanes, normal, f2))
    along = jnp.concatenate([high, high, low], axis=0)
    across = weights(rows, wrap, f1)

    def plane(k, sums):
        mixed = jnp.dot(table[k], along, preferred_element_type=f32)
        ws = jnp.where(span == k, 1.0 - f0, jnp.where(span + 1 == k, f0, 0.0))
        new = []
        for c in range(5):
            total = mixed[c * rows : c * rows + 8] * across[0:8]
            for r in range(8, rows, 8):
                total += mixed[c * rows + r : c * rows + r + 8] * across[r : r + 8]
            new.append(sums[c] + ws * total)
        return tuple(new)

    sums = lax.fori_loop(0, spans, plane, tuple(jnp.zeros((8, tile), f32) for _ in range(5)), unroll=4)
    for c in range(5):
        out_ref[w, c : c + 1, pl.ds(t0, tile)] = jnp.sum(sums[c], axis=0, keepdims=True)


def donors(cell, frac, state, tile=256):
    _, spans, rows, lanes = state.shape
    count, slots = cell.shape
    return pl.pallas_call(
        functools.partial(donor_kernel, tile=tile),
        grid=(count * slots // tile,),
        in_specs=[whole(cell.shape), whole(frac.shape), whole(state.shape)],
        out_specs=whole((count, 5, slots)),
        out_shape=jax.ShapeDtypeStruct((count, 5, slots), f32),
        scratch_shapes=[pltpu.VMEM((spans, 5 * rows, 3 * lanes), bf16)],
        compiler_params=params(),
        name="donors",
    )(cell, frac, state)


def fill_kernel(from_ref, mask_ref, q_ref, slot_ref, out_ref, norm_lo, norm_hi, span_lo, span_hi, table):
    planes = pl.num_programs(0)
    rows, lanes = from_ref.shape[1:]
    low = 256
    highs = table.shape[0] // 10
    j = pl.program_id(0)

    @pl.when(j == 0)
    def _():
        per = slot_ref.shape[2] // low
        for c in range(5):
            for w in range(slot_ref.shape[0]):
                for r in range(per):
                    value = slot_ref[w, c : c + 1, r * low : (r + 1) * low]
                    table[c * highs + w * per + r : c * highs + w * per + r + 1, :] = value
        for r in range(0, 5 * highs, 8):
            value = table[r : r + 8, :]
            table[5 * highs + r : 5 * highs + r + 8, :] = value - value.astype(bf16).astype(f32)

    both = table[...].astype(bf16)
    sub = lax.broadcasted_iota(i32, (8, lanes), 0)
    cells = lax.broadcasted_iota(i32, (low, lanes), 0).astype(f32).astype(bf16)
    one, zero = jnp.ones((), bf16), jnp.zeros((), bf16)

    def row(s, _):
        at = from_ref[0, pl.ds(s, 1), :]
        pick = jnp.where(cells == (at & (low - 1)).astype(f32).astype(bf16), one, zero)
        high = at // low
        found = jnp.dot(both, pick, preferred_element_type=f32)
        masks = [sub + 8 * g == high for g in range(highs // 8)]
        keep = mask_ref[0, pl.ds(s, 1), :] == 1
        for c in range(5):
            value = None
            for g, mask in enumerate(masks):
                r = c * highs + 8 * g
                piece = found[r : r + 8] + found[5 * highs + r : 5 * highs + r + 8]
                value = jnp.where(mask, piece, 0.0 if value is None else value)
            value = jnp.sum(value, axis=0, keepdims=True)
            out_ref[c, 0, pl.ds(s, 1), :] = jnp.where(keep, q_ref[c, 0, pl.ds(s, 1), :], value)
        return 0

    lax.fori_loop(0, rows, row, 0, unroll=16)

    for c in range(5):
        for l in range(2):
            span_lo[c, l, pl.ds(j, 1), :] = out_ref[c, 0, l : l + 1, :]
            span_hi[c, l, pl.ds(j, 1), :] = out_ref[c, 0, rows - 2 + l : rows - 1 + l, :]

    @pl.when(j < 2)
    def _():
        for c in range(5):
            norm_lo[c, j] = out_ref[c, 0]

    @pl.when(j >= planes - 2)
    def _():
        for c in range(5):
            norm_hi[c, j - (planes - 2)] = out_ref[c, 0]


def fill(source, mask, state, slot):
    _, planes, rows, lanes = state.shape
    count, _, slots = slot.shape
    plane = pl.BlockSpec((1, rows, lanes), lambda j: (j, 0, 0))
    state_plane = pl.BlockSpec((5, 1, rows, lanes), lambda j: (0, j, 0, 0))
    edges = [(5, 2, rows, lanes)] * 2 + [(5, 2, planes, lanes)] * 2
    return pl.pallas_call(
        fill_kernel,
        grid=(planes,),
        in_specs=[plane, plane, state_plane, whole(slot.shape)],
        out_specs=[state_plane] + [whole(s) for s in edges],
        out_shape=[jax.ShapeDtypeStruct(s, f32) for s in [state.shape] + edges],
        scratch_shapes=[pltpu.VMEM((10 * count * slots // 256, 256), f32)],
        compiler_params=params(),
        cost_estimate=pl.CostEstimate(flops=24 * 10**9, bytes_accessed=6 * 10**6, transcendentals=0),
        name="fill",
    )(source, mask, state, slot)


def body(
    cgrid_state, cgrid_metric, flap_state, flap_metric, iblank, fringe_from, donor_cell, donor_frac
):
    wrap_count, span_count = lax.axis_size("wrap"), lax.axis_size("span")
    place = jnp.stack([lax.axis_index("wrap"), jnp.int32(wrap_count)]).astype(i32)

    def onward(value, axis):
        size = lax.axis_size(axis)
        return lax.ppermute(value, axis, [(i, (i + 1) % size) for i in range(size)])

    def back(value, axis):
        size = lax.axis_size(axis)
        return lax.ppermute(value, axis, [((i + 1) % size, i) for i in range(size)])

    wrap_lo, wrap_hi, span_lo, span_hi, wall = pack(cgrid_state)
    far = lax.ppermute(
        wall[:, :, 0:32], "wrap", [(i, wrap_count - 1 - i) for i in range(wrap_count)]
    )
    far = jnp.pad(far, ((0, 0), (0, 0), (0, 96)))
    majors = (onward(span_hi, "span"), back(span_lo, "span"))
    subs = (onward(wrap_hi, "wrap"), back(wrap_lo, "wrap"))

    slot = donors(donor_cell[0], jnp.transpose(donor_frac[0], (1, 0, 2)), cgrid_state)
    slot = lax.all_to_all(slot, "wrap", split_axis=0, concat_axis=0, tiled=True)

    turned = lambda x: jnp.swapaxes(x, -3, -2)
    mask = turned(iblank)
    filled, norm_lo, norm_hi, edge_lo, edge_hi = fill(turned(fringe_from), mask, turned(flap_state), slot)
    flap_majors = (onward(norm_hi, "wrap"), back(norm_lo, "wrap"))
    flap_subs = (onward(edge_hi, "span"), back(edge_lo, "span"))

    cgrid_rate = rate(
        place,
        cgrid_state,
        majors,
        subs,
        (wrap_lo, wrap_hi),
        (wall, far),
        cgrid_metric,
        None,
        cgrid=True,
        step_planes=4,
        components=(3, 1, 2),
        metric_rows=(0, 1, 2),
    )
    none = jnp.zeros((5, 8, 128), f32)
    flap_rate = rate(
        place,
        filled,
        flap_majors,
        flap_subs,
        (none, none),
        (none, none),
        turned(flap_metric),
        mask,
        cgrid=False,
        step_planes=3,
        components=(2, 3, 1),
        metric_rows=(1, 0, 2),
    )
    return (cgrid_rate, turned(flap_rate))


def solution(mesh):
    return jax.shard_map(
        body,
        mesh=mesh,
        in_specs=(
            P(None, "span", "wrap", None),
            P(None, "span", "wrap", None),
            P(None, "span", "wrap", None),
            P(None, "span", "wrap", None),
            P("span", "wrap", None),
            P("span", "wrap", None),
            P(("wrap", "span"), None, None),
            P(("wrap", "span"), None, None, None),
        ),
        out_specs=(P(None, "span", "wrap", None), P(None, "span", "wrap", None)),
        check_vma=False,
    )
```

```python
import functools

import jax
import jax.numpy as jnp
from jax import lax
from jax.experimental import pallas as pl
from jax.experimental.pallas import tpu as pltpu
from jax.sharding import PartitionSpec as P

viscosity = 0.05
conduction = 0.07
damping = 1.0 / 32.0
VMEM_LIMIT = 56 * 1024 * 1024
GROUP = 8

f32, bf16, i32 = jnp.float32, jnp.bfloat16, jnp.int32


def whole(shape):
    return pl.BlockSpec(shape, lambda *_: (0,) * len(shape))


def params():
    return pltpu.CompilerParams(vmem_limit_bytes=VMEM_LIMIT)


def primitives(q):
    inverse = 1.0 / q[0]
    v = [q[m] * inverse for m in (1, 2, 3)]
    kinetic = 0.5 * (v[0] * v[0] + v[1] * v[1] + v[2] * v[2])
    pressure = 0.4 * (q[4] - q[0] * kinetic)
    return v + [pressure, viscosity * kinetic + conduction * (pressure * inverse)]


def flux(q, prims, m):
    u = prims[m - 1]
    f = [q[0] * u]
    for c in (1, 2, 3):
        f.append(q[c] * u + prims[3] if c == m else q[c] * u)
    f.append((q[4] + prims[3]) * u)
    return f


def pack_kernel(q_ref, wrap_lo, wrap_hi, span_lo, span_hi, wall):
    spans, rows = q_ref.shape[1], q_ref.shape[2]
    lane = lax.broadcasted_iota(i32, (rows, 128), 1)
    for c in range(5):
        for l in range(2):
            span_lo[c, l] = q_ref[c, l]
            span_hi[c, l] = q_ref[c, spans - 2 + l]
        cells = jnp.zeros((rows, 128), f32)
        for k in range(spans):
            for l in range(2):
                wrap_lo[c, l, k : k + 1, :] = q_ref[c, k, l : l + 1, :]
                wrap_hi[c, l, k : k + 1, :] = q_ref[c, k, rows - 2 + l : rows - 1 + l, :]
            near = q_ref[c, k, :, 0:128]
            if k:
                near = pltpu.roll(near, 2 * k, 1)
            cells = jnp.where(lane // 2 == k, near, cells)
        wall[c] = cells[:, 0 : 2 * spans]


def pack(state):
    _, spans, rows, lanes = state.shape
    shapes = [(5, 2, spans, lanes)] * 2 + [(5, 2, rows, lanes)] * 2 + [(5, rows, 2 * spans)]
    return pl.pallas_call(
        pack_kernel,
        in_specs=[whole(state.shape)],
        out_specs=[whole(s) for s in shapes],
        out_shape=[jax.ShapeDtypeStruct(s, f32) for s in shapes],
        grid=(1,),
        compiler_params=params(),
        name="cgrid_pack",
    )(state)


def rate_kernel(
    q_hbm,
    major_lo,
    major_hi,
    sub_lo,
    sub_hi,
    *refs,
    cgrid,
    step_planes,
    components,
    metric_rows,
):
    if cgrid:
        own_lo, own_hi, wall_own, wall_far, metric_ref, out_ref, qe, prim, sub_edge, lane_edge, sems = refs
    else:
        own_lo = own_hi = None
        mask_ref, metric_ref, out_ref, qe, prim, sub_edge, sems = refs
    planes, rows, lanes = qe.shape[1] - 4, qe.shape[2], qe.shape[3]
    step = pl.program_id(0)
    place, count = lax.axis_index("wrap"), lax.axis_size("wrap")
    at_start = place == 0
    at_end = place == count - 1
    major_m, sub_m, lane_m = components

    def edge_fields(q1, q2, m, side):
        prims = primitives(q1)
        fl = flux(q1, prims, m)
        lead = [(-0.5 * side) * fl[c] + 0.125 * q1[c] - damping * q2[c] for c in range(5)]
        return lead + q1 + prims[:3] + prims[4:]

    def store_prims(k, slot):
        for i, x in enumerate(primitives([qe[c, k] for c in range(5)])):
            prim[slot, i] = x

    @pl.when(step == 0)
    def _():
        copies = [
            pltpu.make_async_copy(q_hbm, qe.at[:, pl.ds(2, planes)], sems.at[0]),
            pltpu.make_async_copy(major_lo, qe.at[:, pl.ds(0, 2)], sems.at[1]),
            pltpu.make_async_copy(major_hi, qe.at[:, pl.ds(planes + 2, 2)], sems.at[2]),
        ]
        for copy in copies:
            copy.start()
        for side, ref, own in ((-1, sub_lo, own_lo), (1, sub_hi, own_hi)):
            near, far = (1, 0) if side < 0 else (0, 1)
            q1 = [ref[c, near] for c in range(5)]
            q2 = [ref[c, far] for c in range(5)]
            if cgrid:
                edge = at_start if side < 0 else at_end
                clamp = 0 if side < 0 else 1
                q1 = [jnp.where(edge, own[c, clamp], q1[c]) for c in range(5)]
                q2 = [jnp.where(edge, own[c, clamp], q2[c]) for c in range(5)]
            for i, x in enumerate(edge_fields(q1, q2, sub_m, side)):
                sub_edge[(side + 1) // 2, i] = x
        if cgrid:
            in_wake = (place < count // 4) | (place >= count - count // 4)
            turn = 7 - lax.broadcasted_iota(i32, (8, 128), 0)
            ghosts = []
            for c in range(5):
                sign = -1.0 if c in (1, 2, 3) else 1.0
                parts = []
                for r in range(rows // 8):
                    far = wall_far[c, rows - 8 - 8 * r : rows - 8 * r, :]
                    own = wall_own[c, 8 * r : 8 * r + 8, :]
                    own = jnp.concatenate([own, jnp.zeros((8, 128 - own.shape[1]), f32)], axis=1)
                    far = jnp.concatenate([far, jnp.zeros((8, 128 - far.shape[1]), f32)], axis=1)
                    far = jnp.take_along_axis(far, turn, axis=0, mode="promise_in_bounds")
                    parts.append(jnp.where(in_wake, far, sign * own))
                ghosts.append(jnp.concatenate(parts, axis=0))
            second = [pltpu.roll(x, 127, 1) for x in ghosts]
            for i, x in enumerate(edge_fields(ghosts, second, lane_m, -1)):
                lane_edge[i] = x
        for copy in copies:
            copy.wait()
        if not cgrid:

            @pl.when(at_start)
            def _():
                for c in range(5):
                    sign = -1.0 if c in (1, 2, 3) else 1.0
                    qe[c, 1] = sign * qe[c, 2]
                    qe[c, 0] = sign * qe[c, 3]

            @pl.when(at_end)
            def _():
                for c in range(5):
                    qe[c, planes + 2] = qe[c, planes + 1]
                    qe[c, planes + 3] = qe[c, planes + 1]

        store_prims(1, 0)
        store_prims(2, 1)

    row_at = lax.broadcasted_iota(i32, (rows, lanes), 0)
    lane_at = lax.broadcasted_iota(i32, (rows, lanes), 1)
    row_first, row_last = row_at == 0, row_at == rows - 1
    lane_first, lane_last = lane_at == 0, lane_at == lanes - 1

    def one(b, _):
        k = step * step_planes + b
        here, below, above = lax.rem(k + 1, 3), lax.rem(k, 3), lax.rem(k + 2, 3)
        store_prims(k + 3, above)

        def sub_next(x, i):
            return jnp.where(row_last, sub_edge[1, i, pl.ds(k, 1), :], pltpu.roll(x, rows - 1, 0))

        def sub_prior(x, i):
            return jnp.where(row_first, sub_edge[0, i, pl.ds(k, 1), :], pltpu.roll(x, 1, 0))

        def lane_next(x):
            moved = pltpu.roll(x, lanes - 1, 1)
            return jnp.where(lane_last, x, moved) if cgrid else moved

        def lane_prior(x, i):
            moved = pltpu.roll(x, 1, 1)
            if not cgrid:
                return moved
            ghost = pltpu.roll(lane_edge[i], lax.rem(128 - 2 * k, 128), 1)
            ghost = jnp.concatenate([ghost] * (lanes // 128), axis=1)
            return jnp.where(lane_first, ghost, moved)

        gm = metric_ref[metric_rows[0], b]
        gs = metric_ref[metric_rows[1], b]
        gl = metric_ref[metric_rows[2], b]
        gm2, gs2, gl2 = gm * gm, gs * gs, gl * gl
        mine = [prim[here, i] for i in range(5)]
        viscous = {}
        for i, field, c, e in ((0, 0, 1, 10), (1, 1, 2, 11), (2, 2, 3, 12), (4, 4, 4, 13)):
            x = mine[field]
            twice = 2.0 * x
            total = gm2 * (prim[above, i] + prim[below, i] - twice)
            total += gs2 * (sub_next(x, e) + sub_prior(x, e) - twice)
            total += gl2 * (lane_next(x) + lane_prior(x, e) - twice)
            viscous[c] = total if c == 4 else viscosity * total
        q = [qe[c, k + 2] for c in range(5)]
        sub_flux = flux(q, mine, sub_m)
        lane_flux = flux(q, mine, lane_m)
        next_flux = flux([qe[c, k + 3] for c in range(5)], [prim[above, i] for i in range(5)], major_m)
        prior_flux = flux([qe[c, k + 1] for c in range(5)], [prim[below, i] for i in range(5)], major_m)
        for c in range(5):
            x = q[c]
            middle = (6.0 * damping) * x
            eighth = 0.125 * x
            bend = (
                0.125 * (qe[c, k + 3] + qe[c, k + 1])
                - damping * (qe[c, k + 4] + qe[c, k])
                - 0.5 * (next_flux[c] - prior_flux[c])
                - middle
            )
            total = gm * bend
            half = 0.5 * sub_flux[c]
            up = eighth - half - damping * sub_next(x, 5 + c)
            down = eighth + half - damping * sub_prior(x, 5 + c)
            total += gs * (sub_next(up, c) + sub_prior(down, c) - middle)
            half = 0.5 * lane_flux[c]
            up = eighth - half - damping * lane_next(x)
            down = eighth + half - damping * lane_prior(x, 5 + c)
            total += gl * (lane_next(up) + lane_prior(down, c) - middle)
            if c:
                total += viscous[c]
            if not cgrid:
                total = jnp.where(mask_ref[b] == 1, total, 0.0)
            out_ref[c, b] = total
        return 0

    lax.fori_loop(0, step_planes, one, 0)


def rate(q, majors, subs, extras, metric, mask, *, cgrid, step_planes, components, metric_rows):
    _, planes, rows, lanes = q.shape
    anywhere = pl.BlockSpec(memory_space=pl.ANY)
    block = lambda n: pl.BlockSpec((n, step_planes, rows, lanes), lambda i: (0, i, 0, 0))
    last_specs = [block(3)]
    last = (metric,)
    if mask is not None:
        last_specs = [pl.BlockSpec((step_planes, rows, lanes), lambda i: (i, 0, 0))] + last_specs
        last = (mask, metric)
    return pl.pallas_call(
        functools.partial(
            rate_kernel,
            cgrid=cgrid,
            step_planes=step_planes,
            components=components,
            metric_rows=metric_rows,
        ),
        grid=(planes // step_planes,),
        in_specs=[anywhere] * 3 + [whole(x.shape) for x in (*subs, *extras)] + last_specs,
        out_specs=block(5),
        out_shape=jax.ShapeDtypeStruct(q.shape, f32),
        scratch_shapes=[
            pltpu.VMEM((5, planes + 4, rows, lanes), f32),
            pltpu.VMEM((3, 5, rows, lanes), f32),
            pltpu.VMEM((2, 14, planes, lanes), f32),
        ]
        + [pltpu.VMEM((14, rows, 128), f32)] * cgrid
        + [pltpu.SemaphoreType.DMA((3,))],
        compiler_params=params(),
        cost_estimate=pl.CostEstimate(
            flops=300 * planes * rows * lanes, bytes_accessed=60 * planes * rows * lanes, transcendentals=0
        ),
        name="cgrid_rate" if cgrid else "flap_rate",
    )(q, *majors, *subs, *extras, *last)


def split_two(x):
    high = x.astype(bf16)
    return high, (x - high.astype(f32)).astype(bf16)


def lookup(both, at):
    width = at.shape[1]
    highs = both.shape[0] // 10
    cells = lax.broadcasted_iota(i32, (256, width), 0).astype(f32).astype(bf16)
    sub = lax.broadcasted_iota(i32, (8, width), 0)
    pick = jnp.where(
        cells == (at & 255).astype(f32).astype(bf16), jnp.ones((), bf16), jnp.zeros((), bf16)
    )
    high = at // 256
    found = jnp.dot(both, pick, preferred_element_type=f32)
    masks = [sub + 8 * g == high for g in range(highs // 8)]
    values = []
    for c in range(5):
        value = None
        for g, mask in enumerate(masks):
            r = c * highs + 8 * g
            piece = found[r : r + 8] + found[5 * highs + r : 5 * highs + r + 8]
            value = jnp.where(mask, piece, 0.0 if value is None else value)
        values.append(jnp.sum(value, axis=0, keepdims=True))
    return values


def add_remainders(table):
    half = table.shape[0] // 2
    for r in range(0, half, 8):
        value = table[r : r + 8, :]
        table[half + r : half + r + 8, :] = value - value.astype(bf16).astype(f32)


def donor_kernel(
    cell_ref, frac_ref, q_ref, out_ref, planes, pieces, rank_ref, ordered, where_ref, first, partial, table, sem
):
    spans, rows, lanes = q_ref.shape[1:]
    count, slots = cell_ref.shape
    tile = 256
    tiles = count * slots // tile
    wide = slots // 128
    one, zero = jnp.ones((), bf16), jnp.zeros((), bf16)

    def prepare(k, _):
        for c in range(5):
            high, low = split_two(q_ref[c, k])
            here = pl.ds(pl.multiple_of(k * 5 * rows + c * rows, 16), rows)
            planes[here, 0:lanes] = high
            planes[here, lanes : 2 * lanes] = low
            planes[here, 2 * lanes : 3 * lanes] = high
        return 0

    lax.fori_loop(0, spans, prepare, 0)
    planes[spans * 5 * rows :, :] = jnp.zeros((5 * rows, 3 * lanes), bf16)

    cell = cell_ref[...]
    upper = jnp.floor((cell.astype(f32) + 0.5) * (1.0 / (lanes - 1)))
    span = jnp.floor((upper + 0.5) * (1.0 / (rows - 1)))
    pieces[0] = span
    pieces[1] = upper - span * (rows - 1)
    pieces[2] = cell.astype(f32) - upper * (lanes - 1)
    for d in range(3):
        f = frac_ref[d]
        high = f.astype(bf16).astype(f32)
        pieces[3 + 2 * d] = high
        pieces[4 + 2 * d] = f - high

    lines = jnp.concatenate([span[:, 128 * t : 128 * t + 128] for t in range(wide)], axis=0)
    depth = lines.shape[0]
    hits = [jnp.where(lines == b, 1.0, 0.0).astype(bf16) for b in range(spans)]
    into = lax.broadcasted_iota(i32, (128, 256), 0)
    onto = lax.broadcasted_iota(i32, (128, 256), 1)
    before = jnp.where((into < onto) | (onto >= 128), 1.0, 0.0).astype(bf16)
    inside = jnp.dot(jnp.concatenate(hits, axis=0), before, preferred_element_type=f32)
    sums = [inside[b * depth : (b + 1) * depth, 128:256] for b in range(spans)]
    lower = lax.broadcasted_iota(i32, (depth, depth), 1) < lax.broadcasted_iota(i32, (depth, depth), 0)
    above = jnp.dot(
        jnp.where(lower, 1.0, 0.0).astype(bf16),
        jnp.concatenate([x.astype(bf16) for x in sums], axis=1),
        preferred_element_type=f32,
    )
    start = jnp.zeros((1, 128), f32)
    rank = jnp.zeros((depth, 128), f32)
    for b in range(spans):
        over = above[:, b * 128 : (b + 1) * 128]
        rank = jnp.where(lines == b, inside[b * depth : (b + 1) * depth, 0:128] + over + start, rank)
        start = start + over[depth - 1 :] + sums[b][depth - 1 :]
    rank = rank.astype(i32)
    for t in range(wide):
        rank_ref[:, 128 * t : 128 * t + 128] = rank[8 * t : 8 * t + 8]

    tile_at = lax.broadcasted_iota(i32, (tiles, slots), 0).astype(f32).astype(bf16)
    place_at = lax.broadcasted_iota(i32, (tile, slots), 0).astype(f32).astype(bf16)
    ordered[...] = jnp.zeros_like(ordered)

    def order(w, _):
        to = rank_ref[pl.ds(w, 1), :]
        in_tile = jnp.where(tile_at == (to // tile).astype(f32).astype(bf16), one, zero)
        at_place = jnp.where(place_at == (to & (tile - 1)).astype(f32).astype(bf16), one, zero)
        parts = [in_tile * pieces[p, pl.ds(w, 1), :].astype(bf16) for p in range(9)]
        ordered[...] += lax.dot_general(
            jnp.concatenate(parts, axis=0),
            at_place,
            (((1,), (1,)), ((), ())),
            preferred_element_type=f32,
        )
        return 0

    lax.fori_loop(0, count, order, 0)
    where_ref[...] = ordered[0:tiles, :].astype(i32)
    copy = pltpu.make_async_copy(where_ref, first, sem)
    copy.start()
    copy.wait()

    def weights(cells, at, frac):
        here = lax.broadcasted_iota(i32, (cells, tile), 0)
        return jnp.where(here == at, 1.0 - frac, jnp.where(here == at + 1, frac, 0.0))

    def tile_of(i):
        def piece(p):
            return ordered[pl.ds(p * tiles + i, 1), :]

        span, wrap, normal = piece(0).astype(i32), piece(1).astype(i32), piece(2).astype(i32)
        f0, f1, f2 = [piece(3 + 2 * d) + piece(4 + 2 * d) for d in range(3)]
        high, low = split_two(weights(lanes, normal, f2))
        return span, f0, jnp.concatenate([high, high, low], axis=0), weights(rows, wrap, f1)

    def pair(k, made, sums):
        span, f0, along, across = made
        from_row = pl.ds(pl.multiple_of(k * 5 * rows, 16), 10 * rows)
        mixed = jnp.dot(planes[from_row, :], along, preferred_element_type=f32)
        new = list(sums)
        for n in range(2):
            ws = jnp.where(span == k + n, 1.0 - f0, jnp.where(span + 1 == k + n, f0, 0.0))
            for c in range(5):
                r0 = (5 * n + c) * rows
                total = mixed[r0 : r0 + 8] * across[0:8]
                for r in range(8, rows, 8):
                    total += mixed[r0 + r : r0 + r + 8] * across[r : r + 8]
                new[c] = ws * total if new[c] is None else new[c] + ws * total
        return tuple(new)

    def step(g, _):
        for n in range(GROUP):
            i = g * GROUP + n
            for c, x in enumerate(pair(first[i, 0], tile_of(i), (None,) * 5)):
                partial[n, c] = x
        for n in range(GROUP):
            i = g * GROUP + n
            lowest = first[i, 0]
            more = (first[i, tile - 1] + 1 - lowest) // 2

            @pl.when(more > 0)
            def _():
                made = tile_of(i)

                def again(m, _):
                    sums = pair(lowest + 2 + 2 * m, made, tuple(partial[n, c] for c in range(5)))
                    for c in range(5):
                        partial[n, c] = sums[c]
                    return 0

                lax.fori_loop(0, more, again, 0)

        for n in range(GROUP):
            i = g * GROUP + n
            for c in range(5):
                table[pl.ds(c * tiles + i, 1), :] = jnp.sum(partial[n, c], axis=0, keepdims=True)
        return 0

    lax.fori_loop(0, tiles // GROUP, step, 0)

    add_remainders(table)
    both = table[...].astype(bf16)

    def put_back(w, _):
        for t in range(0, slots, 512):
            for c, value in enumerate(lookup(both, rank_ref[pl.ds(w, 1), t : t + 512])):
                out_ref[w, c : c + 1, t : t + 512] = value
        return 0

    lax.fori_loop(0, count, put_back, 0, unroll=8)


def donors(cell, frac, state):
    _, spans, rows, lanes = state.shape
    count, slots = cell.shape
    tiles = count * slots // 256
    return pl.pallas_call(
        donor_kernel,
        grid=(1,),
        in_specs=[whole(cell.shape), whole(frac.shape), whole(state.shape)],
        out_specs=whole((count, 5, slots)),
        out_shape=jax.ShapeDtypeStruct((count, 5, slots), f32),
        scratch_shapes=[
            pltpu.VMEM(((spans + 1) * 5 * rows, 3 * lanes), bf16),
            pltpu.VMEM((9, count, slots), f32),
            pltpu.VMEM((count, slots), i32),
            pltpu.VMEM((9 * tiles, 256), f32),
            pltpu.VMEM((tiles, 256), i32),
            pltpu.SMEM((tiles, 256), i32),
            pltpu.VMEM((GROUP, 5, 8, 256), f32),
            pltpu.VMEM((10 * tiles, 256), f32),
            pltpu.SemaphoreType.DMA(()),
        ],
        compiler_params=params(),
        name="donors",
    )(cell, frac, state)


def fill_kernel(from_ref, mask_ref, q_ref, slot_ref, out_ref, norm_lo, norm_hi, span_lo, span_hi, table):
    planes = pl.num_programs(0)
    rows, lanes = from_ref.shape[1:]
    low = 256
    highs = table.shape[0] // 10
    j = pl.program_id(0)

    @pl.when(j == 0)
    def _():
        per = slot_ref.shape[2] // low
        for c in range(5):
            for w in range(slot_ref.shape[0]):
                for r in range(per):
                    value = slot_ref[w, c : c + 1, r * low : (r + 1) * low]
                    table[c * highs + w * per + r : c * highs + w * per + r + 1, :] = value
        add_remainders(table)

    both = table[...].astype(bf16)

    def row(s, _):
        keep = mask_ref[0, pl.ds(s, 1), :] == 1
        for c, value in enumerate(lookup(both, from_ref[0, pl.ds(s, 1), :])):
            out_ref[c, 0, pl.ds(s, 1), :] = jnp.where(keep, q_ref[c, 0, pl.ds(s, 1), :], value)
        return 0

    lax.fori_loop(0, rows, row, 0, unroll=16)

    for c in range(5):
        for l in range(2):
            span_lo[c, l, pl.ds(j, 1), :] = out_ref[c, 0, l : l + 1, :]
            span_hi[c, l, pl.ds(j, 1), :] = out_ref[c, 0, rows - 2 + l : rows - 1 + l, :]

    @pl.when(j < 2)
    def _():
        for c in range(5):
            norm_lo[c, j] = out_ref[c, 0]

    @pl.when(j >= planes - 2)
    def _():
        for c in range(5):
            norm_hi[c, j - (planes - 2)] = out_ref[c, 0]


def fill(source, mask, state, slot):
    _, planes, rows, lanes = state.shape
    count, _, slots = slot.shape
    plane = pl.BlockSpec((1, rows, lanes), lambda j: (j, 0, 0))
    state_plane = pl.BlockSpec((5, 1, rows, lanes), lambda j: (0, j, 0, 0))
    edges = [(5, 2, rows, lanes)] * 2 + [(5, 2, planes, lanes)] * 2
    return pl.pallas_call(
        fill_kernel,
        grid=(planes,),
        in_specs=[plane, plane, state_plane, whole(slot.shape)],
        out_specs=[state_plane] + [whole(s) for s in edges],
        out_shape=[jax.ShapeDtypeStruct(s, f32) for s in [state.shape] + edges],
        scratch_shapes=[pltpu.VMEM((10 * count * slots // 256, 256), f32)],
        compiler_params=params(),
        cost_estimate=pl.CostEstimate(flops=24 * 10**9, bytes_accessed=6 * 10**6, transcendentals=0),
        name="fill",
    )(source, mask, state, slot)


def body(
    cgrid_state, cgrid_metric, flap_state, flap_metric, iblank, fringe_from, donor_cell, donor_frac
):
    wrap_count = lax.axis_size("wrap")

    def onward(value, axis):
        size = lax.axis_size(axis)
        return lax.ppermute(value, axis, [(i, (i + 1) % size) for i in range(size)])

    def back(value, axis):
        size = lax.axis_size(axis)
        return lax.ppermute(value, axis, [((i + 1) % size, i) for i in range(size)])

    wrap_lo, wrap_hi, span_lo, span_hi, wall = pack(cgrid_state)
    far = lax.ppermute(
        wall, "wrap", [(i, wrap_count - 1 - i) for i in range(wrap_count)]
    )
    majors = (onward(span_hi, "span"), back(span_lo, "span"))
    subs = (onward(wrap_hi, "wrap"), back(wrap_lo, "wrap"))

    slot = donors(donor_cell[0], jnp.transpose(donor_frac[0], (1, 0, 2)), cgrid_state)
    slot = lax.all_to_all(slot, "wrap", split_axis=0, concat_axis=0, tiled=True)

    turned = lambda x: jnp.swapaxes(x, -3, -2)
    mask = turned(iblank)
    filled, norm_lo, norm_hi, edge_lo, edge_hi = fill(turned(fringe_from), mask, turned(flap_state), slot)
    flap_majors = (onward(norm_hi, "wrap"), back(norm_lo, "wrap"))
    flap_subs = (onward(edge_hi, "span"), back(edge_lo, "span"))

    cgrid_rate = rate(
        cgrid_state,
        majors,
        subs,
        (wrap_lo, wrap_hi, wall, far),
        cgrid_metric,
        None,
        cgrid=True,
        step_planes=4,
        components=(3, 1, 2),
        metric_rows=(0, 1, 2),
    )
    flap_rate = rate(
        filled,
        flap_majors,
        flap_subs,
        (),
        turned(flap_metric),
        mask,
        cgrid=False,
        step_planes=3,
        components=(2, 3, 1),
        metric_rows=(1, 0, 2),
    )
    return (cgrid_rate, turned(flap_rate))


def solution(mesh):
    return jax.shard_map(
        body,
        mesh=mesh,
        in_specs=(
            P(None, "span", "wrap", None),
            P(None, "span", "wrap", None),
            P(None, "span", "wrap", None),
            P(None, "span", "wrap", None),
            P("span", "wrap", None),
            P("span", "wrap", None),
            P(("wrap", "span"), None, None),
            P(("wrap", "span"), None, None, None),
        ),
        out_specs=(P(None, "span", "wrap", None), P(None, "span", "wrap", None)),
        check_vma=False,
    )
```

```python
import functools

import jax
import jax.numpy as jnp
from jax import lax
from jax.experimental import pallas as pl
from jax.experimental.pallas import tpu as pltpu
from jax.sharding import PartitionSpec as P

viscosity = 0.05
conduction = 0.07
damping = 1.0 / 32.0
VMEM_LIMIT = 56 * 1024 * 1024
GROUP = 8

f32, bf16, i32 = jnp.float32, jnp.bfloat16, jnp.int32


def whole(shape):
    return pl.BlockSpec(shape, lambda *_: (0,) * len(shape))


def params():
    return pltpu.CompilerParams(vmem_limit_bytes=VMEM_LIMIT)


def primitives(q):
    inverse = 1.0 / q[0]
    v = [q[m] * inverse for m in (1, 2, 3)]
    kinetic = 0.5 * (v[0] * v[0] + v[1] * v[1] + v[2] * v[2])
    pressure = 0.4 * (q[4] - q[0] * kinetic)
    return v + [pressure, kinetic + (conduction / viscosity) * (pressure * inverse)]


def wrapped(place, count):
    return (place < count // 4) | (place >= count - count // 4)


def flux(q, prims, m):
    u = (0.5 / damping) * prims[m - 1]
    f = [q[0] * u]
    for c in (1, 2, 3):
        f.append(q[c] * u + (0.5 / damping) * prims[3] if c == m else q[c] * u)
    f.append((q[4] + prims[3]) * u)
    return f


def pack(q_ref, wrap_lo, wrap_hi, span_lo, span_hi, wall):
    spans, rows = q_ref.shape[1], q_ref.shape[2]
    lane = lax.broadcasted_iota(i32, (rows, 128), 1)
    for c in range(5):
        for l in range(2):
            span_lo[c, l] = q_ref[c, l]
            span_hi[c, l] = q_ref[c, spans - 2 + l]
        cells = jnp.zeros((rows, 128), f32)
        for k in range(spans):
            for l in range(2):
                wrap_lo[c, l, k : k + 1, :] = q_ref[c, k, l : l + 1, :]
                wrap_hi[c, l, k : k + 1, :] = q_ref[c, k, rows - 2 + l : rows - 1 + l, :]
            near = q_ref[c, k, :, 0:128]
            if k:
                near = pltpu.roll(near, 2 * k, 1)
            cells = jnp.where(lane // 2 == k, near, cells)
        wall[c] = cells[:, 0 : 2 * spans]


def rate_kernel(
    q_hbm,
    major_lo,
    major_hi,
    sub_lo,
    sub_hi,
    *refs,
    cgrid,
    step_planes,
    components,
    metric_rows,
):
    if cgrid:
        own_lo, own_hi, wall_own, wall_far, metric_ref, out_ref, qe, prim, sub_edge, lane_edge, sems = refs
    else:
        own_lo = own_hi = None
        mask_ref, metric_ref, out_ref, qe, prim, sub_edge, sems = refs
    planes, rows, lanes = qe.shape[1] - 4, qe.shape[2], qe.shape[3]
    step = pl.program_id(0)
    place, count = lax.axis_index("wrap"), lax.axis_size("wrap")
    at_start = place == 0
    at_end = place == count - 1
    major_m, sub_m, lane_m = components

    def edge_fields(q1, q2, m, side):
        prims = primitives(q1)
        fl = flux(q1, prims, m)
        lead = [4.0 * q1[c] - side * fl[c] - q2[c] for c in range(5)]
        return lead + q1 + prims[:3] + prims[4:]

    def store_prims(k, slot):
        q = [qe[c, k] for c in range(5)]
        prims = primitives(q)
        for i, x in enumerate(prims + flux(q, prims, major_m)):
            prim[slot, i] = x

    steps = planes // step_planes

    def part(n):
        n = n * step_planes
        return pltpu.make_async_copy(
            q_hbm.at[:, pl.ds(n, step_planes)], qe.at[:, pl.ds(n + 2, step_planes)], sems.at[n // step_planes]
        )

    @pl.when(step == 0)
    def _():
        copies = [
            pltpu.make_async_copy(major_lo, qe.at[:, pl.ds(0, 2)], sems.at[steps]),
            pltpu.make_async_copy(major_hi, qe.at[:, pl.ds(planes + 2, 2)], sems.at[steps + 1]),
        ]
        copies[0].start()
        for n in range(steps):
            part(n).start()
        copies[1].start()
        for side, ref, own in ((-1, sub_lo, own_lo), (1, sub_hi, own_hi)):
            near, far = (1, 0) if side < 0 else (0, 1)
            q1 = [ref[c, near] for c in range(5)]
            q2 = [ref[c, far] for c in range(5)]
            if cgrid:
                edge = at_start if side < 0 else at_end
                clamp = 0 if side < 0 else 1
                q1 = [jnp.where(edge, own[c, clamp], q1[c]) for c in range(5)]
                q2 = [jnp.where(edge, own[c, clamp], q2[c]) for c in range(5)]
            for i, x in enumerate(edge_fields(q1, q2, sub_m, side)):
                sub_edge[(side + 1) // 2, i] = x
        if cgrid:
            in_wake = wrapped(place, count)
            turn = 7 - lax.broadcasted_iota(i32, (8, 128), 0)
            ghosts = []
            for c in range(5):
                sign = -1.0 if c in (1, 2, 3) else 1.0
                parts = []
                for r in range(rows // 8):
                    far = wall_far[c, rows - 8 - 8 * r : rows - 8 * r, :]
                    own = wall_own[c, 8 * r : 8 * r + 8, :]
                    own = jnp.concatenate([own, jnp.zeros((8, 128 - own.shape[1]), f32)], axis=1)
                    far = jnp.concatenate([far, jnp.zeros((8, 128 - far.shape[1]), f32)], axis=1)
                    far = jnp.take_along_axis(far, turn, axis=0, mode="promise_in_bounds")
                    parts.append(jnp.where(in_wake, far, sign * own))
                ghosts.append(jnp.concatenate(parts, axis=0))
            second = [pltpu.roll(x, 127, 1) for x in ghosts]
            for i, x in enumerate(edge_fields(ghosts, second, lane_m, -1)):
                lane_edge[i] = x
        copies[0].wait()
        part(0).wait()
        part(1).wait()
        copies[1].wait()
        if not cgrid:

            @pl.when(at_start)
            def _():
                for c in range(5):
                    sign = -1.0 if c in (1, 2, 3) else 1.0
                    qe[c, 1] = sign * qe[c, 2]
                    qe[c, 0] = sign * qe[c, 3]

        store_prims(1, 0)
        store_prims(2, 1)

    @pl.when((step > 0) & (step < steps - 1))
    def _():
        part(step + 1).wait()

    if not cgrid:

        @pl.when((step == steps - 1) & at_end)
        def _():
            for c in range(5):
                qe[c, planes + 2] = qe[c, planes + 1]
                qe[c, planes + 3] = qe[c, planes + 1]

    row_at = lax.broadcasted_iota(i32, (8, lanes), 0)
    lane_at = lax.broadcasted_iota(i32, (rows, 128), 1)
    row_first, row_last = row_at == 0, row_at == 7
    lane_first, lane_last = lane_at == 0, lane_at == 127

    def one(b, _):
        k = step * step_planes + b
        here, below, above = lax.rem(k + 1, 3), lax.rem(k, 3), lax.rem(k + 2, 3)
        store_prims(k + 3, above)

        def sub_next(x, i):
            moved = [pltpu.roll(x[r : r + 8], 7, 0) for r in range(0, rows, 8)]
            moved.append(sub_edge[1, i, pl.ds(k, 1), :])
            return jnp.concatenate(
                [jnp.where(row_last, moved[r + 1], moved[r]) for r in range(rows // 8)], axis=0
            )

        def sub_prior(x, i):
            moved = [sub_edge[0, i, pl.ds(k, 1), :]]
            moved += [pltpu.roll(x[r : r + 8], 1, 0) for r in range(0, rows, 8)]
            return jnp.concatenate(
                [jnp.where(row_first, moved[r], moved[r + 1]) for r in range(rows // 8)], axis=0
            )

        def lane_next(x):
            moved = [pltpu.roll(x[:, t : t + 128], 127, 1) for t in range(0, lanes, 128)]
            moved.append(x[:, lanes - 128 :] if cgrid else moved[0])
            return jnp.concatenate(
                [jnp.where(lane_last, moved[t + 1], moved[t]) for t in range(lanes // 128)], axis=1
            )

        def lane_prior(x, i):
            moved = [pltpu.roll(x[:, t : t + 128], 1, 1) for t in range(0, lanes, 128)]
            if cgrid:
                moved.insert(0, pltpu.roll(lane_edge[i], lax.rem(128 - 2 * k, 128), 1))
            else:
                moved.insert(0, moved[-1])
            return jnp.concatenate(
                [jnp.where(lane_first, moved[t], moved[t + 1]) for t in range(lanes // 128)], axis=1
            )

        gm = metric_ref[metric_rows[0], b]
        gs = metric_ref[metric_rows[1], b]
        gl = metric_ref[metric_rows[2], b]
        gm2, gs2, gl2 = viscosity * gm * gm, viscosity * gs * gs, viscosity * gl * gl
        gm, gs, gl = damping * gm, damping * gs, damping * gl
        all2 = 2.0 * (gm2 + gs2 + gl2)
        all6 = 6.0 * (gm + gs + gl)
        mine = [prim[here, i] for i in range(5)]
        viscous = {}
        for i, c, e in ((0, 1, 10), (1, 2, 11), (2, 3, 12), (4, 4, 13)):
            x = mine[i]
            total = gm2 * (prim[above, i] + prim[below, i])
            total += gs2 * (sub_next(x, e) + sub_prior(x, e))
            total += gl2 * (lane_next(x) + lane_prior(x, e))
            viscous[c] = total - all2 * x
        q = [qe[c, k + 2] for c in range(5)]
        sub_flux = flux(q, mine, sub_m)
        lane_flux = flux(q, mine, lane_m)
        for c in range(5):
            x = q[c]
            four = 4.0 * x
            total = gm * (
                4.0 * (qe[c, k + 3] + qe[c, k + 1])
                - (qe[c, k + 4] + qe[c, k])
                - (prim[above, 5 + c] - prim[below, 5 + c])
            )
            up = four - sub_flux[c] - sub_next(x, 5 + c)
            down = four + sub_flux[c] - sub_prior(x, 5 + c)
            total += gs * (sub_next(up, c) + sub_prior(down, c))
            up = four - lane_flux[c] - lane_next(x)
            down = four + lane_flux[c] - lane_prior(x, 5 + c)
            total += gl * (lane_next(up) + lane_prior(down, c))
            total -= all6 * x
            if c:
                total += viscous[c]
            if not cgrid:
                total = jnp.where(mask_ref[b] == 1, total, 0.0)
            out_ref[c, b] = total
        return 0

    lax.fori_loop(0, step_planes, one, 0)


def rate(q, majors, subs, extras, metric, mask, *, cgrid, step_planes, components, metric_rows):
    _, planes, rows, lanes = q.shape
    anywhere = pl.BlockSpec(memory_space=pl.ANY)
    block = lambda n: pl.BlockSpec((n, step_planes, rows, lanes), lambda i: (0, i, 0, 0))
    last_specs = [block(3)]
    last = (metric,)
    if mask is not None:
        last_specs = [pl.BlockSpec((step_planes, rows, lanes), lambda i: (i, 0, 0))] + last_specs
        last = (mask, metric)
    return pl.pallas_call(
        functools.partial(
            rate_kernel,
            cgrid=cgrid,
            step_planes=step_planes,
            components=components,
            metric_rows=metric_rows,
        ),
        grid=(planes // step_planes,),
        in_specs=[anywhere] * 3 + [whole(x.shape) for x in (*subs, *extras)] + last_specs,
        out_specs=block(5),
        out_shape=jax.ShapeDtypeStruct(q.shape, f32),
        scratch_shapes=[
            pltpu.VMEM((5, planes + 4, rows, lanes), f32),
            pltpu.VMEM((3, 10, rows, lanes), f32),
            pltpu.VMEM((2, 14, planes, lanes), f32),
        ]
        + [pltpu.VMEM((14, rows, 128), f32)] * cgrid
        + [pltpu.SemaphoreType.DMA((planes // step_planes + 2,))],
        compiler_params=params(),
        cost_estimate=pl.CostEstimate(
            flops=300 * planes * rows * lanes, bytes_accessed=60 * planes * rows * lanes, transcendentals=0
        ),
        name="cgrid_rate" if cgrid else "flap_rate",
    )(q, *majors, *subs, *extras, *last)


def split_two(x):
    high = x.astype(bf16)
    return high, (x - high.astype(f32)).astype(bf16)


def lookup(both, at):
    width = at.shape[1]
    highs = both.shape[0] // 10
    cells = lax.broadcasted_iota(i32, (256, width), 0).astype(f32).astype(bf16)
    sub = lax.broadcasted_iota(i32, (8, width), 0)
    pick = jnp.where(
        cells == (at & 255).astype(f32).astype(bf16), jnp.ones((), bf16), jnp.zeros((), bf16)
    )
    high = at // 256
    found = jnp.dot(both, pick, preferred_element_type=f32)
    masks = [sub + 8 * g == high for g in range(highs // 8)]
    values = []
    for c in range(5):
        value = None
        for g, mask in enumerate(masks):
            r = c * highs + 8 * g
            piece = found[r : r + 8] + found[5 * highs + r : 5 * highs + r + 8]
            value = jnp.where(mask, piece, 0.0 if value is None else value)
        values.append(jnp.sum(value, axis=0, keepdims=True))
    return values


def add_remainders(table):
    half = table.shape[0] // 2
    for r in range(0, half, 8):
        value = table[r : r + 8, :]
        table[half + r : half + r + 8, :] = value - value.astype(bf16).astype(f32)


def donor_kernel(
    cell_ref,
    frac_ref,
    q_ref,
    out_ref,
    wrap_lo,
    wrap_hi,
    span_lo,
    span_hi,
    wall,
    planes,
    pieces,
    rank_ref,
    ordered,
    where_ref,
    first,
    partial,
    table,
    sem,
):
    spans, rows, lanes = q_ref.shape[1:]
    count, slots = cell_ref.shape
    tile = 256
    tiles = count * slots // tile
    wide = slots // 128
    one, zero = jnp.ones((), bf16), jnp.zeros((), bf16)
    pack(q_ref, wrap_lo, wrap_hi, span_lo, span_hi, wall)

    def prepare(k, _):
        for c in range(5):
            high, low = split_two(q_ref[c, k])
            here = pl.ds(pl.multiple_of(k * 5 * rows + c * rows, 16), rows)
            planes[here, 0:lanes] = high
            planes[here, lanes : 2 * lanes] = low
            planes[here, 2 * lanes : 3 * lanes] = high
        return 0

    lax.fori_loop(0, spans, prepare, 0)
    planes[spans * 5 * rows :, :] = jnp.zeros((5 * rows, 3 * lanes), bf16)

    cell = cell_ref[...]
    upper = jnp.floor((cell.astype(f32) + 0.5) * (1.0 / (lanes - 1)))
    span = jnp.floor((upper + 0.5) * (1.0 / (rows - 1)))
    pieces[0] = span
    pieces[1] = upper - span * (rows - 1)
    pieces[2] = cell.astype(f32) - upper * (lanes - 1)
    for d in range(3):
        f = frac_ref[d]
        high = f.astype(bf16).astype(f32)
        pieces[3 + 2 * d] = high
        pieces[4 + 2 * d] = f - high

    lines = jnp.concatenate([span[:, 128 * t : 128 * t + 128] for t in range(wide)], axis=0)
    depth = lines.shape[0]
    hits = [jnp.where(lines == b, 1.0, 0.0).astype(bf16) for b in range(spans)]
    into = lax.broadcasted_iota(i32, (128, 256), 0)
    onto = lax.broadcasted_iota(i32, (128, 256), 1)
    before = jnp.where((into < onto) | (onto >= 128), 1.0, 0.0).astype(bf16)
    inside = jnp.dot(jnp.concatenate(hits, axis=0), before, preferred_element_type=f32)
    sums = [inside[b * depth : (b + 1) * depth, 128:256] for b in range(spans)]
    lower = lax.broadcasted_iota(i32, (depth, depth), 1) < lax.broadcasted_iota(i32, (depth, depth), 0)
    above = jnp.dot(
        jnp.where(lower, 1.0, 0.0).astype(bf16),
        jnp.concatenate([x.astype(bf16) for x in sums], axis=1),
        preferred_element_type=f32,
    )
    start = jnp.zeros((1, 128), f32)
    rank = jnp.zeros((depth, 128), f32)
    for b in range(spans):
        over = above[:, b * 128 : (b + 1) * 128]
        rank = jnp.where(lines == b, inside[b * depth : (b + 1) * depth, 0:128] + over + start, rank)
        start = start + over[depth - 1 :] + sums[b][depth - 1 :]
    rank = rank.astype(i32)
    for t in range(wide):
        rank_ref[:, 128 * t : 128 * t + 128] = rank[8 * t : 8 * t + 8]

    tile_at = lax.broadcasted_iota(i32, (tiles, slots), 0).astype(f32).astype(bf16)
    place_at = lax.broadcasted_iota(i32, (tile, slots), 0).astype(f32).astype(bf16)
    ordered[...] = jnp.zeros_like(ordered)

    def order(w, _):
        to = rank_ref[pl.ds(w, 1), :]
        in_tile = jnp.where(tile_at == (to // tile).astype(f32).astype(bf16), one, zero)
        at_place = jnp.where(place_at == (to & (tile - 1)).astype(f32).astype(bf16), one, zero)
        parts = [in_tile * pieces[p, pl.ds(w, 1), :].astype(bf16) for p in range(9)]
        ordered[...] += lax.dot_general(
            jnp.concatenate(parts, axis=0),
            at_place,
            (((1,), (1,)), ((), ())),
            preferred_element_type=f32,
        )
        return 0

    lax.fori_loop(0, count, order, 0)
    where_ref[...] = ordered[0:tiles, :].astype(i32)
    copy = pltpu.make_async_copy(where_ref, first, sem)
    copy.start()
    copy.wait()

    def weights(cells, at, frac):
        here = lax.broadcasted_iota(i32, (cells, tile), 0)
        return jnp.where(here == at, 1.0 - frac, jnp.where(here == at + 1, frac, 0.0))

    def tile_of(i):
        def piece(p):
            return ordered[pl.ds(p * tiles + i, 1), :]

        span, wrap, normal = piece(0).astype(i32), piece(1).astype(i32), piece(2).astype(i32)
        f0, f1, f2 = [piece(3 + 2 * d) + piece(4 + 2 * d) for d in range(3)]
        high, low = split_two(weights(lanes, normal, f2))
        return span, f0, jnp.concatenate([high, high, low], axis=0), weights(rows, wrap, f1)

    def pair(k, made, sums):
        span, f0, along, across = made
        from_row = pl.ds(pl.multiple_of(k * 5 * rows, 16), 10 * rows)
        mixed = jnp.dot(planes[from_row, :], along, preferred_element_type=f32)
        new = list(sums)
        for n in range(2):
            ws = jnp.where(span == k + n, 1.0 - f0, jnp.where(span + 1 == k + n, f0, 0.0))
            for c in range(5):
                r0 = (5 * n + c) * rows
                total = mixed[r0 : r0 + 8] * across[0:8]
                for r in range(8, rows, 8):
                    total += mixed[r0 + r : r0 + r + 8] * across[r : r + 8]
                new[c] = ws * total if new[c] is None else new[c] + ws * total
        return tuple(new)

    def step(g, _):
        for n in range(GROUP):
            i = g * GROUP + n
            for c, x in enumerate(pair(first[i, 0], tile_of(i), (None,) * 5)):
                partial[n, c] = x
        for n in range(GROUP):
            i = g * GROUP + n
            lowest = first[i, 0]
            more = (first[i, tile - 1] + 1 - lowest) // 2

            @pl.when(more > 0)
            def _():
                made = tile_of(i)

                def again(m, _):
                    sums = pair(lowest + 2 + 2 * m, made, tuple(partial[n, c] for c in range(5)))
                    for c in range(5):
                        partial[n, c] = sums[c]
                    return 0

                lax.fori_loop(0, more, again, 0)

        for n in range(GROUP):
            i = g * GROUP + n
            for c in range(5):
                table[pl.ds(c * tiles + i, 1), :] = jnp.sum(partial[n, c], axis=0, keepdims=True)
        return 0

    lax.fori_loop(0, tiles // GROUP, step, 0)

    add_remainders(table)
    both = table[...].astype(bf16)

    def put_back(w, _):
        for t in range(0, slots, 512):
            for c, value in enumerate(lookup(both, rank_ref[pl.ds(w, 1), t : t + 512])):
                out_ref[w, c : c + 1, t : t + 512] = value
        return 0

    lax.fori_loop(0, count, put_back, 0, unroll=8)


def donors(cell, frac, state):
    _, spans, rows, lanes = state.shape
    count, slots = cell.shape
    tiles = count * slots // 256
    shapes = [(count, 5, slots)]
    shapes += [(5, 2, spans, lanes)] * 2 + [(5, 2, rows, lanes)] * 2 + [(5, rows, 2 * spans)]
    return pl.pallas_call(
        donor_kernel,
        grid=(1,),
        in_specs=[whole(cell.shape), whole(frac.shape), whole(state.shape)],
        out_specs=[whole(x) for x in shapes],
        out_shape=[jax.ShapeDtypeStruct(x, f32) for x in shapes],
        scratch_shapes=[
            pltpu.VMEM(((spans + 1) * 5 * rows, 3 * lanes), bf16),
            pltpu.VMEM((9, count, slots), f32),
            pltpu.VMEM((count, slots), i32),
            pltpu.VMEM((9 * tiles, 256), f32),
            pltpu.VMEM((tiles, 256), i32),
            pltpu.SMEM((tiles, 256), i32),
            pltpu.VMEM((GROUP, 5, 8, 256), f32),
            pltpu.VMEM((10 * tiles, 256), f32),
            pltpu.SemaphoreType.DMA(()),
        ],
        compiler_params=params(),
        name="donors",
    )(cell, frac, state)


def fill_kernel(from_ref, mask_ref, q_ref, slot_ref, out_ref, norm_lo, norm_hi, span_lo, span_hi, table):
    planes = pl.num_programs(0)
    rows, lanes = from_ref.shape[1:]
    low = 256
    highs = table.shape[0] // 10
    j = pl.program_id(0)

    @pl.when(j == 0)
    def _():
        per = slot_ref.shape[2] // low
        for c in range(5):
            for w in range(slot_ref.shape[0]):
                for r in range(per):
                    value = slot_ref[w, c : c + 1, r * low : (r + 1) * low]
                    table[c * highs + w * per + r : c * highs + w * per + r + 1, :] = value
        add_remainders(table)

    both = table[...].astype(bf16)

    def row(s, _):
        keep = mask_ref[0, pl.ds(s, 1), :] == 1
        for c, value in enumerate(lookup(both, from_ref[0, pl.ds(s, 1), :])):
            out_ref[c, 0, pl.ds(s, 1), :] = jnp.where(keep, q_ref[c, 0, pl.ds(s, 1), :], value)
        return 0

    lax.fori_loop(0, rows, row, 0, unroll=16)

    for c in range(5):
        for l in range(2):
            span_lo[c, l, pl.ds(j, 1), :] = out_ref[c, 0, l : l + 1, :]
            span_hi[c, l, pl.ds(j, 1), :] = out_ref[c, 0, rows - 2 + l : rows - 1 + l, :]

    @pl.when(j < 2)
    def _():
        for c in range(5):
            norm_lo[c, j] = out_ref[c, 0]

    @pl.when(j >= planes - 2)
    def _():
        for c in range(5):
            norm_hi[c, j - (planes - 2)] = out_ref[c, 0]


def fill(source, mask, state, slot):
    _, planes, rows, lanes = state.shape
    count, _, slots = slot.shape
    plane = pl.BlockSpec((1, rows, lanes), lambda j: (j, 0, 0))
    state_plane = pl.BlockSpec((5, 1, rows, lanes), lambda j: (0, j, 0, 0))
    edges = [(5, 2, rows, lanes)] * 2 + [(5, 2, planes, lanes)] * 2
    return pl.pallas_call(
        fill_kernel,
        grid=(planes,),
        in_specs=[plane, plane, state_plane, whole(slot.shape)],
        out_specs=[state_plane] + [whole(s) for s in edges],
        out_shape=[jax.ShapeDtypeStruct(s, f32) for s in [state.shape] + edges],
        scratch_shapes=[pltpu.VMEM((10 * count * slots // 256, 256), f32)],
        compiler_params=params(),
        cost_estimate=pl.CostEstimate(flops=24 * 10**9, bytes_accessed=6 * 10**6, transcendentals=0),
        name="fill",
    )(source, mask, state, slot)


def body(
    cgrid_state, cgrid_metric, flap_state, flap_metric, iblank, fringe_from, donor_cell, donor_frac
):
    wrap_count = lax.axis_size("wrap")

    def ring(axis):
        size = lax.axis_size(axis)
        return [(i, (i + 1) % size) for i in range(size if axis == "span" else size - 1)]

    def onward(value, axis):
        return lax.ppermute(value, axis, ring(axis))

    def back(value, axis):
        return lax.ppermute(value, axis, [(j, i) for i, j in ring(axis)])

    slot, wrap_lo, wrap_hi, span_lo, span_hi, wall = donors(
        donor_cell[0], jnp.transpose(donor_frac[0], (1, 0, 2)), cgrid_state
    )
    far = lax.ppermute(
        wall, "wrap", [(i, wrap_count - 1 - i) for i in range(wrap_count) if wrapped(i, wrap_count)]
    )
    majors = (onward(span_hi, "span"), back(span_lo, "span"))
    subs = (onward(wrap_hi, "wrap"), back(wrap_lo, "wrap"))

    slot = lax.all_to_all(slot, "wrap", split_axis=0, concat_axis=0, tiled=True)

    turned = lambda x: jnp.swapaxes(x, -3, -2)
    mask = turned(iblank)
    filled, norm_lo, norm_hi, edge_lo, edge_hi = fill(turned(fringe_from), mask, turned(flap_state), slot)
    flap_majors = (onward(norm_hi, "wrap"), back(norm_lo, "wrap"))
    flap_subs = (onward(edge_hi, "span"), back(edge_lo, "span"))

    cgrid_rate = rate(
        cgrid_state,
        majors,
        subs,
        (wrap_lo, wrap_hi, wall, far),
        cgrid_metric,
        None,
        cgrid=True,
        step_planes=4,
        components=(3, 1, 2),
        metric_rows=(0, 1, 2),
    )
    flap_rate = rate(
        filled,
        flap_majors,
        flap_subs,
        (),
        turned(flap_metric),
        mask,
        cgrid=False,
        step_planes=3,
        components=(2, 3, 1),
        metric_rows=(1, 0, 2),
    )
    return (cgrid_rate, turned(flap_rate))


def solution(mesh):
    return jax.shard_map(
        body,
        mesh=mesh,
        in_specs=(
            P(None, "span", "wrap", None),
            P(None, "span", "wrap", None),
            P(None, "span", "wrap", None),
            P(None, "span", "wrap", None),
            P("span", "wrap", None),
            P("span", "wrap", None),
            P(("wrap", "span"), None, None),
            P(("wrap", "span"), None, None, None),
        ),
        out_specs=(P(None, "span", "wrap", None), P(None, "span", "wrap", None)),
        check_vma=False,
    )
```

```python
import functools

import jax
import jax.numpy as jnp
from jax import lax
from jax.experimental import pallas as pl
from jax.experimental.pallas import tpu as pltpu
from jax.sharding import PartitionSpec as P

viscosity = 0.05
conduction = 0.07
damping = 1.0 / 32.0
VMEM_LIMIT = 40 * 1024 * 1024
IN_VMEM = pl.BlockSpec(memory_space=pltpu.VMEM)
GROUP = 8

f32, bf16, i32 = jnp.float32, jnp.bfloat16, jnp.int32


def whole(shape):
    return pl.BlockSpec(shape, lambda *_: (0,) * len(shape))


def params():
    return pltpu.CompilerParams(vmem_limit_bytes=VMEM_LIMIT)


def primitives(q):
    inverse = 1.0 / q[0]
    v = [q[m] * inverse for m in (1, 2, 3)]
    kinetic = 0.5 * (v[0] * v[0] + v[1] * v[1] + v[2] * v[2])
    pressure = 0.4 * (q[4] - q[0] * kinetic)
    return v + [pressure, kinetic + (conduction / viscosity) * (pressure * inverse)]


def wrapped(place, count):
    return (place < count // 4) | (place >= count - count // 4)


def flux(q, prims, m):
    u = (0.5 / damping) * prims[m - 1]
    f = [q[0] * u]
    for c in (1, 2, 3):
        f.append(q[c] * u + (0.5 / damping) * prims[3] if c == m else q[c] * u)
    f.append((q[4] + prims[3]) * u)
    return f


def pack(q_ref, wrap_lo, wrap_hi, span_lo, span_hi, wall):
    spans, rows = q_ref.shape[1], q_ref.shape[2]
    lane = lax.broadcasted_iota(i32, (rows, 128), 1)
    for c in range(5):
        for l in range(2):
            span_lo[c, l] = q_ref[c, l]
            span_hi[c, l] = q_ref[c, spans - 2 + l]
        cells = jnp.zeros((rows, 128), f32)
        for k in range(spans):
            for l in range(2):
                wrap_lo[c, l, k : k + 1, :] = q_ref[c, k, l : l + 1, :]
                wrap_hi[c, l, k : k + 1, :] = q_ref[c, k, rows - 2 + l : rows - 1 + l, :]
            near = q_ref[c, k, :, 0:128]
            if k:
                near = pltpu.roll(near, 2 * k, 1)
            cells = jnp.where(lane // 2 == k, near, cells)
        wall[c] = cells[:, 0 : 2 * spans]


def rate_kernel(
    q_hbm,
    major_lo,
    major_hi,
    sub_lo,
    sub_hi,
    *refs,
    cgrid,
    step_planes,
    components,
    metric_rows,
):
    if cgrid:
        own_lo, own_hi, wall_own, wall_far, metric_ref, out_ref, qe, prim, sub_edge, lane_edge, sems = refs
    else:
        own_lo = own_hi = None
        mask_ref, metric_ref, out_ref, qe, prim, sub_edge, sems = refs
    planes, rows, lanes = qe.shape[1] - 4, qe.shape[2], qe.shape[3]
    step = pl.program_id(0)
    place, count = lax.axis_index("wrap"), lax.axis_size("wrap")
    at_start = place == 0
    at_end = place == count - 1
    major_m, sub_m, lane_m = components

    def edge_fields(q1, q2, m, side):
        prims = primitives(q1)
        fl = flux(q1, prims, m)
        lead = [4.0 * q1[c] - side * fl[c] - q2[c] for c in range(5)]
        return lead + q1 + prims[:3] + prims[4:]

    def store_prims(k, slot):
        q = [qe[c, k] for c in range(5)]
        prims = primitives(q)
        for i, x in enumerate(prims + flux(q, prims, major_m)):
            prim[slot, i] = x

    steps = planes // step_planes

    def part(n):
        n = n * step_planes
        return pltpu.make_async_copy(
            q_hbm.at[:, pl.ds(n, step_planes)], qe.at[:, pl.ds(n + 2, step_planes)], sems.at[n // step_planes]
        )

    @pl.when(step == 0)
    def _():
        copies = [
            pltpu.make_async_copy(major_lo, qe.at[:, pl.ds(0, 2)], sems.at[steps]),
            pltpu.make_async_copy(major_hi, qe.at[:, pl.ds(planes + 2, 2)], sems.at[steps + 1]),
        ]
        copies[0].start()
        for n in range(steps):
            part(n).start()
        copies[1].start()
        for side, ref, own in ((-1, sub_lo, own_lo), (1, sub_hi, own_hi)):
            near, far = (1, 0) if side < 0 else (0, 1)
            q1 = [ref[c, near] for c in range(5)]
            q2 = [ref[c, far] for c in range(5)]
            if cgrid:
                edge = at_start if side < 0 else at_end
                clamp = 0 if side < 0 else 1
                q1 = [jnp.where(edge, own[c, clamp], q1[c]) for c in range(5)]
                q2 = [jnp.where(edge, own[c, clamp], q2[c]) for c in range(5)]
            for i, x in enumerate(edge_fields(q1, q2, sub_m, side)):
                sub_edge[(side + 1) // 2, i] = x
        if cgrid:
            in_wake = wrapped(place, count)
            turn = 7 - lax.broadcasted_iota(i32, (8, 128), 0)
            ghosts = []
            for c in range(5):
                sign = -1.0 if c in (1, 2, 3) else 1.0
                parts = []
                for r in range(rows // 8):
                    far = wall_far[c, rows - 8 - 8 * r : rows - 8 * r, :]
                    own = wall_own[c, 8 * r : 8 * r + 8, :]
                    own = jnp.concatenate([own, jnp.zeros((8, 128 - own.shape[1]), f32)], axis=1)
                    far = jnp.concatenate([far, jnp.zeros((8, 128 - far.shape[1]), f32)], axis=1)
                    far = jnp.take_along_axis(far, turn, axis=0, mode="promise_in_bounds")
                    parts.append(jnp.where(in_wake, far, sign * own))
                ghosts.append(jnp.concatenate(parts, axis=0))
            second = [pltpu.roll(x, 127, 1) for x in ghosts]
            for i, x in enumerate(edge_fields(ghosts, second, lane_m, -1)):
                lane_edge[i] = x
        copies[0].wait()
        part(0).wait()
        part(1).wait()
        copies[1].wait()
        if not cgrid:

            @pl.when(at_start)
            def _():
                for c in range(5):
                    sign = -1.0 if c in (1, 2, 3) else 1.0
                    qe[c, 1] = sign * qe[c, 2]
                    qe[c, 0] = sign * qe[c, 3]

        store_prims(1, 0)
        store_prims(2, 1)

    @pl.when((step > 0) & (step < steps - 1))
    def _():
        part(step + 1).wait()

    if not cgrid:

        @pl.when((step == steps - 1) & at_end)
        def _():
            for c in range(5):
                qe[c, planes + 2] = qe[c, planes + 1]
                qe[c, planes + 3] = qe[c, planes + 1]

    row_at = lax.broadcasted_iota(i32, (8, lanes), 0)
    lane_at = lax.broadcasted_iota(i32, (rows, 128), 1)
    row_first, row_last = row_at == 0, row_at == 7
    lane_first, lane_last = lane_at == 0, lane_at == 127

    def one(b, _):
        k = step * step_planes + b
        here, below, above = lax.rem(k + 1, 3), lax.rem(k, 3), lax.rem(k + 2, 3)
        store_prims(k + 3, above)

        def sub_next(x, i):
            moved = [pltpu.roll(x[r : r + 8], 7, 0) for r in range(0, rows, 8)]
            moved.append(sub_edge[1, i, pl.ds(k, 1), :])
            return jnp.concatenate(
                [jnp.where(row_last, moved[r + 1], moved[r]) for r in range(rows // 8)], axis=0
            )

        def sub_prior(x, i):
            moved = [sub_edge[0, i, pl.ds(k, 1), :]]
            moved += [pltpu.roll(x[r : r + 8], 1, 0) for r in range(0, rows, 8)]
            return jnp.concatenate(
                [jnp.where(row_first, moved[r], moved[r + 1]) for r in range(rows // 8)], axis=0
            )

        def lane_next(x):
            moved = [pltpu.roll(x[:, t : t + 128], 127, 1) for t in range(0, lanes, 128)]
            moved.append(x[:, lanes - 128 :] if cgrid else moved[0])
            return jnp.concatenate(
                [jnp.where(lane_last, moved[t + 1], moved[t]) for t in range(lanes // 128)], axis=1
            )

        def lane_prior(x, i):
            moved = [pltpu.roll(x[:, t : t + 128], 1, 1) for t in range(0, lanes, 128)]
            if cgrid:
                moved.insert(0, pltpu.roll(lane_edge[i], lax.rem(128 - 2 * k, 128), 1))
            else:
                moved.insert(0, moved[-1])
            return jnp.concatenate(
                [jnp.where(lane_first, moved[t], moved[t + 1]) for t in range(lanes // 128)], axis=1
            )

        gm = metric_ref[metric_rows[0], b]
        gs = metric_ref[metric_rows[1], b]
        gl = metric_ref[metric_rows[2], b]
        gm2, gs2, gl2 = viscosity * gm * gm, viscosity * gs * gs, viscosity * gl * gl
        gm, gs, gl = damping * gm, damping * gs, damping * gl
        all2 = 2.0 * (gm2 + gs2 + gl2)
        all6 = 6.0 * (gm + gs + gl)
        mine = [prim[here, i] for i in range(5)]
        viscous = {}
        for i, c, e in ((0, 1, 10), (1, 2, 11), (2, 3, 12), (4, 4, 13)):
            x = mine[i]
            total = gm2 * (prim[above, i] + prim[below, i])
            total += gs2 * (sub_next(x, e) + sub_prior(x, e))
            total += gl2 * (lane_next(x) + lane_prior(x, e))
            viscous[c] = total - all2 * x
        q = [qe[c, k + 2] for c in range(5)]
        sub_flux = flux(q, mine, sub_m)
        lane_flux = flux(q, mine, lane_m)
        for c in range(5):
            x = q[c]
            four = 4.0 * x
            total = gm * (
                4.0 * (qe[c, k + 3] + qe[c, k + 1])
                - (qe[c, k + 4] + qe[c, k])
                - (prim[above, 5 + c] - prim[below, 5 + c])
            )
            up = four - sub_flux[c] - sub_next(x, 5 + c)
            down = four + sub_flux[c] - sub_prior(x, 5 + c)
            total += gs * (sub_next(up, c) + sub_prior(down, c))
            up = four - lane_flux[c] - lane_next(x)
            down = four + lane_flux[c] - lane_prior(x, 5 + c)
            total += gl * (lane_next(up) + lane_prior(down, c))
            total -= all6 * x
            if c:
                total += viscous[c]
            if not cgrid:
                total = jnp.where(mask_ref[b] == 1, total, 0.0)
            out_ref[c, b] = total
        return 0

    lax.fori_loop(0, step_planes, one, 0)


def rate(q, majors, subs, extras, metric, mask, *, cgrid, step_planes, components, metric_rows):
    _, planes, rows, lanes = q.shape
    anywhere = pl.BlockSpec(memory_space=pl.ANY)
    block = lambda n: pl.BlockSpec((n, step_planes, rows, lanes), lambda i: (0, i, 0, 0))
    last_specs = [block(3)]
    last = (metric,)
    if mask is not None:
        last_specs = [pl.BlockSpec((step_planes, rows, lanes), lambda i: (i, 0, 0))] + last_specs
        last = (mask, metric)
    return pl.pallas_call(
        functools.partial(
            rate_kernel,
            cgrid=cgrid,
            step_planes=step_planes,
            components=components,
            metric_rows=metric_rows,
        ),
        grid=(planes // step_planes,),
        in_specs=[anywhere] + [IN_VMEM] * (4 + len(extras)) + last_specs,
        out_specs=block(5),
        out_shape=jax.ShapeDtypeStruct(q.shape, f32),
        scratch_shapes=[
            pltpu.VMEM((5, planes + 4, rows, lanes), f32),
            pltpu.VMEM((3, 10, rows, lanes), f32),
            pltpu.VMEM((2, 14, planes, lanes), f32),
        ]
        + [pltpu.VMEM((14, rows, 128), f32)] * cgrid
        + [pltpu.SemaphoreType.DMA((planes // step_planes + 2,))],
        compiler_params=params(),
        cost_estimate=pl.CostEstimate(
            flops=300 * planes * rows * lanes, bytes_accessed=60 * planes * rows * lanes, transcendentals=0
        ),
        name="cgrid_rate" if cgrid else "flap_rate",
    )(q, *majors, *subs, *extras, *last)


def split_two(x):
    high = x.astype(bf16)
    return high, (x - high.astype(f32)).astype(bf16)


def lookup(both, at):
    width = at.shape[1]
    highs = 32
    components = both.shape[0] // (2 * highs)
    cells = lax.broadcasted_iota(i32, (256, width), 0).astype(f32).astype(bf16)
    sub = lax.broadcasted_iota(i32, (8, width), 0)
    pick = jnp.where(
        cells == (at & 255).astype(f32).astype(bf16), jnp.ones((), bf16), jnp.zeros((), bf16)
    )
    high = at // 256
    found = jnp.dot(both, pick, preferred_element_type=f32)
    masks = [sub + 8 * g == high for g in range(highs // 8)]
    values = []
    for c in range(components):
        value = None
        for g, mask in enumerate(masks):
            r = c * highs + 8 * g
            remainder = components * highs + r
            piece = found[r : r + 8] + found[remainder : remainder + 8]
            value = jnp.where(mask, piece, 0.0 if value is None else value)
        values.append(jnp.sum(value, axis=0, keepdims=True))
    return values


def take_lanes(values, lanes):
    return lax.gather(
        values,
        lanes[..., None],
        lax.GatherDimensionNumbers(
            offset_dims=(),
            collapsed_slice_dims=(1,),
            start_index_map=(1,),
            operand_batching_dims=(0,),
            start_indices_batching_dims=(0,),
        ),
        slice_sizes=(1, 1),
        mode=lax.GatherScatterMode.PROMISE_IN_BOUNDS,
    )


def add_remainders(table):
    half = table.shape[0] // 2
    for r in range(0, half, 8):
        value = table[r : r + 8, :]
        table[half + r : half + r + 8, :] = value - value.astype(bf16).astype(f32)


def donor_kernel(
    cell_ref,
    frac_ref,
    q_ref,
    out_ref,
    wrap_lo,
    wrap_hi,
    span_lo,
    span_hi,
    wall,
    planes,
    pieces,
    rank_ref,
    ordered,
    where_ref,
    first,
    partial,
    table,
    sem,
):
    spans, rows, lanes = q_ref.shape[1:]
    count, slots = cell_ref.shape
    tile = 256
    tiles = count * slots // tile
    wide = slots // 128
    one, zero = jnp.ones((), bf16), jnp.zeros((), bf16)
    pack(q_ref, wrap_lo, wrap_hi, span_lo, span_hi, wall)

    def prepare(k, _):
        for c in range(5):
            high, low = split_two(q_ref[c, k])
            here = pl.ds(pl.multiple_of(k * 5 * rows + c * rows, 16), rows)
            planes[here, 0:lanes] = high
            planes[here, lanes : 2 * lanes] = low
            planes[here, 2 * lanes : 3 * lanes] = high
        return 0

    lax.fori_loop(0, spans, prepare, 0)
    planes[spans * 5 * rows :, :] = jnp.zeros((5 * rows, 3 * lanes), bf16)

    cell = cell_ref[...]
    upper = jnp.floor((cell.astype(f32) + 0.5) * (1.0 / (lanes - 1)))
    span = jnp.floor((upper + 0.5) * (1.0 / (rows - 1)))
    pieces[0] = span
    pieces[1] = upper - span * (rows - 1)
    pieces[2] = cell.astype(f32) - upper * (lanes - 1)
    for d in range(3):
        f = frac_ref[d]
        high = f.astype(bf16).astype(f32)
        pieces[3 + 2 * d] = high
        pieces[4 + 2 * d] = f - high

    lines = jnp.concatenate([span[:, 128 * t : 128 * t + 128] for t in range(wide)], axis=0)
    depth = lines.shape[0]
    hits = [jnp.where(lines == b, 1.0, 0.0).astype(bf16) for b in range(spans)]
    into = lax.broadcasted_iota(i32, (128, 256), 0)
    onto = lax.broadcasted_iota(i32, (128, 256), 1)
    before = jnp.where((into < onto) | (onto >= 128), 1.0, 0.0).astype(bf16)
    inside = jnp.dot(jnp.concatenate(hits, axis=0), before, preferred_element_type=f32)
    sums = [inside[b * depth : (b + 1) * depth, 128:256] for b in range(spans)]
    lower = lax.broadcasted_iota(i32, (depth, depth), 1) < lax.broadcasted_iota(i32, (depth, depth), 0)
    above = jnp.dot(
        jnp.where(lower, 1.0, 0.0).astype(bf16),
        jnp.concatenate([x.astype(bf16) for x in sums], axis=1),
        preferred_element_type=f32,
    )
    start = jnp.zeros((1, 128), f32)
    rank = jnp.zeros((depth, 128), f32)
    for b in range(spans):
        over = above[:, b * 128 : (b + 1) * 128]
        rank = jnp.where(lines == b, inside[b * depth : (b + 1) * depth, 0:128] + over + start, rank)
        start = start + over[depth - 1 :] + sums[b][depth - 1 :]
    rank = rank.astype(i32)
    for t in range(wide):
        rank_ref[:, 128 * t : 128 * t + 128] = rank[8 * t : 8 * t + 8]

    tile_at = lax.broadcasted_iota(i32, (tiles, slots), 0).astype(f32).astype(bf16)
    place_at = lax.broadcasted_iota(i32, (tile, slots), 0).astype(f32).astype(bf16)
    ordered[...] = jnp.zeros_like(ordered)

    def order(w, _):
        to = rank_ref[pl.ds(w, 1), :]
        in_tile = jnp.where(tile_at == (to // tile).astype(f32).astype(bf16), one, zero)
        at_place = jnp.where(place_at == (to & (tile - 1)).astype(f32).astype(bf16), one, zero)
        parts = [in_tile * pieces[p, pl.ds(w, 1), :].astype(bf16) for p in range(9)]
        ordered[...] += lax.dot_general(
            jnp.concatenate(parts, axis=0),
            at_place,
            (((1,), (1,)), ((), ())),
            preferred_element_type=f32,
        )
        return 0

    lax.fori_loop(0, count, order, 0)
    where_ref[...] = ordered[0:tiles, :].astype(i32)
    copy = pltpu.make_async_copy(where_ref, first, sem)
    copy.start()
    copy.wait()

    def weights(cells, at, frac):
        here = lax.broadcasted_iota(i32, (cells, tile), 0)
        return jnp.where(here == at, 1.0 - frac, jnp.where(here == at + 1, frac, 0.0))

    def tile_of(i):
        def piece(p):
            return ordered[pl.ds(p * tiles + i, 1), :]

        span, wrap, normal = piece(0).astype(i32), piece(1).astype(i32), piece(2).astype(i32)
        f0, f1, f2 = [piece(3 + 2 * d) + piece(4 + 2 * d) for d in range(3)]
        high, low = split_two(weights(lanes, normal, f2))
        return span, f0, jnp.concatenate([high, high, low], axis=0), weights(rows, wrap, f1)

    def pair(k, made, sums):
        span, f0, along, across = made
        from_row = pl.ds(pl.multiple_of(k * 5 * rows, 16), 10 * rows)
        mixed = jnp.dot(planes[from_row, :], along, preferred_element_type=f32)
        new = list(sums)
        for n in range(2):
            ws = jnp.where(span == k + n, 1.0 - f0, jnp.where(span + 1 == k + n, f0, 0.0))
            for c in range(5):
                r0 = (5 * n + c) * rows
                total = mixed[r0 : r0 + 8] * across[0:8]
                for r in range(8, rows, 8):
                    total += mixed[r0 + r : r0 + r + 8] * across[r : r + 8]
                new[c] = ws * total if new[c] is None else new[c] + ws * total
        return tuple(new)

    def step(g, _):
        for n in range(GROUP):
            i = g * GROUP + n
            for c, x in enumerate(pair(first[i, 0], tile_of(i), (None,) * 5)):
                partial[n, c] = x
        for n in range(GROUP):
            i = g * GROUP + n
            lowest = first[i, 0]
            more = (first[i, tile - 1] + 1 - lowest) // 2

            @pl.when(more > 0)
            def _():
                made = tile_of(i)

                def again(m, _):
                    sums = pair(lowest + 2 + 2 * m, made, tuple(partial[n, c] for c in range(5)))
                    for c in range(5):
                        partial[n, c] = sums[c]
                    return 0

                lax.fori_loop(0, more, again, 0)

        for n in range(GROUP):
            i = g * GROUP + n
            for c in range(5):
                table[pl.ds(c * tiles + i, 1), :] = jnp.sum(partial[n, c], axis=0, keepdims=True)
        return 0

    lax.fori_loop(0, tiles // GROUP, step, 0)

    add_remainders(table)
    both = table[...].astype(bf16)

    def put_back(w, _):
        for t in range(0, slots, 512):
            for c, value in enumerate(lookup(both, rank_ref[pl.ds(w, 1), t : t + 512])):
                out_ref[w, c : c + 1, t : t + 512] = value
        return 0

    lax.fori_loop(0, count, put_back, 0, unroll=8)


def donors(cell, frac, state):
    _, spans, rows, lanes = state.shape
    count, slots = cell.shape
    tiles = count * slots // 256
    shapes = [(count, 5, slots)]
    shapes += [(5, 2, spans, lanes)] * 2 + [(5, 2, rows, lanes)] * 2 + [(5, rows, 2 * spans)]
    return pl.pallas_call(
        donor_kernel,
        grid=(1,),
        in_specs=[whole(cell.shape), whole(frac.shape), whole(state.shape)],
        out_specs=[whole(x) for x in shapes],
        out_shape=[jax.ShapeDtypeStruct(x, f32) for x in shapes],
        scratch_shapes=[
            pltpu.VMEM(((spans + 1) * 5 * rows, 3 * lanes), bf16),
            pltpu.VMEM((9, count, slots), f32),
            pltpu.VMEM((count, slots), i32),
            pltpu.VMEM((9 * tiles, 256), f32),
            pltpu.VMEM((tiles, 256), i32),
            pltpu.SMEM((tiles, 256), i32),
            pltpu.VMEM((GROUP, 5, 8, 256), f32),
            pltpu.VMEM((10 * tiles, 256), f32),
            pltpu.SemaphoreType.DMA(()),
        ],
        compiler_params=params(),
        name="donors",
    )(cell, frac, state)


def fill_kernel(
    from_ref, mask_ref, q_ref, slot_ref, out_ref, norm_lo, norm_hi, span_lo, span_hi, table, spread
):
    planes = pl.num_programs(0)
    rows, lanes = from_ref.shape[1:]
    count, _, slots = slot_ref.shape
    j = pl.program_id(0)

    @pl.when(j == 0)
    def _():
        per = slots // 256
        for c in range(4):
            for w in range(count):
                for r in range(per):
                    at = c * count * per + w * per + r
                    table[at : at + 1, :] = slot_ref[w, c : c + 1, r * 256 : (r + 1) * 256]
        add_remainders(table)
        for w in range(count):
            for r in range(slots // 128):
                value = slot_ref[w, 4:5, r * 128 : (r + 1) * 128]
                spread[w * (slots // 128) + r] = jnp.broadcast_to(value, (8, 128))

    both = table[...].astype(bf16)
    lines = spread.shape[0]
    share = (rows // 8) * (lanes // 128) * lines // rows
    value = None
    for s in range(rows):
        keep = mask_ref[0, s : s + 1, :] == 1
        for c, found in enumerate(lookup(both, from_ref[0, s : s + 1, :])):
            out_ref[c, 0, s : s + 1, :] = jnp.where(keep, q_ref[c, 0, s : s + 1, :], found)
        for n in range(s * share, (s + 1) * share):
            line = n % lines
            if line == 0:
                row, lane = divmod(n // lines, lanes // 128)
                here = (slice(8 * row, 8 * row + 8), slice(128 * lane, 128 * lane + 128))
                at = from_ref[0, here[0], here[1]]
                low, high = at & 127, at // 128
                value = jnp.zeros((8, 128), f32)
            value = jnp.where(high == line, take_lanes(spread[line], low), value)
            if line == lines - 1:
                keep = mask_ref[0, here[0], here[1]] == 1
                out_ref[4, 0, here[0], here[1]] = jnp.where(keep, q_ref[4, 0, here[0], here[1]], value)

    for c in range(5):
        for l in range(2):
            span_lo[c, l, pl.ds(j, 1), :] = out_ref[c, 0, l : l + 1, :]
            span_hi[c, l, pl.ds(j, 1), :] = out_ref[c, 0, rows - 2 + l : rows - 1 + l, :]

    @pl.when(j < 2)
    def _():
        for c in range(5):
            norm_lo[c, j] = out_ref[c, 0]

    @pl.when(j >= planes - 2)
    def _():
        for c in range(5):
            norm_hi[c, j - (planes - 2)] = out_ref[c, 0]


def fill(source, mask, state, slot):
    _, planes, rows, lanes = state.shape
    count, _, slots = slot.shape
    plane = pl.BlockSpec((1, rows, lanes), lambda j: (j, 0, 0))
    state_plane = pl.BlockSpec((5, 1, rows, lanes), lambda j: (0, j, 0, 0))
    edges = [(5, 2, rows, lanes)] * 2 + [(5, 2, planes, lanes)] * 2
    return pl.pallas_call(
        fill_kernel,
        grid=(planes,),
        in_specs=[plane, plane, state_plane, IN_VMEM],
        out_specs=[state_plane] + [whole(s) for s in edges],
        out_shape=[jax.ShapeDtypeStruct(s, f32) for s in [state.shape] + edges],
        scratch_shapes=[
            pltpu.VMEM((8 * count * slots // 256, 256), f32),
            pltpu.VMEM((count * slots // 128, 8, 128), f32),
        ],
        compiler_params=params(),
        cost_estimate=pl.CostEstimate(flops=24 * 10**9, bytes_accessed=6 * 10**6, transcendentals=0),
        name="fill",
    )(source, mask, state, slot)


def body(
    cgrid_state, cgrid_metric, flap_state, flap_metric, iblank, fringe_from, donor_cell, donor_frac
):
    wrap_count = lax.axis_size("wrap")

    def ring(axis):
        size = lax.axis_size(axis)
        return [(i, (i + 1) % size) for i in range(size)]

    def onward(value, axis):
        return lax.ppermute(value, axis, ring(axis))

    def back(value, axis):
        return lax.ppermute(value, axis, [(j, i) for i, j in ring(axis)])

    slot, wrap_lo, wrap_hi, span_lo, span_hi, wall = donors(
        donor_cell[0], jnp.transpose(donor_frac[0], (1, 0, 2)), cgrid_state
    )
    far = lax.ppermute(
        wall,
        "wrap",
        [(i, wrap_count - 1 - i if wrapped(i, wrap_count) else i) for i in range(wrap_count)],
    )
    majors = (onward(span_hi, "span"), back(span_lo, "span"))
    subs = (onward(wrap_hi, "wrap"), back(wrap_lo, "wrap"))

    slot = lax.all_to_all(slot, "wrap", split_axis=0, concat_axis=0, tiled=True)

    turned = lambda x: jnp.swapaxes(x, -3, -2)
    mask = turned(iblank)
    filled, norm_lo, norm_hi, edge_lo, edge_hi = fill(turned(fringe_from), mask, turned(flap_state), slot)
    flap_majors = (onward(norm_hi, "wrap"), back(norm_lo, "wrap"))
    flap_subs = (onward(edge_hi, "span"), back(edge_lo, "span"))

    cgrid_rate = rate(
        cgrid_state,
        majors,
        subs,
        (wrap_lo, wrap_hi, wall, far),
        cgrid_metric,
        None,
        cgrid=True,
        step_planes=4,
        components=(3, 1, 2),
        metric_rows=(0, 1, 2),
    )
    flap_rate = rate(
        filled,
        flap_majors,
        flap_subs,
        (),
        turned(flap_metric),
        mask,
        cgrid=False,
        step_planes=3,
        components=(2, 3, 1),
        metric_rows=(1, 0, 2),
    )
    return (cgrid_rate, turned(flap_rate))


def solution(mesh):
    return jax.shard_map(
        body,
        mesh=mesh,
        in_specs=(
            P(None, "span", "wrap", None),
            P(None, "span", "wrap", None),
            P(None, "span", "wrap", None),
            P(None, "span", "wrap", None),
            P("span", "wrap", None),
            P("span", "wrap", None),
            P(("wrap", "span"), None, None),
            P(("wrap", "span"), None, None, None),
        ),
        out_specs=(P(None, "span", "wrap", None), P(None, "span", "wrap", None)),
        check_vma=False,
    )
```

```python
import functools

import jax
import jax.numpy as jnp
from jax import lax
from jax.experimental import pallas as pl
from jax.experimental.pallas import tpu as pltpu
from jax.sharding import PartitionSpec as P

viscosity = 0.05
conduction = 0.07
damping = 1.0 / 32.0
VMEM_LIMIT = 40 * 1024 * 1024
IN_HBM = pl.BlockSpec(memory_space=pltpu.HBM)
IN_VMEM = pl.BlockSpec(memory_space=pltpu.VMEM)
GROUP = 8

f32, bf16, i32 = jnp.float32, jnp.bfloat16, jnp.int32


def whole(shape):
    return pl.BlockSpec(shape, lambda *_: (0,) * len(shape))


def params():
    return pltpu.CompilerParams(vmem_limit_bytes=VMEM_LIMIT)


def primitives(q):
    inverse = 1.0 / q[0]
    v = [q[m] * inverse for m in (1, 2, 3)]
    kinetic = 0.5 * (v[0] * v[0] + v[1] * v[1] + v[2] * v[2])
    pressure = 0.4 * (q[4] - q[0] * kinetic)
    return v + [pressure, kinetic + (conduction / viscosity) * (pressure * inverse)]


def wrapped(place, count):
    return (place < count // 4) | (place >= count - count // 4)


def flux(q, prims, m):
    u = (0.5 / damping) * prims[m - 1]
    f = [q[0] * u]
    for c in (1, 2, 3):
        f.append(q[c] * u + (0.5 / damping) * prims[3] if c == m else q[c] * u)
    f.append((q[4] + prims[3]) * u)
    return f


def pack(q_ref, wrap_lo, wrap_hi, span_lo, span_hi, wall):
    spans, rows = q_ref.shape[1], q_ref.shape[2]
    lane = lax.broadcasted_iota(i32, (rows, 128), 1)
    for c in range(5):
        for l in range(2):
            span_lo[c, l] = q_ref[c, l]
            span_hi[c, l] = q_ref[c, spans - 2 + l]
        cells = jnp.zeros((rows, 128), f32)
        for k in range(spans):
            for l in range(2):
                wrap_lo[c, l, k : k + 1, :] = q_ref[c, k, l : l + 1, :]
                wrap_hi[c, l, k : k + 1, :] = q_ref[c, k, rows - 2 + l : rows - 1 + l, :]
            near = q_ref[c, k, :, 0:128]
            if k:
                near = pltpu.roll(near, 2 * k, 1)
            cells = jnp.where(lane // 2 == k, near, cells)
        wall[c] = cells[:, 0 : 2 * spans]


def rate_kernel(
    q_hbm,
    major_lo,
    major_hi,
    sub_lo,
    sub_hi,
    *refs,
    cgrid,
    step_planes,
    components,
    metric_rows,
):
    if cgrid:
        own_lo, own_hi, wall_own, wall_far, metric_ref, out_ref, qe, prim, sub_edge, lane_edge, sems = refs
    else:
        own_lo = own_hi = None
        mask_ref, metric_ref, out_ref, qe, prim, sub_edge, sems = refs
    planes, rows, lanes = qe.shape[1] - 4, qe.shape[2], qe.shape[3]
    step = pl.program_id(0)
    place, count = lax.axis_index("wrap"), lax.axis_size("wrap")
    at_start = place == 0
    at_end = place == count - 1
    major_m, sub_m, lane_m = components

    def edge_fields(q1, q2, m, side):
        prims = primitives(q1)
        fl = flux(q1, prims, m)
        lead = [4.0 * q1[c] - side * fl[c] - q2[c] for c in range(5)]
        return lead + q1 + prims[:3] + prims[4:]

    def store_prims(k, slot):
        q = [qe[c, k] for c in range(5)]
        prims = primitives(q)
        for i, x in enumerate(prims + flux(q, prims, major_m)):
            prim[slot, i] = x

    steps = planes // step_planes

    def part(n):
        n = n * step_planes
        return pltpu.make_async_copy(
            q_hbm.at[:, pl.ds(n, step_planes)], qe.at[:, pl.ds(n + 2, step_planes)], sems.at[n // step_planes]
        )

    @pl.when(step == 0)
    def _():
        copies = [
            pltpu.make_async_copy(major_lo, qe.at[:, pl.ds(0, 2)], sems.at[steps]),
            pltpu.make_async_copy(major_hi, qe.at[:, pl.ds(planes + 2, 2)], sems.at[steps + 1]),
        ]
        copies[0].start()
        for n in range(steps):
            part(n).start()
        copies[1].start()
        for side, ref, own in ((-1, sub_lo, own_lo), (1, sub_hi, own_hi)):
            near, far = (1, 0) if side < 0 else (0, 1)
            q1 = [ref[c, near] for c in range(5)]
            q2 = [ref[c, far] for c in range(5)]
            if cgrid:
                edge = at_start if side < 0 else at_end
                clamp = 0 if side < 0 else 1
                q1 = [jnp.where(edge, own[c, clamp], q1[c]) for c in range(5)]
                q2 = [jnp.where(edge, own[c, clamp], q2[c]) for c in range(5)]
            for i, x in enumerate(edge_fields(q1, q2, sub_m, side)):
                sub_edge[(side + 1) // 2, i] = x
        if cgrid:
            in_wake = wrapped(place, count)
            turn = 7 - lax.broadcasted_iota(i32, (8, 128), 0)
            ghosts = []
            for c in range(5):
                sign = -1.0 if c in (1, 2, 3) else 1.0
                parts = []
                for r in range(rows // 8):
                    far = wall_far[c, rows - 8 - 8 * r : rows - 8 * r, :]
                    own = wall_own[c, 8 * r : 8 * r + 8, :]
                    own = jnp.concatenate([own, jnp.zeros((8, 128 - own.shape[1]), f32)], axis=1)
                    far = jnp.concatenate([far, jnp.zeros((8, 128 - far.shape[1]), f32)], axis=1)
                    far = jnp.take_along_axis(far, turn, axis=0, mode="promise_in_bounds")
                    parts.append(jnp.where(in_wake, far, sign * own))
                ghosts.append(jnp.concatenate(parts, axis=0))
            second = [pltpu.roll(x, 127, 1) for x in ghosts]
            for i, x in enumerate(edge_fields(ghosts, second, lane_m, -1)):
                lane_edge[i] = x
        copies[0].wait()
        part(0).wait()
        part(1).wait()
        copies[1].wait()
        if not cgrid:

            @pl.when(at_start)
            def _():
                for c in range(5):
                    sign = -1.0 if c in (1, 2, 3) else 1.0
                    qe[c, 1] = sign * qe[c, 2]
                    qe[c, 0] = sign * qe[c, 3]

        store_prims(1, 0)
        store_prims(2, 1)

    @pl.when((step > 0) & (step < steps - 1))
    def _():
        part(step + 1).wait()

    if not cgrid:

        @pl.when((step == steps - 1) & at_end)
        def _():
            for c in range(5):
                qe[c, planes + 2] = qe[c, planes + 1]
                qe[c, planes + 3] = qe[c, planes + 1]

    row_at = lax.broadcasted_iota(i32, (8, lanes), 0)
    lane_at = lax.broadcasted_iota(i32, (rows, 128), 1)
    row_first, row_last = row_at == 0, row_at == 7
    lane_first, lane_last = lane_at == 0, lane_at == 127

    def one(b, _):
        k = step * step_planes + b
        here, below, above = lax.rem(k + 1, 3), lax.rem(k, 3), lax.rem(k + 2, 3)
        store_prims(k + 3, above)

        def sub_next(x, i):
            moved = [pltpu.roll(x[r : r + 8], 7, 0) for r in range(0, rows, 8)]
            moved.append(sub_edge[1, i, pl.ds(k, 1), :])
            return jnp.concatenate(
                [jnp.where(row_last, moved[r + 1], moved[r]) for r in range(rows // 8)], axis=0
            )

        def sub_prior(x, i):
            moved = [sub_edge[0, i, pl.ds(k, 1), :]]
            moved += [pltpu.roll(x[r : r + 8], 1, 0) for r in range(0, rows, 8)]
            return jnp.concatenate(
                [jnp.where(row_first, moved[r], moved[r + 1]) for r in range(rows // 8)], axis=0
            )

        def lane_next(x):
            moved = [pltpu.roll(x[:, t : t + 128], 127, 1) for t in range(0, lanes, 128)]
            moved.append(x[:, lanes - 128 :] if cgrid else moved[0])
            return jnp.concatenate(
                [jnp.where(lane_last, moved[t + 1], moved[t]) for t in range(lanes // 128)], axis=1
            )

        def lane_prior(x, i):
            moved = [pltpu.roll(x[:, t : t + 128], 1, 1) for t in range(0, lanes, 128)]
            if cgrid:
                moved.insert(0, pltpu.roll(lane_edge[i], lax.rem(128 - 2 * k, 128), 1))
            else:
                moved.insert(0, moved[-1])
            return jnp.concatenate(
                [jnp.where(lane_first, moved[t], moved[t + 1]) for t in range(lanes // 128)], axis=1
            )

        gm = metric_ref[metric_rows[0], b]
        gs = metric_ref[metric_rows[1], b]
        gl = metric_ref[metric_rows[2], b]
        gm2, gs2, gl2 = viscosity * gm * gm, viscosity * gs * gs, viscosity * gl * gl
        gm, gs, gl = damping * gm, damping * gs, damping * gl
        all2 = 2.0 * (gm2 + gs2 + gl2)
        all6 = 6.0 * (gm + gs + gl)
        mine = [prim[here, i] for i in range(5)]
        viscous = {}
        for i, c, e in ((0, 1, 10), (1, 2, 11), (2, 3, 12), (4, 4, 13)):
            x = mine[i]
            total = gm2 * (prim[above, i] + prim[below, i])
            total += gs2 * (sub_next(x, e) + sub_prior(x, e))
            total += gl2 * (lane_next(x) + lane_prior(x, e))
            viscous[c] = total - all2 * x
        q = [qe[c, k + 2] for c in range(5)]
        sub_flux = flux(q, mine, sub_m)
        lane_flux = flux(q, mine, lane_m)
        for c in range(5):
            x = q[c]
            four = 4.0 * x
            total = gm * (
                4.0 * (qe[c, k + 3] + qe[c, k + 1])
                - (qe[c, k + 4] + qe[c, k])
                - (prim[above, 5 + c] - prim[below, 5 + c])
            )
            up = four - sub_flux[c] - sub_next(x, 5 + c)
            down = four + sub_flux[c] - sub_prior(x, 5 + c)
            total += gs * (sub_next(up, c) + sub_prior(down, c))
            up = four - lane_flux[c] - lane_next(x)
            down = four + lane_flux[c] - lane_prior(x, 5 + c)
            total += gl * (lane_next(up) + lane_prior(down, c))
            total -= all6 * x
            if c:
                total += viscous[c]
            if not cgrid:
                total = jnp.where(mask_ref[b] == 1, total, 0.0)
            out_ref[c, b] = total
        return 0

    lax.fori_loop(0, step_planes, one, 0)


def rate(q, majors, subs, extras, metric, mask, *, cgrid, step_planes, components, metric_rows):
    _, planes, rows, lanes = q.shape
    anywhere = pl.BlockSpec(memory_space=pl.ANY)
    block = lambda n: pl.BlockSpec((n, step_planes, rows, lanes), lambda i: (0, i, 0, 0))
    last_specs = [block(3)]
    last = (metric,)
    if mask is not None:
        last_specs = [pl.BlockSpec((step_planes, rows, lanes), lambda i: (i, 0, 0))] + last_specs
        last = (mask, metric)
    return pl.pallas_call(
        functools.partial(
            rate_kernel,
            cgrid=cgrid,
            step_planes=step_planes,
            components=components,
            metric_rows=metric_rows,
        ),
        grid=(planes // step_planes,),
        in_specs=[anywhere] + [IN_VMEM] * (4 + len(extras)) + last_specs,
        out_specs=block(5),
        out_shape=jax.ShapeDtypeStruct(q.shape, f32),
        scratch_shapes=[
            pltpu.VMEM((5, planes + 4, rows, lanes), f32),
            pltpu.VMEM((3, 10, rows, lanes), f32),
            pltpu.VMEM((2, 14, planes, lanes), f32),
        ]
        + [pltpu.VMEM((14, rows, 128), f32)] * cgrid
        + [pltpu.SemaphoreType.DMA((planes // step_planes + 2,))],
        compiler_params=params(),
        cost_estimate=pl.CostEstimate(
            flops=300 * planes * rows * lanes, bytes_accessed=60 * planes * rows * lanes, transcendentals=0
        ),
        name="cgrid_rate" if cgrid else "flap_rate",
    )(q, *majors, *subs, *extras, *last)


def split_two(x):
    high = x.astype(bf16)
    return high, (x - high.astype(f32)).astype(bf16)


def lookup(both, at):
    width = at.shape[1]
    highs = 32
    components = both.shape[0] // (2 * highs)
    cells = lax.broadcasted_iota(i32, (256, width), 0).astype(f32).astype(bf16)
    sub = lax.broadcasted_iota(i32, (8, width), 0)
    pick = jnp.where(
        cells == (at & 255).astype(f32).astype(bf16), jnp.ones((), bf16), jnp.zeros((), bf16)
    )
    high = at // 256
    found = jnp.dot(both, pick, preferred_element_type=f32)
    masks = [sub + 8 * g == high for g in range(highs // 8)]
    values = []
    for c in range(components):
        value = None
        for g, mask in enumerate(masks):
            r = c * highs + 8 * g
            remainder = components * highs + r
            piece = found[r : r + 8] + found[remainder : remainder + 8]
            value = jnp.where(mask, piece, 0.0 if value is None else value)
        values.append(jnp.sum(value, axis=0, keepdims=True))
    return values


def take_lanes(values, lanes):
    return lax.gather(
        values,
        lanes[..., None],
        lax.GatherDimensionNumbers(
            offset_dims=(),
            collapsed_slice_dims=(1,),
            start_index_map=(1,),
            operand_batching_dims=(0,),
            start_indices_batching_dims=(0,),
        ),
        slice_sizes=(1, 1),
        mode=lax.GatherScatterMode.PROMISE_IN_BOUNDS,
    )


def add_remainders(table):
    half = table.shape[0] // 2
    for r in range(0, half, 8):
        value = table[r : r + 8, :]
        table[half + r : half + r + 8, :] = value - value.astype(bf16).astype(f32)


def donor_kernel(
    cell_ref,
    frac_ref,
    q_hbm,
    out_ref,
    wrap_lo,
    wrap_hi,
    span_lo,
    span_hi,
    wall,
    q_ref,
    planes,
    pieces,
    rank_ref,
    ordered,
    where_ref,
    first,
    partial,
    table,
    sems,
):
    spans, rows, lanes = q_ref.shape[1:]
    count, slots = cell_ref.shape
    tile = 256
    tiles = count * slots // tile
    wide = slots // 128
    one, zero = jnp.ones((), bf16), jnp.zeros((), bf16)
    fetch = pltpu.make_async_copy(q_hbm, q_ref, sems.at[0])
    fetch.start()

    cell = cell_ref[...]
    upper = jnp.floor((cell.astype(f32) + 0.5) * (1.0 / (lanes - 1)))
    span = jnp.floor((upper + 0.5) * (1.0 / (rows - 1)))
    pieces[0] = span
    pieces[1] = upper - span * (rows - 1)
    pieces[2] = cell.astype(f32) - upper * (lanes - 1)
    for d in range(3):
        f = frac_ref[d]
        high = f.astype(bf16).astype(f32)
        pieces[3 + 2 * d] = high
        pieces[4 + 2 * d] = f - high

    lines = jnp.concatenate([span[:, 128 * t : 128 * t + 128] for t in range(wide)], axis=0)
    depth = lines.shape[0]
    hits = [jnp.where(lines == b, 1.0, 0.0).astype(bf16) for b in range(spans)]
    into = lax.broadcasted_iota(i32, (128, 256), 0)
    onto = lax.broadcasted_iota(i32, (128, 256), 1)
    before = jnp.where((into < onto) | (onto >= 128), 1.0, 0.0).astype(bf16)
    inside = jnp.dot(jnp.concatenate(hits, axis=0), before, preferred_element_type=f32)
    sums = [inside[b * depth : (b + 1) * depth, 128:256] for b in range(spans)]
    lower = lax.broadcasted_iota(i32, (depth, depth), 1) < lax.broadcasted_iota(i32, (depth, depth), 0)
    above = jnp.dot(
        jnp.where(lower, 1.0, 0.0).astype(bf16),
        jnp.concatenate([x.astype(bf16) for x in sums], axis=1),
        preferred_element_type=f32,
    )
    start = jnp.zeros((1, 128), f32)
    rank = jnp.zeros((depth, 128), f32)
    for b in range(spans):
        over = above[:, b * 128 : (b + 1) * 128]
        rank = jnp.where(lines == b, inside[b * depth : (b + 1) * depth, 0:128] + over + start, rank)
        start = start + over[depth - 1 :] + sums[b][depth - 1 :]
    rank = rank.astype(i32)
    for t in range(wide):
        rank_ref[:, 128 * t : 128 * t + 128] = rank[8 * t : 8 * t + 8]

    tile_at = lax.broadcasted_iota(i32, (tiles, slots), 0).astype(f32).astype(bf16)
    place_at = lax.broadcasted_iota(i32, (tile, slots), 0).astype(f32).astype(bf16)
    ordered[...] = jnp.zeros_like(ordered)

    def order(w, _):
        to = rank_ref[pl.ds(w, 1), :]
        in_tile = jnp.where(tile_at == (to // tile).astype(f32).astype(bf16), one, zero)
        at_place = jnp.where(place_at == (to & (tile - 1)).astype(f32).astype(bf16), one, zero)
        parts = [in_tile * pieces[p, pl.ds(w, 1), :].astype(bf16) for p in range(9)]
        ordered[...] += lax.dot_general(
            jnp.concatenate(parts, axis=0),
            at_place,
            (((1,), (1,)), ((), ())),
            preferred_element_type=f32,
        )
        return 0

    lax.fori_loop(0, count, order, 0, unroll=4)
    where_ref[...] = ordered[0:tiles, :].astype(i32)
    copy = pltpu.make_async_copy(where_ref, first, sems.at[1])
    copy.start()

    fetch.wait()
    pack(q_ref, wrap_lo, wrap_hi, span_lo, span_hi, wall)

    def prepare(k, _):
        for c in range(5):
            high, low = split_two(q_ref[c, k])
            here = pl.ds(pl.multiple_of(k * 5 * rows + c * rows, 16), rows)
            planes[here, 0:lanes] = high
            planes[here, lanes : 2 * lanes] = low
            planes[here, 2 * lanes : 3 * lanes] = high
        return 0

    lax.fori_loop(0, spans, prepare, 0)
    copy.wait()

    def weights(cells, at, frac):
        here = lax.broadcasted_iota(i32, (cells, tile), 0)
        return jnp.where(here == at, 1.0 - frac, jnp.where(here == at + 1, frac, 0.0))

    def tile_of(i):
        def piece(p):
            return ordered[pl.ds(p * tiles + i, 1), :]

        span, wrap, normal = piece(0).astype(i32), piece(1).astype(i32), piece(2).astype(i32)
        f0, f1, f2 = [piece(3 + 2 * d) + piece(4 + 2 * d) for d in range(3)]
        cells = lax.broadcasted_iota(i32, (lanes, tile), 0).astype(f32).astype(bf16)
        at_lower, at_upper = [cells == (normal + n).astype(f32).astype(bf16) for n in range(2)]
        (lower_high, lower_low), (upper_high, upper_low) = split_two(1.0 - f2), split_two(f2)
        high = jnp.where(at_lower, lower_high, jnp.where(at_upper, upper_high, zero))
        low = jnp.where(at_lower, lower_low, jnp.where(at_upper, upper_low, zero))
        return span, f0, jnp.concatenate([high, high, low], axis=0), weights(rows, wrap, f1)

    def add_planes(k, number, made, sums):
        span, f0, along, across = made
        from_row = pl.ds(pl.multiple_of(k * 5 * rows, 16), number * 5 * rows)
        mixed = jnp.dot(planes[from_row, :], along, preferred_element_type=f32)
        new = list(sums)
        for n in range(number):
            ws = jnp.where(span == k + n, 1.0 - f0, jnp.where(span + 1 == k + n, f0, 0.0))
            for c in range(5):
                r0 = (5 * n + c) * rows
                total = mixed[r0 : r0 + 8] * across[0:8]
                for r in range(8, rows, 8):
                    total += mixed[r0 + r : r0 + r + 8] * across[r : r + 8]
                new[c] = ws * total if new[c] is None else new[c] + ws * total
        return tuple(new)

    def step(g, _):
        for n in range(GROUP):
            i = g * GROUP + n
            for c, x in enumerate(add_planes(first[i, 0], 2, tile_of(i), (None,) * 5)):
                partial[n, c] = x
        for n in range(GROUP):
            i = g * GROUP + n
            lowest = first[i, 0]
            more = first[i, tile - 1] - lowest

            @pl.when(more > 0)
            def _():
                made = tile_of(i)

                def again(m, _):
                    sums = add_planes(lowest + 2 + m, 1, made, tuple(partial[n, c] for c in range(5)))
                    for c in range(5):
                        partial[n, c] = sums[c]
                    return 0

                lax.fori_loop(0, more, again, 0)

        for n in range(GROUP):
            i = g * GROUP + n
            for c in range(5):
                table[pl.ds(c * tiles + i, 1), :] = jnp.sum(partial[n, c], axis=0, keepdims=True)
        return 0

    lax.fori_loop(0, tiles // GROUP, step, 0)

    add_remainders(table)
    both = table[...].astype(bf16)

    def put_back(w, _):
        for t in range(0, slots, 512):
            for c, value in enumerate(lookup(both, rank_ref[pl.ds(w, 1), t : t + 512])):
                out_ref[w, c : c + 1, t : t + 512] = value
        return 0

    lax.fori_loop(0, count, put_back, 0, unroll=8)


def donors(cell, frac, state):
    _, spans, rows, lanes = state.shape
    count, slots = cell.shape
    tiles = count * slots // 256
    shapes = [(count, 5, slots)]
    shapes += [(5, 2, spans, lanes)] * 2 + [(5, 2, rows, lanes)] * 2 + [(5, rows, 2 * spans)]
    return pl.pallas_call(
        donor_kernel,
        grid=(1,),
        in_specs=[IN_VMEM, IN_VMEM, IN_HBM],
        out_specs=[whole(x) for x in shapes],
        out_shape=[jax.ShapeDtypeStruct(x, f32) for x in shapes],
        scratch_shapes=[
            pltpu.VMEM(state.shape, f32),
            pltpu.VMEM((spans * 5 * rows, 3 * lanes), bf16),
            pltpu.VMEM((9, count, slots), f32),
            pltpu.VMEM((count, slots), i32),
            pltpu.VMEM((9 * tiles, 256), f32),
            pltpu.VMEM((tiles, 256), i32),
            pltpu.SMEM((tiles, 256), i32),
            pltpu.VMEM((GROUP, 5, 8, 256), f32),
            pltpu.VMEM((10 * tiles, 256), f32),
            pltpu.SemaphoreType.DMA((2,)),
        ],
        compiler_params=params(),
        name="donors",
    )(cell, frac, state)


def fill_kernel(
    from_ref,
    mask_ref,
    q_hbm,
    slot_ref,
    out_ref,
    norm_lo,
    norm_hi,
    span_lo,
    span_hi,
    table,
    spread,
    q_ref,
    sems,
):
    planes = pl.num_programs(0)
    rows, lanes = from_ref.shape[1:]
    count, _, slots = slot_ref.shape
    j = pl.program_id(0)

    def fetch(n):
        return pltpu.make_async_copy(q_hbm.at[:, n], q_ref.at[:, n], sems.at[n])

    @pl.when(j == 0)
    def _():
        for n in range(q_ref.shape[1]):
            fetch(n).start()
        per = slots // 256
        for c in range(4):
            for w in range(count):
                for r in range(per):
                    at = c * count * per + w * per + r
                    table[at : at + 1, :] = slot_ref[w, c : c + 1, r * 256 : (r + 1) * 256]
        add_remainders(table)
        for w in range(count):
            for r in range(slots // 128):
                value = slot_ref[w, 4:5, r * 128 : (r + 1) * 128]
                spread[w * (slots // 128) + r] = jnp.broadcast_to(value, (8, 128))

    fetch(j).wait()
    both = table[...].astype(bf16)
    lines = spread.shape[0]
    share = (rows // 8) * (lanes // 128) * lines // rows
    value = None
    for s in range(rows):
        keep = mask_ref[0, s : s + 1, :] == 1
        for c, found in enumerate(lookup(both, from_ref[0, s : s + 1, :])):
            out_ref[c, 0, s : s + 1, :] = jnp.where(keep, q_ref[c, j, s : s + 1, :], found)
        for n in range(s * share, (s + 1) * share):
            line = n % lines
            if line == 0:
                row, lane = divmod(n // lines, lanes // 128)
                here = (slice(8 * row, 8 * row + 8), slice(128 * lane, 128 * lane + 128))
                at = from_ref[0, here[0], here[1]]
                low, high = at & 127, at // 128
                value = jnp.zeros((8, 128), f32)
            value = jnp.where(high == line, take_lanes(spread[line], low), value)
            if line == lines - 1:
                keep = mask_ref[0, here[0], here[1]] == 1
                out_ref[4, 0, here[0], here[1]] = jnp.where(keep, q_ref[4, j, here[0], here[1]], value)

    for c in range(5):
        for l in range(2):
            span_lo[c, l, pl.ds(j, 1), :] = out_ref[c, 0, l : l + 1, :]
            span_hi[c, l, pl.ds(j, 1), :] = out_ref[c, 0, rows - 2 + l : rows - 1 + l, :]

    @pl.when(j < 2)
    def _():
        for c in range(5):
            norm_lo[c, j] = out_ref[c, 0]

    @pl.when(j >= planes - 2)
    def _():
        for c in range(5):
            norm_hi[c, j - (planes - 2)] = out_ref[c, 0]


def fill(source, mask, state, slot):
    _, planes, rows, lanes = state.shape
    count, _, slots = slot.shape
    plane = pl.BlockSpec((1, rows, lanes), lambda j: (j, 0, 0))
    state_plane = pl.BlockSpec((5, 1, rows, lanes), lambda j: (0, j, 0, 0))
    edges = [(5, 2, rows, lanes)] * 2 + [(5, 2, planes, lanes)] * 2
    return pl.pallas_call(
        fill_kernel,
        grid=(planes,),
        in_specs=[plane, plane, IN_HBM, IN_VMEM],
        out_specs=[state_plane] + [whole(s) for s in edges],
        out_shape=[jax.ShapeDtypeStruct(s, f32) for s in [state.shape] + edges],
        scratch_shapes=[
            pltpu.VMEM((8 * count * slots // 256, 256), f32),
            pltpu.VMEM((count * slots // 128, 8, 128), f32),
            pltpu.VMEM(state.shape, f32),
            pltpu.SemaphoreType.DMA((planes,)),
        ],
        compiler_params=params(),
        cost_estimate=pl.CostEstimate(flops=24 * 10**9, bytes_accessed=6 * 10**6, transcendentals=0),
        name="fill",
    )(source, mask, state, slot)


def body(
    cgrid_state, cgrid_metric, flap_state, flap_metric, iblank, fringe_from, donor_cell, donor_frac
):
    wrap_count = lax.axis_size("wrap")

    def ring(axis):
        size = lax.axis_size(axis)
        return [(i, (i + 1) % size) for i in range(size)]

    def onward(value, axis):
        return lax.ppermute(value, axis, ring(axis))

    def back(value, axis):
        return lax.ppermute(value, axis, [(j, i) for i, j in ring(axis)])

    slot, wrap_lo, wrap_hi, span_lo, span_hi, wall = donors(
        donor_cell[0], jnp.transpose(donor_frac[0], (1, 0, 2)), cgrid_state
    )
    far = lax.ppermute(
        wall,
        "wrap",
        [(i, wrap_count - 1 - i if wrapped(i, wrap_count) else i) for i in range(wrap_count)],
    )
    majors = (onward(span_hi, "span"), back(span_lo, "span"))
    subs = (onward(wrap_hi, "wrap"), back(wrap_lo, "wrap"))

    slot = lax.all_to_all(slot, "wrap", split_axis=0, concat_axis=0, tiled=True)

    turned = lambda x: jnp.swapaxes(x, -3, -2)
    mask = turned(iblank)
    filled, norm_lo, norm_hi, edge_lo, edge_hi = fill(turned(fringe_from), mask, turned(flap_state), slot)
    flap_majors = (onward(norm_hi, "wrap"), back(norm_lo, "wrap"))
    flap_subs = (onward(edge_hi, "span"), back(edge_lo, "span"))

    cgrid_rate = rate(
        cgrid_state,
        majors,
        subs,
        (wrap_lo, wrap_hi, wall, far),
        cgrid_metric,
        None,
        cgrid=True,
        step_planes=4,
        components=(3, 1, 2),
        metric_rows=(0, 1, 2),
    )
    flap_rate = rate(
        filled,
        flap_majors,
        flap_subs,
        (),
        turned(flap_metric),
        mask,
        cgrid=False,
        step_planes=3,
        components=(2, 3, 1),
        metric_rows=(1, 0, 2),
    )
    return (cgrid_rate, turned(flap_rate))


def solution(mesh):
    return jax.shard_map(
        body,
        mesh=mesh,
        in_specs=(
            P(None, "span", "wrap", None),
            P(None, "span", "wrap", None),
            P(None, "span", "wrap", None),
            P(None, "span", "wrap", None),
            P("span", "wrap", None),
            P("span", "wrap", None),
            P(("wrap", "span"), None, None),
            P(("wrap", "span"), None, None, None),
        ),
        out_specs=(P(None, "span", "wrap", None), P(None, "span", "wrap", None)),
        check_vma=False,
    )
```

```python
import functools

import jax
import jax.numpy as jnp
from jax import lax
from jax.experimental import pallas as pl
from jax.experimental.pallas import tpu as pltpu
from jax.sharding import PartitionSpec as P

viscosity = 0.05
conduction = 0.07
damping = 1.0 / 32.0
VMEM_LIMIT = 40 * 1024 * 1024
IN_HBM = pl.BlockSpec(memory_space=pltpu.HBM)
IN_VMEM = pl.BlockSpec(memory_space=pltpu.VMEM)
GROUP = 8

f32, bf16, i32 = jnp.float32, jnp.bfloat16, jnp.int32


def whole(shape):
    return pl.BlockSpec(shape, lambda *_: (0,) * len(shape))


def params(limit=VMEM_LIMIT):
    return pltpu.CompilerParams(vmem_limit_bytes=limit)


def primitives(q):
    inverse = 1.0 / q[0]
    v = [q[m] * inverse for m in (1, 2, 3)]
    kinetic = 0.5 * (v[0] * v[0] + v[1] * v[1] + v[2] * v[2])
    pressure = 0.4 * (q[4] - q[0] * kinetic)
    return v + [pressure, kinetic + (conduction / viscosity) * (pressure * inverse)]


def wrapped(place, count):
    return (place < count // 4) | (place >= count - count // 4)


def flux(q, prims, m):
    u = (0.5 / damping) * prims[m - 1]
    f = [q[0] * u]
    for c in (1, 2, 3):
        f.append(q[c] * u + (0.5 / damping) * prims[3] if c == m else q[c] * u)
    f.append((q[4] + prims[3]) * u)
    return f


def pack(q_ref, wrap_lo, wrap_hi, span_lo, span_hi, wall):
    spans, rows = q_ref.shape[1], q_ref.shape[2]
    lane = lax.broadcasted_iota(i32, (rows, 128), 1)
    for c in range(5):
        for l in range(2):
            span_lo[c, l] = q_ref[c, l]
            span_hi[c, l] = q_ref[c, spans - 2 + l]
        cells = jnp.zeros((rows, 128), f32)
        for k in range(spans):
            for l in range(2):
                wrap_lo[c, l, k : k + 1, :] = q_ref[c, k, l : l + 1, :]
                wrap_hi[c, l, k : k + 1, :] = q_ref[c, k, rows - 2 + l : rows - 1 + l, :]
            near = q_ref[c, k, :, 0:128]
            if k:
                near = pltpu.roll(near, 2 * k, 1)
            cells = jnp.where(lane // 2 == k, near, cells)
        wall[c] = cells[:, 0 : 2 * spans]


def rate_kernel(
    q_hbm,
    major_lo,
    major_hi,
    sub_lo,
    sub_hi,
    *refs,
    cgrid,
    step_planes,
    components,
    metric_rows,
):
    if cgrid:
        own_lo, own_hi, wall_own, wall_far, metric_ref, out_ref, qe, prim, sub_edge, lane_edge, sems = refs
    else:
        own_lo = own_hi = None
        mask_ref, metric_ref, out_ref, qe, prim, sub_edge, sems = refs
    planes, rows, lanes = qe.shape[1] - 4, qe.shape[2], qe.shape[3]
    step = pl.program_id(0)
    place, count = lax.axis_index("wrap"), lax.axis_size("wrap")
    at_start = place == 0
    at_end = place == count - 1
    major_m, sub_m, lane_m = components

    def edge_fields(q1, q2, m, side):
        prims = primitives(q1)
        fl = flux(q1, prims, m)
        lead = [4.0 * q1[c] - side * fl[c] - q2[c] for c in range(5)]
        return lead + q1 + prims[:3] + prims[4:]

    def store_prims(k, slot):
        q = [qe[c, k] for c in range(5)]
        prims = primitives(q)
        for i, x in enumerate(prims + flux(q, prims, major_m)):
            prim[slot, i] = x

    steps = planes // step_planes

    def part(n):
        n = n * step_planes
        return pltpu.make_async_copy(
            q_hbm.at[:, pl.ds(n, step_planes)], qe.at[:, pl.ds(n + 2, step_planes)], sems.at[n // step_planes]
        )

    @pl.when(step == 0)
    def _():
        copies = [
            pltpu.make_async_copy(major_lo, qe.at[:, pl.ds(0, 2)], sems.at[steps]),
            pltpu.make_async_copy(major_hi, qe.at[:, pl.ds(planes + 2, 2)], sems.at[steps + 1]),
        ]
        copies[0].start()
        for n in range(steps):
            part(n).start()
        copies[1].start()
        for side, ref, own in ((-1, sub_lo, own_lo), (1, sub_hi, own_hi)):
            near, far = (1, 0) if side < 0 else (0, 1)
            q1 = [ref[c, near] for c in range(5)]
            q2 = [ref[c, far] for c in range(5)]
            if cgrid:
                edge = at_start if side < 0 else at_end
                clamp = 0 if side < 0 else 1
                q1 = [jnp.where(edge, own[c, clamp], q1[c]) for c in range(5)]
                q2 = [jnp.where(edge, own[c, clamp], q2[c]) for c in range(5)]
            for i, x in enumerate(edge_fields(q1, q2, sub_m, side)):
                sub_edge[(side + 1) // 2, i] = x
        if cgrid:
            in_wake = wrapped(place, count)
            turn = 7 - lax.broadcasted_iota(i32, (8, 128), 0)
            ghosts = []
            for c in range(5):
                sign = -1.0 if c in (1, 2, 3) else 1.0
                parts = []
                for r in range(rows // 8):
                    far = wall_far[c, rows - 8 - 8 * r : rows - 8 * r, :]
                    own = wall_own[c, 8 * r : 8 * r + 8, :]
                    own = jnp.concatenate([own, jnp.zeros((8, 128 - own.shape[1]), f32)], axis=1)
                    far = jnp.concatenate([far, jnp.zeros((8, 128 - far.shape[1]), f32)], axis=1)
                    far = jnp.take_along_axis(far, turn, axis=0, mode="promise_in_bounds")
                    parts.append(jnp.where(in_wake, far, sign * own))
                ghosts.append(jnp.concatenate(parts, axis=0))
            second = [pltpu.roll(x, 127, 1) for x in ghosts]
            for i, x in enumerate(edge_fields(ghosts, second, lane_m, -1)):
                lane_edge[i] = x
        copies[0].wait()
        part(0).wait()
        part(1).wait()
        copies[1].wait()
        if not cgrid:

            @pl.when(at_start)
            def _():
                for c in range(5):
                    sign = -1.0 if c in (1, 2, 3) else 1.0
                    qe[c, 1] = sign * qe[c, 2]
                    qe[c, 0] = sign * qe[c, 3]

        store_prims(1, 0)
        store_prims(2, 1)

    @pl.when((step > 0) & (step < steps - 1))
    def _():
        part(step + 1).wait()

    if not cgrid:

        @pl.when((step == steps - 1) & at_end)
        def _():
            for c in range(5):
                qe[c, planes + 2] = qe[c, planes + 1]
                qe[c, planes + 3] = qe[c, planes + 1]

    row_at = lax.broadcasted_iota(i32, (8, lanes), 0)
    lane_at = lax.broadcasted_iota(i32, (rows, 128), 1)
    row_first, row_last = row_at == 0, row_at == 7
    lane_first, lane_last = lane_at == 0, lane_at == 127

    def one(b, _):
        k = step * step_planes + b
        here, below, above = lax.rem(k + 1, 3), lax.rem(k, 3), lax.rem(k + 2, 3)
        store_prims(k + 3, above)

        def sub_next(x, i):
            moved = [pltpu.roll(x[r : r + 8], 7, 0) for r in range(0, rows, 8)]
            moved.append(sub_edge[1, i, pl.ds(k, 1), :])
            return jnp.concatenate(
                [jnp.where(row_last, moved[r + 1], moved[r]) for r in range(rows // 8)], axis=0
            )

        def sub_prior(x, i):
            moved = [sub_edge[0, i, pl.ds(k, 1), :]]
            moved += [pltpu.roll(x[r : r + 8], 1, 0) for r in range(0, rows, 8)]
            return jnp.concatenate(
                [jnp.where(row_first, moved[r], moved[r + 1]) for r in range(rows // 8)], axis=0
            )

        def lane_next(x):
            moved = [pltpu.roll(x[:, t : t + 128], 127, 1) for t in range(0, lanes, 128)]
            moved.append(x[:, lanes - 128 :] if cgrid else moved[0])
            return jnp.concatenate(
                [jnp.where(lane_last, moved[t + 1], moved[t]) for t in range(lanes // 128)], axis=1
            )

        def lane_prior(x, i):
            moved = [pltpu.roll(x[:, t : t + 128], 1, 1) for t in range(0, lanes, 128)]
            if cgrid:
                moved.insert(0, pltpu.roll(lane_edge[i], lax.rem(128 - 2 * k, 128), 1))
            else:
                moved.insert(0, moved[-1])
            return jnp.concatenate(
                [jnp.where(lane_first, moved[t], moved[t + 1]) for t in range(lanes // 128)], axis=1
            )

        gm = metric_ref[metric_rows[0], b]
        gs = metric_ref[metric_rows[1], b]
        gl = metric_ref[metric_rows[2], b]
        gm2, gs2, gl2 = viscosity * gm * gm, viscosity * gs * gs, viscosity * gl * gl
        gm, gs, gl = damping * gm, damping * gs, damping * gl
        all2 = 2.0 * (gm2 + gs2 + gl2)
        all6 = 6.0 * (gm + gs + gl)
        mine = [prim[here, i] for i in range(5)]
        viscous = {}
        for i, c, e in ((0, 1, 10), (1, 2, 11), (2, 3, 12), (4, 4, 13)):
            x = mine[i]
            total = gm2 * (prim[above, i] + prim[below, i])
            total += gs2 * (sub_next(x, e) + sub_prior(x, e))
            total += gl2 * (lane_next(x) + lane_prior(x, e))
            viscous[c] = total - all2 * x
        q = [qe[c, k + 2] for c in range(5)]
        sub_flux = flux(q, mine, sub_m)
        lane_flux = flux(q, mine, lane_m)
        for c in range(5):
            x = q[c]
            four = 4.0 * x
            total = gm * (
                4.0 * (qe[c, k + 3] + qe[c, k + 1])
                - (qe[c, k + 4] + qe[c, k])
                - (prim[above, 5 + c] - prim[below, 5 + c])
            )
            up = four - sub_flux[c] - sub_next(x, 5 + c)
            down = four + sub_flux[c] - sub_prior(x, 5 + c)
            total += gs * (sub_next(up, c) + sub_prior(down, c))
            up = four - lane_flux[c] - lane_next(x)
            down = four + lane_flux[c] - lane_prior(x, 5 + c)
            total += gl * (lane_next(up) + lane_prior(down, c))
            total -= all6 * x
            if c:
                total += viscous[c]
            if not cgrid:
                total = jnp.where(mask_ref[b] == 1, total, 0.0)
            out_ref[c, b] = total
        return 0

    lax.fori_loop(0, step_planes, one, 0)


def rate(q, majors, subs, extras, metric, mask, *, cgrid, step_planes, components, metric_rows):
    _, planes, rows, lanes = q.shape
    anywhere = pl.BlockSpec(memory_space=pl.ANY)
    block = lambda n: pl.BlockSpec((n, step_planes, rows, lanes), lambda i: (0, i, 0, 0))
    last_specs = [block(3)]
    last = (metric,)
    if mask is not None:
        last_specs = [pl.BlockSpec((step_planes, rows, lanes), lambda i: (i, 0, 0))] + last_specs
        last = (mask, metric)
    return pl.pallas_call(
        functools.partial(
            rate_kernel,
            cgrid=cgrid,
            step_planes=step_planes,
            components=components,
            metric_rows=metric_rows,
        ),
        grid=(planes // step_planes,),
        in_specs=[anywhere] + [IN_VMEM] * (4 + len(extras)) + last_specs,
        out_specs=block(5),
        out_shape=jax.ShapeDtypeStruct(q.shape, f32),
        scratch_shapes=[
            pltpu.VMEM((5, planes + 4, rows, lanes), f32),
            pltpu.VMEM((3, 10, rows, lanes), f32),
            pltpu.VMEM((2, 14, planes, lanes), f32),
        ]
        + [pltpu.VMEM((14, rows, 128), f32)] * cgrid
        + [pltpu.SemaphoreType.DMA((planes // step_planes + 2,))],
        compiler_params=params(),
        cost_estimate=pl.CostEstimate(
            flops=300 * planes * rows * lanes, bytes_accessed=60 * planes * rows * lanes, transcendentals=0
        ),
        name="cgrid_rate" if cgrid else "flap_rate",
    )(q, *majors, *subs, *extras, *last)


def split_two(x):
    high = x.astype(bf16)
    return high, (x - high.astype(f32)).astype(bf16)


def lookup(both, at):
    width = at.shape[1]
    highs = 32
    components = both.shape[0] // (2 * highs)
    cells = lax.broadcasted_iota(i32, (256, width), 0).astype(f32).astype(bf16)
    sub = lax.broadcasted_iota(i32, (8, width), 0)
    pick = jnp.where(
        cells == (at & 255).astype(f32).astype(bf16), jnp.ones((), bf16), jnp.zeros((), bf16)
    )
    high = at // 256
    found = jnp.dot(both, pick, preferred_element_type=f32)
    masks = [sub + 8 * g == high for g in range(highs // 8)]
    values = []
    for c in range(components):
        value = None
        for g, mask in enumerate(masks):
            r = c * highs + 8 * g
            remainder = components * highs + r
            piece = found[r : r + 8] + found[remainder : remainder + 8]
            value = jnp.where(mask, piece, 0.0 if value is None else value)
        values.append(jnp.sum(value, axis=0, keepdims=True))
    return values


def take_lanes(values, lanes):
    return lax.gather(
        values,
        lanes[..., None],
        lax.GatherDimensionNumbers(
            offset_dims=(),
            collapsed_slice_dims=(1,),
            start_index_map=(1,),
            operand_batching_dims=(0,),
            start_indices_batching_dims=(0,),
        ),
        slice_sizes=(1, 1),
        mode=lax.GatherScatterMode.PROMISE_IN_BOUNDS,
    )


def add_remainders(table):
    half = table.shape[0] // 2
    for r in range(0, half, 8):
        value = table[r : r + 8, :]
        table[half + r : half + r + 8, :] = value - value.astype(bf16).astype(f32)


def donor_kernel(
    cell_ref,
    frac_ref,
    q_hbm,
    out_ref,
    wrap_lo,
    wrap_hi,
    span_lo,
    span_hi,
    wall,
    q_ref,
    planes,
    pieces,
    rank_ref,
    ordered,
    where_ref,
    first,
    partial,
    table,
    sems,
):
    spans, rows, lanes = q_ref.shape[1:]
    count, slots = cell_ref.shape
    tile = 256
    tiles = count * slots // tile
    wide = slots // 128
    one, zero = jnp.ones((), bf16), jnp.zeros((), bf16)
    fetch = pltpu.make_async_copy(q_hbm, q_ref, sems.at[0])
    fetch.start()

    cell = cell_ref[...]
    upper = jnp.floor((cell.astype(f32) + 0.5) * (1.0 / (lanes - 1)))
    span = jnp.floor((upper + 0.5) * (1.0 / (rows - 1)))
    pieces[0] = span
    pieces[1] = upper - span * (rows - 1)
    pieces[2] = cell.astype(f32) - upper * (lanes - 1)
    for d in range(3):
        f = frac_ref[d]
        high = f.astype(bf16).astype(f32)
        pieces[3 + 2 * d] = high
        pieces[4 + 2 * d] = f - high

    lines = jnp.concatenate([span[:, 128 * t : 128 * t + 128] for t in range(wide)], axis=0)
    depth = lines.shape[0]
    hits = [jnp.where(lines == b, 1.0, 0.0).astype(bf16) for b in range(spans)]
    into = lax.broadcasted_iota(i32, (128, 256), 0)
    onto = lax.broadcasted_iota(i32, (128, 256), 1)
    before = jnp.where((into < onto) | (onto >= 128), 1.0, 0.0).astype(bf16)
    inside = jnp.dot(jnp.concatenate(hits, axis=0), before, preferred_element_type=f32)
    sums = [inside[b * depth : (b + 1) * depth, 128:256] for b in range(spans)]
    lower = lax.broadcasted_iota(i32, (depth, depth), 1) < lax.broadcasted_iota(i32, (depth, depth), 0)
    above = jnp.dot(
        jnp.where(lower, 1.0, 0.0).astype(bf16),
        jnp.concatenate([x.astype(bf16) for x in sums], axis=1),
        preferred_element_type=f32,
    )
    start = jnp.zeros((1, 128), f32)
    rank = jnp.zeros((depth, 128), f32)
    for b in range(spans):
        over = above[:, b * 128 : (b + 1) * 128]
        rank = jnp.where(lines == b, inside[b * depth : (b + 1) * depth, 0:128] + over + start, rank)
        start = start + over[depth - 1 :] + sums[b][depth - 1 :]
    rank = rank.astype(i32)
    for t in range(wide):
        rank_ref[:, 128 * t : 128 * t + 128] = rank[8 * t : 8 * t + 8]

    tile_at = lax.broadcasted_iota(i32, (tiles, slots), 0).astype(f32).astype(bf16)
    place_at = lax.broadcasted_iota(i32, (tile, slots), 0).astype(f32).astype(bf16)
    ordered[...] = jnp.zeros_like(ordered)

    def order(w, _):
        to = rank_ref[pl.ds(w, 1), :]
        in_tile = jnp.where(tile_at == (to // tile).astype(f32).astype(bf16), one, zero)
        at_place = jnp.where(place_at == (to & (tile - 1)).astype(f32).astype(bf16), one, zero)
        parts = [in_tile * pieces[p, pl.ds(w, 1), :].astype(bf16) for p in range(9)]
        ordered[...] += lax.dot_general(
            jnp.concatenate(parts, axis=0),
            at_place,
            (((1,), (1,)), ((), ())),
            preferred_element_type=f32,
        )
        return 0

    lax.fori_loop(0, count, order, 0, unroll=4)
    where_ref[...] = ordered[0:tiles, :].astype(i32)
    copy = pltpu.make_async_copy(where_ref, first, sems.at[1])
    copy.start()

    fetch.wait()
    pack(q_ref, wrap_lo, wrap_hi, span_lo, span_hi, wall)

    def prepare(k, _):
        for c in range(5):
            high, low = split_two(q_ref[c, k])
            here = pl.ds(pl.multiple_of(k * 5 * rows + c * rows, 16), rows)
            planes[here, 0:lanes] = high
            planes[here, lanes : 2 * lanes] = low
            planes[here, 2 * lanes : 3 * lanes] = high
        return 0

    lax.fori_loop(0, spans, prepare, 0)
    copy.wait()

    def weights(cells, at, frac):
        here = lax.broadcasted_iota(i32, (cells, tile), 0)
        return jnp.where(here == at, 1.0 - frac, jnp.where(here == at + 1, frac, 0.0))

    def tile_of(i):
        def piece(p):
            return ordered[pl.ds(p * tiles + i, 1), :]

        span, wrap, normal = piece(0).astype(i32), piece(1).astype(i32), piece(2).astype(i32)
        f0, f1, f2 = [piece(3 + 2 * d) + piece(4 + 2 * d) for d in range(3)]
        cells = lax.broadcasted_iota(i32, (lanes, tile), 0).astype(f32).astype(bf16)
        at_lower, at_upper = [cells == (normal + n).astype(f32).astype(bf16) for n in range(2)]
        (lower_high, lower_low), (upper_high, upper_low) = split_two(1.0 - f2), split_two(f2)
        high = jnp.where(at_lower, lower_high, jnp.where(at_upper, upper_high, zero))
        low = jnp.where(at_lower, lower_low, jnp.where(at_upper, upper_low, zero))
        return span, f0, jnp.concatenate([high, high, low], axis=0), weights(rows, wrap, f1)

    def add_planes(k, number, made, sums):
        span, f0, along, across = made
        from_row = pl.ds(pl.multiple_of(k * 5 * rows, 16), number * 5 * rows)
        mixed = jnp.dot(planes[from_row, :], along, preferred_element_type=f32)
        new = list(sums)
        for n in range(number):
            ws = jnp.where(span == k + n, 1.0 - f0, jnp.where(span + 1 == k + n, f0, 0.0))
            for c in range(5):
                r0 = (5 * n + c) * rows
                total = mixed[r0 : r0 + 8] * across[0:8]
                for r in range(8, rows, 8):
                    total += mixed[r0 + r : r0 + r + 8] * across[r : r + 8]
                new[c] = ws * total if new[c] is None else new[c] + ws * total
        return tuple(new)

    def step(g, _):
        for n in range(GROUP):
            i = g * GROUP + n
            for c, x in enumerate(add_planes(first[i, 0], 2, tile_of(i), (None,) * 5)):
                partial[n, c] = x
        for n in range(GROUP):
            i = g * GROUP + n
            lowest = first[i, 0]
            more = first[i, tile - 1] - lowest

            @pl.when(more > 0)
            def _():
                made = tile_of(i)

                def again(m, _):
                    sums = add_planes(lowest + 2 + m, 1, made, tuple(partial[n, c] for c in range(5)))
                    for c in range(5):
                        partial[n, c] = sums[c]
                    return 0

                lax.fori_loop(0, more, again, 0)

        for n in range(GROUP):
            i = g * GROUP + n
            for c in range(5):
                table[pl.ds(c * tiles + i, 1), :] = jnp.sum(partial[n, c], axis=0, keepdims=True)
        return 0

    lax.fori_loop(0, tiles // GROUP, step, 0)

    add_remainders(table)
    both = table[...].astype(bf16)

    def put_back(w, _):
        for t in range(0, slots, 512):
            for c, value in enumerate(lookup(both, rank_ref[pl.ds(w, 1), t : t + 512])):
                out_ref[w, c : c + 1, t : t + 512] = value
        return 0

    lax.fori_loop(0, count, put_back, 0, unroll=8)


def donors(cell, frac, state):
    _, spans, rows, lanes = state.shape
    count, slots = cell.shape
    tiles = count * slots // 256
    shapes = [(count, 5, slots)]
    shapes += [(5, 2, spans, lanes)] * 2 + [(5, 2, rows, lanes)] * 2 + [(5, rows, 2 * spans)]
    return pl.pallas_call(
        donor_kernel,
        grid=(1,),
        in_specs=[IN_VMEM, IN_VMEM, IN_HBM],
        out_specs=[whole(x) for x in shapes],
        out_shape=[jax.ShapeDtypeStruct(x, f32) for x in shapes],
        scratch_shapes=[
            pltpu.VMEM(state.shape, f32),
            pltpu.VMEM((spans * 5 * rows, 3 * lanes), bf16),
            pltpu.VMEM((9, count, slots), f32),
            pltpu.VMEM((count, slots), i32),
            pltpu.VMEM((9 * tiles, 256), f32),
            pltpu.VMEM((tiles, 256), i32),
            pltpu.SMEM((tiles, 256), i32),
            pltpu.VMEM((GROUP, 5, 8, 256), f32),
            pltpu.VMEM((10 * tiles, 256), f32),
            pltpu.SemaphoreType.DMA((2,)),
        ],
        compiler_params=params(60 * 1024 * 1024),
        name="donors",
    )(cell, frac, state)


def fill_kernel(
    from_ref,
    mask_ref,
    q_hbm,
    slot_ref,
    out_ref,
    norm_lo,
    norm_hi,
    span_lo,
    span_hi,
    table,
    spread,
    q_ref,
    sems,
):
    planes = pl.num_programs(0)
    rows, lanes = from_ref.shape[1:]
    count, _, slots = slot_ref.shape
    j = pl.program_id(0)

    def fetch(n):
        return pltpu.make_async_copy(q_hbm.at[:, n], q_ref.at[:, n], sems.at[n])

    @pl.when(j == 0)
    def _():
        for n in range(q_ref.shape[1]):
            fetch(n).start()
        per = slots // 256
        for c in range(4):
            for w in range(count):
                for r in range(per):
                    at = c * count * per + w * per + r
                    table[at : at + 1, :] = slot_ref[w, c : c + 1, r * 256 : (r + 1) * 256]
        add_remainders(table)
        for w in range(count):
            for r in range(slots // 128):
                value = slot_ref[w, 4:5, r * 128 : (r + 1) * 128]
                spread[w * (slots // 128) + r] = jnp.broadcast_to(value, (8, 128))

    fetch(j).wait()
    both = table[...].astype(bf16)
    lines = spread.shape[0]
    share = (rows // 8) * (lanes // 128) * lines // rows
    value = None
    for s in range(rows):
        keep = mask_ref[0, s : s + 1, :] == 1
        for c, found in enumerate(lookup(both, from_ref[0, s : s + 1, :])):
            out_ref[c, 0, s : s + 1, :] = jnp.where(keep, q_ref[c, j, s : s + 1, :], found)
        for n in range(s * share, (s + 1) * share):
            line = n % lines
            if line == 0:
                row, lane = divmod(n // lines, lanes // 128)
                here = (slice(8 * row, 8 * row + 8), slice(128 * lane, 128 * lane + 128))
                at = from_ref[0, here[0], here[1]]
                low, high = at & 127, at // 128
                value = jnp.zeros((8, 128), f32)
            value = jnp.where(high == line, take_lanes(spread[line], low), value)
            if line == lines - 1:
                keep = mask_ref[0, here[0], here[1]] == 1
                out_ref[4, 0, here[0], here[1]] = jnp.where(keep, q_ref[4, j, here[0], here[1]], value)

    for c in range(5):
        for l in range(2):
            span_lo[c, l, pl.ds(j, 1), :] = out_ref[c, 0, l : l + 1, :]
            span_hi[c, l, pl.ds(j, 1), :] = out_ref[c, 0, rows - 2 + l : rows - 1 + l, :]

    @pl.when(j < 2)
    def _():
        for c in range(5):
            norm_lo[c, j] = out_ref[c, 0]

    @pl.when(j >= planes - 2)
    def _():
        for c in range(5):
            norm_hi[c, j - (planes - 2)] = out_ref[c, 0]


def fill(source, mask, state, slot):
    _, planes, rows, lanes = state.shape
    count, _, slots = slot.shape
    plane = pl.BlockSpec((1, rows, lanes), lambda j: (j, 0, 0))
    state_plane = pl.BlockSpec((5, 1, rows, lanes), lambda j: (0, j, 0, 0))
    edges = [(5, 2, rows, lanes)] * 2 + [(5, 2, planes, lanes)] * 2
    return pl.pallas_call(
        fill_kernel,
        grid=(planes,),
        in_specs=[plane, plane, IN_HBM, IN_VMEM],
        out_specs=[state_plane] + [whole(s) for s in edges],
        out_shape=[jax.ShapeDtypeStruct(s, f32) for s in [state.shape] + edges],
        scratch_shapes=[
            pltpu.VMEM((8 * count * slots // 256, 256), f32),
            pltpu.VMEM((count * slots // 128, 8, 128), f32),
            pltpu.VMEM(state.shape, f32),
            pltpu.SemaphoreType.DMA((planes,)),
        ],
        compiler_params=params(52 * 1024 * 1024),
        cost_estimate=pl.CostEstimate(flops=24 * 10**9, bytes_accessed=6 * 10**6, transcendentals=0),
        name="fill",
    )(source, mask, state, slot)


def body(
    cgrid_state, cgrid_metric, flap_state, flap_metric, iblank, fringe_from, donor_cell, donor_frac
):
    wrap_count = lax.axis_size("wrap")

    def ring(axis):
        size = lax.axis_size(axis)
        return [(i, (i + 1) % size) for i in range(size)]

    def onward(value, axis):
        return lax.ppermute(value, axis, ring(axis))

    def back(value, axis):
        return lax.ppermute(value, axis, [(j, i) for i, j in ring(axis)])

    slot, wrap_lo, wrap_hi, span_lo, span_hi, wall = donors(
        donor_cell[0], jnp.transpose(donor_frac[0], (1, 0, 2)), cgrid_state
    )
    far = lax.ppermute(
        wall,
        "wrap",
        [(i, wrap_count - 1 - i if wrapped(i, wrap_count) else i) for i in range(wrap_count)],
    )
    majors = (onward(span_hi, "span"), back(span_lo, "span"))
    subs = (onward(wrap_hi, "wrap"), back(wrap_lo, "wrap"))

    slot = lax.all_to_all(slot, "wrap", split_axis=0, concat_axis=0, tiled=True)

    turned = lambda x: jnp.swapaxes(x, -3, -2)
    mask = turned(iblank)
    filled, norm_lo, norm_hi, edge_lo, edge_hi = fill(turned(fringe_from), mask, turned(flap_state), slot)
    flap_majors = (onward(norm_hi, "wrap"), back(norm_lo, "wrap"))
    flap_subs = (onward(edge_hi, "span"), back(edge_lo, "span"))

    cgrid_rate = rate(
        cgrid_state,
        majors,
        subs,
        (wrap_lo, wrap_hi, wall, far),
        cgrid_metric,
        None,
        cgrid=True,
        step_planes=4,
        components=(3, 1, 2),
        metric_rows=(0, 1, 2),
    )
    flap_rate = rate(
        filled,
        flap_majors,
        flap_subs,
        (),
        turned(flap_metric),
        mask,
        cgrid=False,
        step_planes=3,
        components=(2, 3, 1),
        metric_rows=(1, 0, 2),
    )
    return (cgrid_rate, turned(flap_rate))


def solution(mesh):
    return jax.shard_map(
        body,
        mesh=mesh,
        in_specs=(
            P(None, "span", "wrap", None),
            P(None, "span", "wrap", None),
            P(None, "span", "wrap", None),
            P(None, "span", "wrap", None),
            P("span", "wrap", None),
            P("span", "wrap", None),
            P(("wrap", "span"), None, None),
            P(("wrap", "span"), None, None, None),
        ),
        out_specs=(P(None, "span", "wrap", None), P(None, "span", "wrap", None)),
        check_vma=False,
    )
```

```python
import functools

import jax
import jax.numpy as jnp
from jax import lax
from jax.experimental import pallas as pl
from jax.experimental.pallas import tpu as pltpu
from jax.sharding import PartitionSpec as P

viscosity = 0.05
conduction = 0.07
damping = 1.0 / 32.0
VMEM_LIMIT = 40 * 1024 * 1024
IN_HBM = pl.BlockSpec(memory_space=pltpu.HBM)
IN_VMEM = pl.BlockSpec(memory_space=pltpu.VMEM)
GROUP = 8

f32, bf16, i32 = jnp.float32, jnp.bfloat16, jnp.int32


def whole(shape):
    return pl.BlockSpec(shape, lambda *_: (0,) * len(shape))


def params(limit=VMEM_LIMIT):
    return pltpu.CompilerParams(vmem_limit_bytes=limit)


def primitives(q):
    inverse = 1.0 / q[0]
    v = [q[m] * inverse for m in (1, 2, 3)]
    kinetic = 0.5 * (v[0] * v[0] + v[1] * v[1] + v[2] * v[2])
    pressure = 0.4 * (q[4] - q[0] * kinetic)
    return v + [pressure, kinetic + (conduction / viscosity) * (pressure * inverse)]


def wrapped(place, count):
    return (place < count // 4) | (place >= count - count // 4)


def flux(q, prims, m):
    u = (0.5 / damping) * prims[m - 1]
    f = [q[0] * u]
    for c in (1, 2, 3):
        f.append(q[c] * u + (0.5 / damping) * prims[3] if c == m else q[c] * u)
    f.append((q[4] + prims[3]) * u)
    return f


def pack(q_ref, wrap_lo, wrap_hi, span_lo, span_hi, wall):
    spans, rows = q_ref.shape[1], q_ref.shape[2]
    lane = lax.broadcasted_iota(i32, (rows, 128), 1)
    for c in range(5):
        for l in range(2):
            span_lo[c, l] = q_ref[c, l]
            span_hi[c, l] = q_ref[c, spans - 2 + l]
        cells = jnp.zeros((rows, 128), f32)
        for k in range(spans):
            for l in range(2):
                wrap_lo[c, l, k : k + 1, :] = q_ref[c, k, l : l + 1, :]
                wrap_hi[c, l, k : k + 1, :] = q_ref[c, k, rows - 2 + l : rows - 1 + l, :]
            near = q_ref[c, k, :, 0:128]
            if k:
                near = pltpu.roll(near, 2 * k, 1)
            cells = jnp.where(lane // 2 == k, near, cells)
        wall[c] = cells[:, 0 : 2 * spans]


def rate_kernel(
    q_hbm,
    major_lo,
    major_hi,
    sub_lo,
    sub_hi,
    *refs,
    cgrid,
    step_planes,
    components,
    metric_rows,
):
    if cgrid:
        own_lo, own_hi, wall_own, wall_far, metric_ref, out_ref, qe, prim, sub_edge, lane_edge, sems = refs
    else:
        own_lo = own_hi = None
        mask_ref, metric_ref, out_ref, qe, prim, sub_edge, sems = refs
    planes, rows, lanes = qe.shape[1] - 4, qe.shape[2], qe.shape[3]
    step = pl.program_id(0)
    place, count = lax.axis_index("wrap"), lax.axis_size("wrap")
    at_start = place == 0
    at_end = place == count - 1
    major_m, sub_m, lane_m = components

    def edge_fields(q1, q2, m, side):
        prims = primitives(q1)
        fl = flux(q1, prims, m)
        lead = [4.0 * q1[c] - side * fl[c] - q2[c] for c in range(5)]
        return lead + q1 + prims[:3] + prims[4:]

    def store_prims(k, slot):
        q = [qe[c, k] for c in range(5)]
        prims = primitives(q)
        for i, x in enumerate(prims + flux(q, prims, major_m)):
            prim[slot, i] = x

    steps = planes // step_planes

    def part(n):
        n = n * step_planes
        return pltpu.make_async_copy(
            q_hbm.at[:, pl.ds(n, step_planes)], qe.at[:, pl.ds(n + 2, step_planes)], sems.at[n // step_planes]
        )

    @pl.when(step == 0)
    def _():
        copies = [
            pltpu.make_async_copy(major_lo, qe.at[:, pl.ds(0, 2)], sems.at[steps]),
            pltpu.make_async_copy(major_hi, qe.at[:, pl.ds(planes + 2, 2)], sems.at[steps + 1]),
        ]
        copies[0].start()
        for n in range(steps):
            part(n).start()
        copies[1].start()
        for side, ref, own in ((-1, sub_lo, own_lo), (1, sub_hi, own_hi)):
            near, far = (1, 0) if side < 0 else (0, 1)
            q1 = [ref[c, near] for c in range(5)]
            q2 = [ref[c, far] for c in range(5)]
            if cgrid:
                edge = at_start if side < 0 else at_end
                clamp = 0 if side < 0 else 1
                q1 = [jnp.where(edge, own[c, clamp], q1[c]) for c in range(5)]
                q2 = [jnp.where(edge, own[c, clamp], q2[c]) for c in range(5)]
            for i, x in enumerate(edge_fields(q1, q2, sub_m, side)):
                sub_edge[(side + 1) // 2, i] = x
        if cgrid:
            in_wake = wrapped(place, count)
            turn = 7 - lax.broadcasted_iota(i32, (8, 128), 0)
            ghosts = []
            for c in range(5):
                sign = -1.0 if c in (1, 2, 3) else 1.0
                parts = []
                for r in range(rows // 8):
                    far = wall_far[c, rows - 8 - 8 * r : rows - 8 * r, :]
                    own = wall_own[c, 8 * r : 8 * r + 8, :]
                    own = jnp.concatenate([own, jnp.zeros((8, 128 - own.shape[1]), f32)], axis=1)
                    far = jnp.concatenate([far, jnp.zeros((8, 128 - far.shape[1]), f32)], axis=1)
                    far = jnp.take_along_axis(far, turn, axis=0, mode="promise_in_bounds")
                    parts.append(jnp.where(in_wake, far, sign * own))
                ghosts.append(jnp.concatenate(parts, axis=0))
            second = [pltpu.roll(x, 127, 1) for x in ghosts]
            for i, x in enumerate(edge_fields(ghosts, second, lane_m, -1)):
                lane_edge[i] = x
        copies[0].wait()
        part(0).wait()
        part(1).wait()
        copies[1].wait()
        if not cgrid:

            @pl.when(at_start)
            def _():
                for c in range(5):
                    sign = -1.0 if c in (1, 2, 3) else 1.0
                    qe[c, 1] = sign * qe[c, 2]
                    qe[c, 0] = sign * qe[c, 3]

        store_prims(1, 0)
        store_prims(2, 1)

    @pl.when((step > 0) & (step < steps - 1))
    def _():
        part(step + 1).wait()

    if not cgrid:

        @pl.when((step == steps - 1) & at_end)
        def _():
            for c in range(5):
                qe[c, planes + 2] = qe[c, planes + 1]
                qe[c, planes + 3] = qe[c, planes + 1]

    row_at = lax.broadcasted_iota(i32, (8, lanes), 0)
    lane_at = lax.broadcasted_iota(i32, (rows, 128), 1)
    row_first, row_last = row_at == 0, row_at == 7
    lane_first, lane_last = lane_at == 0, lane_at == 127

    def one(b, _):
        k = step * step_planes + b
        here, below, above = lax.rem(k + 1, 3), lax.rem(k, 3), lax.rem(k + 2, 3)
        store_prims(k + 3, above)

        def sub_next(x, i):
            moved = [pltpu.roll(x[r : r + 8], 7, 0) for r in range(0, rows, 8)]
            moved.append(sub_edge[1, i, pl.ds(k, 1), :])
            return jnp.concatenate(
                [jnp.where(row_last, moved[r + 1], moved[r]) for r in range(rows // 8)], axis=0
            )

        def sub_prior(x, i):
            moved = [sub_edge[0, i, pl.ds(k, 1), :]]
            moved += [pltpu.roll(x[r : r + 8], 1, 0) for r in range(0, rows, 8)]
            return jnp.concatenate(
                [jnp.where(row_first, moved[r], moved[r + 1]) for r in range(rows // 8)], axis=0
            )

        def lane_next(x):
            moved = [pltpu.roll(x[:, t : t + 128], 127, 1) for t in range(0, lanes, 128)]
            moved.append(x[:, lanes - 128 :] if cgrid else moved[0])
            return jnp.concatenate(
                [jnp.where(lane_last, moved[t + 1], moved[t]) for t in range(lanes // 128)], axis=1
            )

        def lane_prior(x, i):
            moved = [pltpu.roll(x[:, t : t + 128], 1, 1) for t in range(0, lanes, 128)]
            if cgrid:
                moved.insert(0, pltpu.roll(lane_edge[i], lax.rem(128 - 2 * k, 128), 1))
            else:
                moved.insert(0, moved[-1])
            return jnp.concatenate(
                [jnp.where(lane_first, moved[t], moved[t + 1]) for t in range(lanes // 128)], axis=1
            )

        gm = metric_ref[metric_rows[0], b]
        gs = metric_ref[metric_rows[1], b]
        gl = metric_ref[metric_rows[2], b]
        gm2, gs2, gl2 = viscosity * gm * gm, viscosity * gs * gs, viscosity * gl * gl
        gm, gs, gl = damping * gm, damping * gs, damping * gl
        all2 = 2.0 * (gm2 + gs2 + gl2)
        all6 = 6.0 * (gm + gs + gl)
        mine = [prim[here, i] for i in range(5)]
        viscous = {}
        for i, c, e in ((0, 1, 10), (1, 2, 11), (2, 3, 12), (4, 4, 13)):
            x = mine[i]
            total = gm2 * (prim[above, i] + prim[below, i])
            total += gs2 * (sub_next(x, e) + sub_prior(x, e))
            total += gl2 * (lane_next(x) + lane_prior(x, e))
            viscous[c] = total - all2 * x
        q = [qe[c, k + 2] for c in range(5)]
        sub_flux = flux(q, mine, sub_m)
        lane_flux = flux(q, mine, lane_m)
        for c in range(5):
            x = q[c]
            four = 4.0 * x
            total = gm * (
                4.0 * (qe[c, k + 3] + qe[c, k + 1])
                - (qe[c, k + 4] + qe[c, k])
                - (prim[above, 5 + c] - prim[below, 5 + c])
            )
            up = four - sub_flux[c] - sub_next(x, 5 + c)
            down = four + sub_flux[c] - sub_prior(x, 5 + c)
            total += gs * (sub_next(up, c) + sub_prior(down, c))
            up = four - lane_flux[c] - lane_next(x)
            down = four + lane_flux[c] - lane_prior(x, 5 + c)
            total += gl * (lane_next(up) + lane_prior(down, c))
            total -= all6 * x
            if c:
                total += viscous[c]
            if not cgrid:
                total = jnp.where(mask_ref[b] == 1, total, 0.0)
            out_ref[c, b] = total
        return 0

    lax.fori_loop(0, step_planes, one, 0)


def rate(q, majors, subs, extras, metric, mask, *, cgrid, step_planes, components, metric_rows):
    _, planes, rows, lanes = q.shape
    anywhere = pl.BlockSpec(memory_space=pl.ANY)
    block = lambda n: pl.BlockSpec((n, step_planes, rows, lanes), lambda i: (0, i, 0, 0))
    last_specs = [block(3)]
    last = (metric,)
    if mask is not None:
        last_specs = [pl.BlockSpec((step_planes, rows, lanes), lambda i: (i, 0, 0))] + last_specs
        last = (mask, metric)
    return pl.pallas_call(
        functools.partial(
            rate_kernel,
            cgrid=cgrid,
            step_planes=step_planes,
            components=components,
            metric_rows=metric_rows,
        ),
        grid=(planes // step_planes,),
        in_specs=[anywhere] + [IN_VMEM] * (4 + len(extras)) + last_specs,
        out_specs=block(5),
        out_shape=jax.ShapeDtypeStruct(q.shape, f32),
        scratch_shapes=[
            pltpu.VMEM((5, planes + 4, rows, lanes), f32),
            pltpu.VMEM((3, 10, rows, lanes), f32),
            pltpu.VMEM((2, 14, planes, lanes), f32),
        ]
        + [pltpu.VMEM((14, rows, 128), f32)] * cgrid
        + [pltpu.SemaphoreType.DMA((planes // step_planes + 2,))],
        compiler_params=params(),
        cost_estimate=pl.CostEstimate(
            flops=300 * planes * rows * lanes, bytes_accessed=60 * planes * rows * lanes, transcendentals=0
        ),
        name="cgrid_rate" if cgrid else "flap_rate",
    )(q, *majors, *subs, *extras, *last)


def split_two(x):
    high = x.astype(bf16)
    return high, (x - high.astype(f32)).astype(bf16)


def lookup(both, at):
    width = at.shape[1]
    highs = 32
    components = both.shape[0] // (2 * highs)
    cells = lax.broadcasted_iota(i32, (256, width), 0).astype(f32).astype(bf16)
    sub = lax.broadcasted_iota(i32, (8, width), 0)
    pick = jnp.where(
        cells == (at & 255).astype(f32).astype(bf16), jnp.ones((), bf16), jnp.zeros((), bf16)
    )
    high = at // 256
    found = jnp.dot(both, pick, preferred_element_type=f32)
    masks = [sub + 8 * g == high for g in range(highs // 8)]
    values = []
    for c in range(components):
        value = None
        for g, mask in enumerate(masks):
            r = c * highs + 8 * g
            remainder = components * highs + r
            piece = found[r : r + 8] + found[remainder : remainder + 8]
            value = jnp.where(mask, piece, 0.0 if value is None else value)
        values.append(jnp.sum(value, axis=0, keepdims=True))
    return values


def take_lanes(values, lanes):
    return lax.gather(
        values,
        lanes[..., None],
        lax.GatherDimensionNumbers(
            offset_dims=(),
            collapsed_slice_dims=(1,),
            start_index_map=(1,),
            operand_batching_dims=(0,),
            start_indices_batching_dims=(0,),
        ),
        slice_sizes=(1, 1),
        mode=lax.GatherScatterMode.PROMISE_IN_BOUNDS,
    )


def add_remainders(table):
    half = table.shape[0] // 2
    for r in range(0, half, 8):
        value = table[r : r + 8, :]
        table[half + r : half + r + 8, :] = value - value.astype(bf16).astype(f32)


def donor_kernel(
    cell_ref,
    frac_ref,
    q_hbm,
    out_ref,
    wrap_lo,
    wrap_hi,
    span_lo,
    span_hi,
    wall,
    q_ref,
    planes,
    pieces,
    rank_ref,
    ordered,
    where_ref,
    first,
    partial,
    table,
    sems,
):
    spans, rows, lanes = q_ref.shape[1:]
    count, slots = cell_ref.shape
    tile = 256
    tiles = count * slots // tile
    wide = slots // 128
    one, zero = jnp.ones((), bf16), jnp.zeros((), bf16)
    fetch = pltpu.make_async_copy(q_hbm, q_ref, sems.at[0])
    fetch.start()

    cell = cell_ref[...]
    upper = jnp.floor((cell.astype(f32) + 0.5) * (1.0 / (lanes - 1)))
    span = jnp.floor((upper + 0.5) * (1.0 / (rows - 1)))
    pieces[0] = span
    pieces[1] = upper - span * (rows - 1)
    pieces[2] = cell.astype(f32) - upper * (lanes - 1)
    for d in range(3):
        f = frac_ref[d]
        high = f.astype(bf16).astype(f32)
        pieces[3 + 2 * d] = high
        pieces[4 + 2 * d] = f - high

    lines = jnp.concatenate([span[:, 128 * t : 128 * t + 128] for t in range(wide)], axis=0)
    depth = lines.shape[0]
    hits = [jnp.where(lines == b, 1.0, 0.0).astype(bf16) for b in range(spans)]
    into = lax.broadcasted_iota(i32, (128, 256), 0)
    onto = lax.broadcasted_iota(i32, (128, 256), 1)
    before = jnp.where((into < onto) | (onto >= 128), 1.0, 0.0).astype(bf16)
    inside = jnp.dot(jnp.concatenate(hits, axis=0), before, preferred_element_type=f32)
    sums = [inside[b * depth : (b + 1) * depth, 128:256] for b in range(spans)]
    lower = lax.broadcasted_iota(i32, (depth, depth), 1) < lax.broadcasted_iota(i32, (depth, depth), 0)
    above = jnp.dot(
        jnp.where(lower, 1.0, 0.0).astype(bf16),
        jnp.concatenate([x.astype(bf16) for x in sums], axis=1),
        preferred_element_type=f32,
    )
    start = jnp.zeros((1, 128), f32)
    rank = jnp.zeros((depth, 128), f32)
    for b in range(spans):
        over = above[:, b * 128 : (b + 1) * 128]
        rank = jnp.where(lines == b, inside[b * depth : (b + 1) * depth, 0:128] + over + start, rank)
        start = start + over[depth - 1 :] + sums[b][depth - 1 :]
    rank = rank.astype(i32)
    for t in range(wide):
        rank_ref[:, 128 * t : 128 * t + 128] = rank[8 * t : 8 * t + 8]

    tile_at = lax.broadcasted_iota(i32, (tiles, slots), 0).astype(f32).astype(bf16)
    place_at = lax.broadcasted_iota(i32, (tile, slots), 0).astype(f32).astype(bf16)
    ordered[...] = jnp.zeros_like(ordered)

    def order(w, _):
        to = rank_ref[pl.ds(w, 1), :]
        in_tile = jnp.where(tile_at == (to // tile).astype(f32).astype(bf16), one, zero)
        at_place = jnp.where(place_at == (to & (tile - 1)).astype(f32).astype(bf16), one, zero)
        parts = [in_tile * pieces[p, pl.ds(w, 1), :].astype(bf16) for p in range(9)]
        ordered[...] += lax.dot_general(
            jnp.concatenate(parts, axis=0),
            at_place,
            (((1,), (1,)), ((), ())),
            preferred_element_type=f32,
        )
        return 0

    lax.fori_loop(0, count, order, 0, unroll=4)
    where_ref[...] = ordered[0:tiles, :].astype(i32)
    copy = pltpu.make_async_copy(where_ref, first, sems.at[1])
    copy.start()

    fetch.wait()
    pack(q_ref, wrap_lo, wrap_hi, span_lo, span_hi, wall)

    def prepare(k, _):
        for c in range(5):
            high, low = split_two(q_ref[c, k])
            here = pl.ds(pl.multiple_of(k * 5 * rows + c * rows, 16), rows)
            planes[here, 0:lanes] = high
            planes[here, lanes : 2 * lanes] = low
            planes[here, 2 * lanes : 3 * lanes] = high
        return 0

    lax.fori_loop(0, spans, prepare, 0)
    copy.wait()

    def weights(cells, at, frac):
        here = lax.broadcasted_iota(i32, (cells, tile), 0)
        return jnp.where(here == at, 1.0 - frac, jnp.where(here == at + 1, frac, 0.0))

    def tile_of(i):
        def piece(p):
            return ordered[pl.ds(p * tiles + i, 1), :]

        span, wrap, normal = piece(0).astype(i32), piece(1).astype(i32), piece(2).astype(i32)
        f0, f1, f2 = [piece(3 + 2 * d) + piece(4 + 2 * d) for d in range(3)]
        cells = lax.broadcasted_iota(i32, (lanes, tile), 0).astype(f32).astype(bf16)
        at_lower, at_upper = [cells == (normal + n).astype(f32).astype(bf16) for n in range(2)]
        (lower_high, lower_low), (upper_high, upper_low) = split_two(1.0 - f2), split_two(f2)
        high = jnp.where(at_lower, lower_high, jnp.where(at_upper, upper_high, zero))
        low = jnp.where(at_lower, lower_low, jnp.where(at_upper, upper_low, zero))
        return span, f0, jnp.concatenate([high, high, low], axis=0), weights(rows, wrap, f1)

    def add_planes(k, number, made, sums):
        span, f0, along, across = made
        from_row = pl.ds(pl.multiple_of(k * 5 * rows, 16), number * 5 * rows)
        mixed = jnp.dot(planes[from_row, :], along, preferred_element_type=f32)
        new = list(sums)
        for n in range(number):
            ws = jnp.where(span == k + n, 1.0 - f0, jnp.where(span + 1 == k + n, f0, 0.0))
            for c in range(5):
                r0 = (5 * n + c) * rows
                total = mixed[r0 : r0 + 8] * across[0:8]
                for r in range(8, rows, 8):
                    total += mixed[r0 + r : r0 + r + 8] * across[r : r + 8]
                new[c] = ws * total if new[c] is None else new[c] + ws * total
        return tuple(new)

    def lowest_of(i):
        return jnp.minimum(first[i, 0], spans - 3)

    def step(g, _):
        for n in range(GROUP):
            i = g * GROUP + n
            for c, x in enumerate(add_planes(lowest_of(i), 3, tile_of(i), (None,) * 5)):
                partial[n, c] = x
        for n in range(GROUP):
            i = g * GROUP + n
            lowest = lowest_of(i)
            more = first[i, tile - 1] - 1 - lowest

            @pl.when(more > 0)
            def _():
                made = tile_of(i)

                def again(m, _):
                    sums = add_planes(lowest + 3 + m, 1, made, tuple(partial[n, c] for c in range(5)))
                    for c in range(5):
                        partial[n, c] = sums[c]
                    return 0

                lax.fori_loop(0, more, again, 0)

        for n in range(GROUP):
            i = g * GROUP + n
            for c in range(5):
                table[pl.ds(c * tiles + i, 1), :] = jnp.sum(partial[n, c], axis=0, keepdims=True)
        return 0

    lax.fori_loop(0, tiles // GROUP, step, 0)

    add_remainders(table)
    both = table[...].astype(bf16)

    def put_back(w, _):
        for t in range(0, slots, 512):
            for c, value in enumerate(lookup(both, rank_ref[pl.ds(w, 1), t : t + 512])):
                out_ref[w, c : c + 1, t : t + 512] = value
        return 0

    lax.fori_loop(0, count, put_back, 0, unroll=8)


def donors(cell, frac, state):
    _, spans, rows, lanes = state.shape
    count, slots = cell.shape
    tiles = count * slots // 256
    shapes = [(count, 5, slots)]
    shapes += [(5, 2, spans, lanes)] * 2 + [(5, 2, rows, lanes)] * 2 + [(5, rows, 2 * spans)]
    return pl.pallas_call(
        donor_kernel,
        grid=(1,),
        in_specs=[IN_VMEM, IN_VMEM, IN_HBM],
        out_specs=[whole(x) for x in shapes],
        out_shape=[jax.ShapeDtypeStruct(x, f32) for x in shapes],
        scratch_shapes=[
            pltpu.VMEM(state.shape, f32),
            pltpu.VMEM((spans * 5 * rows, 3 * lanes), bf16),
            pltpu.VMEM((9, count, slots), f32),
            pltpu.VMEM((count, slots), i32),
            pltpu.VMEM((9 * tiles, 256), f32),
            pltpu.VMEM((tiles, 256), i32),
            pltpu.SMEM((tiles, 256), i32),
            pltpu.VMEM((GROUP, 5, 8, 256), f32),
            pltpu.VMEM((10 * tiles, 256), f32),
            pltpu.SemaphoreType.DMA((2,)),
        ],
        compiler_params=params(60 * 1024 * 1024),
        name="donors",
    )(cell, frac, state)


def fill_kernel(
    from_ref,
    mask_ref,
    q_hbm,
    slot_ref,
    out_ref,
    norm_lo,
    norm_hi,
    span_lo,
    span_hi,
    table,
    spread,
    q_ref,
    sems,
):
    planes = pl.num_programs(0)
    rows, lanes = from_ref.shape[1:]
    count, _, slots = slot_ref.shape
    j = pl.program_id(0)

    def fetch(n):
        return pltpu.make_async_copy(q_hbm.at[:, n], q_ref.at[:, n], sems.at[n])

    @pl.when(j == 0)
    def _():
        for n in range(q_ref.shape[1]):
            fetch(n).start()
        per = slots // 256
        for c in range(4):
            for w in range(count):
                for r in range(per):
                    at = c * count * per + w * per + r
                    table[at : at + 1, :] = slot_ref[w, c : c + 1, r * 256 : (r + 1) * 256]
        add_remainders(table)
        for w in range(count):
            for r in range(slots // 128):
                value = slot_ref[w, 4:5, r * 128 : (r + 1) * 128]
                spread[w * (slots // 128) + r] = jnp.broadcast_to(value, (8, 128))

    fetch(j).wait()
    both = table[...].astype(bf16)
    lines = spread.shape[0]
    share = (rows // 8) * (lanes // 128) * lines // rows
    value = None
    for s in range(rows):
        keep = mask_ref[0, s : s + 1, :] == 1
        for c, found in enumerate(lookup(both, from_ref[0, s : s + 1, :])):
            out_ref[c, 0, s : s + 1, :] = jnp.where(keep, q_ref[c, j, s : s + 1, :], found)
        for n in range(s * share, (s + 1) * share):
            line = n % lines
            if line == 0:
                row, lane = divmod(n // lines, lanes // 128)
                here = (slice(8 * row, 8 * row + 8), slice(128 * lane, 128 * lane + 128))
                at = from_ref[0, here[0], here[1]]
                low, high = at & 127, at // 128
                value = jnp.zeros((8, 128), f32)
            value = jnp.where(high == line, take_lanes(spread[line], low), value)
            if line == lines - 1:
                keep = mask_ref[0, here[0], here[1]] == 1
                out_ref[4, 0, here[0], here[1]] = jnp.where(keep, q_ref[4, j, here[0], here[1]], value)

    for c in range(5):
        for l in range(2):
            span_lo[c, l, pl.ds(j, 1), :] = out_ref[c, 0, l : l + 1, :]
            span_hi[c, l, pl.ds(j, 1), :] = out_ref[c, 0, rows - 2 + l : rows - 1 + l, :]

    @pl.when(j < 2)
    def _():
        for c in range(5):
            norm_lo[c, j] = out_ref[c, 0]

    @pl.when(j >= planes - 2)
    def _():
        for c in range(5):
            norm_hi[c, j - (planes - 2)] = out_ref[c, 0]


def fill(source, mask, state, slot):
    _, planes, rows, lanes = state.shape
    count, _, slots = slot.shape
    plane = pl.BlockSpec((1, rows, lanes), lambda j: (j, 0, 0))
    state_plane = pl.BlockSpec((5, 1, rows, lanes), lambda j: (0, j, 0, 0))
    edges = [(5, 2, rows, lanes)] * 2 + [(5, 2, planes, lanes)] * 2
    return pl.pallas_call(
        fill_kernel,
        grid=(planes,),
        in_specs=[plane, plane, IN_HBM, IN_VMEM],
        out_specs=[state_plane] + [whole(s) for s in edges],
        out_shape=[jax.ShapeDtypeStruct(s, f32) for s in [state.shape] + edges],
        scratch_shapes=[
            pltpu.VMEM((8 * count * slots // 256, 256), f32),
            pltpu.VMEM((count * slots // 128, 8, 128), f32),
            pltpu.VMEM(state.shape, f32),
            pltpu.SemaphoreType.DMA((planes,)),
        ],
        compiler_params=params(40 * 1024 * 1024),
        cost_estimate=pl.CostEstimate(flops=24 * 10**9, bytes_accessed=6 * 10**6, transcendentals=0),
        name="fill",
    )(source, mask, state, slot)


def body(
    cgrid_state, cgrid_metric, flap_state, flap_metric, iblank, fringe_from, donor_cell, donor_frac
):
    wrap_count = lax.axis_size("wrap")

    def ring(axis):
        size = lax.axis_size(axis)
        return [(i, (i + 1) % size) for i in range(size)]

    def onward(value, axis):
        return lax.ppermute(value, axis, ring(axis))

    def back(value, axis):
        return lax.ppermute(value, axis, [(j, i) for i, j in ring(axis)])

    slot, wrap_lo, wrap_hi, span_lo, span_hi, wall = donors(
        donor_cell[0], jnp.transpose(donor_frac[0], (1, 0, 2)), cgrid_state
    )
    far = lax.ppermute(
        wall,
        "wrap",
        [(i, wrap_count - 1 - i if wrapped(i, wrap_count) else i) for i in range(wrap_count)],
    )
    majors = (onward(span_hi, "span"), back(span_lo, "span"))
    subs = (onward(wrap_hi, "wrap"), back(wrap_lo, "wrap"))

    slot = lax.all_to_all(slot, "wrap", split_axis=0, concat_axis=0, tiled=True)

    turned = lambda x: jnp.swapaxes(x, -3, -2)
    mask = turned(iblank)
    filled, norm_lo, norm_hi, edge_lo, edge_hi = fill(turned(fringe_from), mask, turned(flap_state), slot)
    flap_majors = (onward(norm_hi, "wrap"), back(norm_lo, "wrap"))
    flap_subs = (onward(edge_hi, "span"), back(edge_lo, "span"))

    cgrid_rate = rate(
        cgrid_state,
        majors,
        subs,
        (wrap_lo, wrap_hi, wall, far),
        cgrid_metric,
        None,
        cgrid=True,
        step_planes=4,
        components=(3, 1, 2),
        metric_rows=(0, 1, 2),
    )
    flap_rate = rate(
        filled,
        flap_majors,
        flap_subs,
        (),
        turned(flap_metric),
        mask,
        cgrid=False,
        step_planes=3,
        components=(2, 3, 1),
        metric_rows=(1, 0, 2),
    )
    return (cgrid_rate, turned(flap_rate))


def solution(mesh):
    return jax.shard_map(
        body,
        mesh=mesh,
        in_specs=(
            P(None, "span", "wrap", None),
            P(None, "span", "wrap", None),
            P(None, "span", "wrap", None),
            P(None, "span", "wrap", None),
            P("span", "wrap", None),
            P("span", "wrap", None),
            P(("wrap", "span"), None, None),
            P(("wrap", "span"), None, None, None),
        ),
        out_specs=(P(None, "span", "wrap", None), P(None, "span", "wrap", None)),
        check_vma=False,
    )
```

```python
import functools

import jax
import jax.numpy as jnp
from jax import lax
from jax.experimental import pallas as pl
from jax.experimental.pallas import tpu as pltpu
from jax.sharding import PartitionSpec as P

viscosity = 0.05
conduction = 0.07
damping = 1.0 / 32.0
VMEM_LIMIT = 40 * 1024 * 1024
IN_HBM = pl.BlockSpec(memory_space=pltpu.HBM)
IN_VMEM = pl.BlockSpec(memory_space=pltpu.VMEM)
GROUP = 8

f32, bf16, i32 = jnp.float32, jnp.bfloat16, jnp.int32


def whole(shape):
    return pl.BlockSpec(shape, lambda *_: (0,) * len(shape))


def params(limit=VMEM_LIMIT):
    return pltpu.CompilerParams(vmem_limit_bytes=limit)


def primitives(q):
    inverse = 1.0 / q[0]
    v = [q[m] * inverse for m in (1, 2, 3)]
    kinetic = 0.5 * (v[0] * v[0] + v[1] * v[1] + v[2] * v[2])
    pressure = 0.4 * (q[4] - q[0] * kinetic)
    return v + [pressure, kinetic + (conduction / viscosity) * (pressure * inverse)]


def wrapped(place, count):
    return (place < count // 4) | (place >= count - count // 4)


def flux(q, prims, m):
    u = (0.5 / damping) * prims[m - 1]
    f = [q[0] * u]
    for c in (1, 2, 3):
        f.append(q[c] * u + (0.5 / damping) * prims[3] if c == m else q[c] * u)
    f.append((q[4] + prims[3]) * u)
    return f


def pack(q_ref, wrap_lo, wrap_hi, span_lo, span_hi, wall):
    spans, rows = q_ref.shape[1], q_ref.shape[2]
    lane = lax.broadcasted_iota(i32, (rows, 128), 1)
    for c in range(5):
        for l in range(2):
            span_lo[c, l] = q_ref[c, l]
            span_hi[c, l] = q_ref[c, spans - 2 + l]
        cells = jnp.zeros((rows, 128), f32)
        for k in range(spans):
            for l in range(2):
                wrap_lo[c, l, k : k + 1, :] = q_ref[c, k, l : l + 1, :]
                wrap_hi[c, l, k : k + 1, :] = q_ref[c, k, rows - 2 + l : rows - 1 + l, :]
            near = q_ref[c, k, :, 0:128]
            if k:
                near = pltpu.roll(near, 2 * k, 1)
            cells = jnp.where(lane // 2 == k, near, cells)
        wall[c] = cells[:, 0 : 2 * spans]


def rate_kernel(
    q_hbm,
    major_lo,
    major_hi,
    sub_lo,
    sub_hi,
    *refs,
    cgrid,
    step_planes,
    components,
    metric_rows,
):
    if cgrid:
        own_lo, own_hi, wall_own, wall_far, metric_ref, out_ref, qe, prim, sub_edge, lane_edge, mix, sems = refs
    else:
        own_lo = own_hi = None
        mask_ref, metric_ref, out_ref, qe, prim, sub_edge, sems = refs
    planes, rows, lanes = qe.shape[1] - 4, qe.shape[2], qe.shape[3]
    step = pl.program_id(0)
    place, count = lax.axis_index("wrap"), lax.axis_size("wrap")
    at_start = place == 0
    at_end = place == count - 1
    major_m, sub_m, lane_m = components

    def edge_fields(q1, q2, m, side):
        prims = primitives(q1)
        fl = flux(q1, prims, m)
        lead = [4.0 * q1[c] - side * fl[c] - q2[c] for c in range(5)]
        return lead + q1 + prims[:3] + prims[4:]

    def store_prims(k, slot):
        q = [qe[c, k] for c in range(5)]
        prims = primitives(q)
        for i, x in enumerate(prims + flux(q, prims, major_m)):
            prim[slot, i] = x

    steps = planes // step_planes

    def part(n):
        n = n * step_planes
        return pltpu.make_async_copy(
            q_hbm.at[:, pl.ds(n, step_planes)], qe.at[:, pl.ds(n + 2, step_planes)], sems.at[n // step_planes]
        )

    @pl.when(step == 0)
    def _():
        copies = [
            pltpu.make_async_copy(major_lo, qe.at[:, pl.ds(0, 2)], sems.at[steps]),
            pltpu.make_async_copy(major_hi, qe.at[:, pl.ds(planes + 2, 2)], sems.at[steps + 1]),
        ]
        copies[0].start()
        for n in range(steps):
            part(n).start()
        copies[1].start()
        for side, ref, own in ((-1, sub_lo, own_lo), (1, sub_hi, own_hi)):
            near, far = (1, 0) if side < 0 else (0, 1)
            q1 = [ref[c, near] for c in range(5)]
            q2 = [ref[c, far] for c in range(5)]
            if cgrid:
                edge = at_start if side < 0 else at_end
                clamp = 0 if side < 0 else 1
                q1 = [jnp.where(edge, own[c, clamp], q1[c]) for c in range(5)]
                q2 = [jnp.where(edge, own[c, clamp], q2[c]) for c in range(5)]
            for i, x in enumerate(edge_fields(q1, q2, sub_m, side)):
                sub_edge[(side + 1) // 2, i] = x
        if cgrid:
            in_wake = wrapped(place, count)
            turn = 7 - lax.broadcasted_iota(i32, (8, 128), 0)
            ghosts = []
            for c in range(5):
                sign = -1.0 if c in (1, 2, 3) else 1.0
                parts = []
                for r in range(rows // 8):
                    far = wall_far[c, rows - 8 - 8 * r : rows - 8 * r, :]
                    own = wall_own[c, 8 * r : 8 * r + 8, :]
                    own = jnp.concatenate([own, jnp.zeros((8, 128 - own.shape[1]), f32)], axis=1)
                    far = jnp.concatenate([far, jnp.zeros((8, 128 - far.shape[1]), f32)], axis=1)
                    far = jnp.take_along_axis(far, turn, axis=0, mode="promise_in_bounds")
                    parts.append(jnp.where(in_wake, far, sign * own))
                ghosts.append(jnp.concatenate(parts, axis=0))
            second = [pltpu.roll(x, 127, 1) for x in ghosts]
            fields = edge_fields(ghosts, second, lane_m, -1)
            even = lax.broadcasted_iota(i32, (rows, 128), 1) % 2 == 0
            for c in range(5):
                lane_edge[c] = jnp.where(even, fields[c], -pltpu.roll(ghosts[c], 1, 1))
            for i in range(4):
                lane_edge[5 + i] = jnp.where(even, fields[10 + i], 0.0)

            source = lax.broadcasted_iota(i32, (lanes, lanes), 0)
            target = lax.broadcasted_iota(i32, (lanes, lanes), 1)

            def band(*pairs):
                total = jnp.zeros((lanes, lanes), f32)
                for distance, factor in pairs:
                    hit = source == jnp.minimum(target + distance, lanes - 1)
                    total += jnp.where(hit, factor, 0.0)
                return total.astype(bf16)

            bands = [band((1, -1.0), (-1, 1.0))] * 2
            bands += [band((1, 4.0), (-1, 4.0), (2, -1.0), (-2, -1.0))] * 2
            bands += [band((1, 1.0), (-1, 1.0))] * 2
            for i, x in enumerate(bands):
                mix[i * lanes : (i + 1) * lanes, :] = x
        copies[0].wait()
        part(0).wait()
        part(1).wait()
        copies[1].wait()
        if not cgrid:

            @pl.when(at_start)
            def _():
                for c in range(5):
                    sign = -1.0 if c in (1, 2, 3) else 1.0
                    qe[c, 1] = sign * qe[c, 2]
                    qe[c, 0] = sign * qe[c, 3]

        store_prims(1, 0)
        store_prims(2, 1)

    @pl.when((step > 0) & (step < steps - 1))
    def _():
        part(step + 1).wait()

    if not cgrid:

        @pl.when((step == steps - 1) & at_end)
        def _():
            for c in range(5):
                qe[c, planes + 2] = qe[c, planes + 1]
                qe[c, planes + 3] = qe[c, planes + 1]

    row_at = lax.broadcasted_iota(i32, (8, lanes), 0)
    lane_at = lax.broadcasted_iota(i32, (rows, 128), 1)
    row_first, row_last = row_at == 0, row_at == 7
    lane_first, lane_last = lane_at == 0, lane_at == 127

    def one(b, _):
        k = step * step_planes + b
        here, below, above = lax.rem(k + 1, 3), lax.rem(k, 3), lax.rem(k + 2, 3)
        store_prims(k + 3, above)

        def sub_next(x, i):
            moved = [pltpu.roll(x[r : r + 8], 7, 0) for r in range(0, rows, 8)]
            moved.append(sub_edge[1, i, pl.ds(k, 1), :])
            return jnp.concatenate(
                [jnp.where(row_last, moved[r + 1], moved[r]) for r in range(rows // 8)], axis=0
            )

        def sub_prior(x, i):
            moved = [sub_edge[0, i, pl.ds(k, 1), :]]
            moved += [pltpu.roll(x[r : r + 8], 1, 0) for r in range(0, rows, 8)]
            return jnp.concatenate(
                [jnp.where(row_first, moved[r], moved[r + 1]) for r in range(rows // 8)], axis=0
            )

        def lane_next(x):
            moved = [pltpu.roll(x[:, t : t + 128], 127, 1) for t in range(0, lanes, 128)]
            moved.append(moved[0])
            return jnp.concatenate(
                [jnp.where(lane_last, moved[t + 1], moved[t]) for t in range(lanes // 128)], axis=1
            )

        def lane_prior(x):
            moved = [pltpu.roll(x[:, t : t + 128], 1, 1) for t in range(0, lanes, 128)]
            moved.insert(0, moved[-1])
            return jnp.concatenate(
                [jnp.where(lane_first, moved[t], moved[t + 1]) for t in range(lanes // 128)], axis=1
            )

        gm = metric_ref[metric_rows[0], b]
        gs = metric_ref[metric_rows[1], b]
        gl = metric_ref[metric_rows[2], b]
        gm2, gs2, gl2 = viscosity * gm * gm, viscosity * gs * gs, viscosity * gl * gl
        gm, gs, gl = damping * gm, damping * gs, damping * gl
        all2 = 2.0 * (gm2 + gs2 + gl2)
        all6 = 6.0 * (gm + gs + gl)
        mine = [prim[here, i] for i in range(5)]
        q = [qe[c, k + 2] for c in range(5)]
        lane_flux = flux(q, mine, lane_m)

        def lane_mixed(groups, mixer, edge):
            parts = [[part for x in group for part in split_two(x)] for group in groups]
            mixed = jnp.concatenate([jnp.concatenate(row, axis=1) for row in parts], axis=0)
            mixed = jnp.dot(mixed, mixer, preferred_element_type=f32)
            results = []
            for i in range(len(groups)):
                x = mixed[i * rows : (i + 1) * rows]
                ghost = pltpu.roll(lane_edge[edge + i], lax.rem(128 - 2 * k, 128), 1)
                results.append(
                    jnp.concatenate([x[:, 0:128] + jnp.where(lane_at < 2, ghost, 0.0), x[:, 128:]], axis=1)
                )
            return results

        if cgrid:
            lane_damped = lane_mixed([(lane_flux[c], q[c]) for c in range(5)], mix[0 : 4 * lanes, :], 0)
            lane_curved = lane_mixed([(mine[i],) for i in (0, 1, 2, 4)], mix[4 * lanes :, :], 5)
        viscous = {}
        for i, c, e in ((0, 1, 10), (1, 2, 11), (2, 3, 12), (4, 4, 13)):
            x = mine[i]
            total = gm2 * (prim[above, i] + prim[below, i])
            total += gs2 * (sub_next(x, e) + sub_prior(x, e))
            total += gl2 * (lane_curved[c - 1] if cgrid else lane_next(x) + lane_prior(x))
            viscous[c] = total - all2 * x
        sub_flux = flux(q, mine, sub_m)
        for c in range(5):
            x = q[c]
            four = 4.0 * x
            total = gm * (
                4.0 * (qe[c, k + 3] + qe[c, k + 1])
                - (qe[c, k + 4] + qe[c, k])
                - (prim[above, 5 + c] - prim[below, 5 + c])
            )
            up = four - sub_flux[c] - sub_next(x, 5 + c)
            down = four + sub_flux[c] - sub_prior(x, 5 + c)
            total += gs * (sub_next(up, c) + sub_prior(down, c))
            if cgrid:
                total += gl * lane_damped[c]
            else:
                up = four - lane_flux[c] - lane_next(x)
                down = four + lane_flux[c] - lane_prior(x)
                total += gl * (lane_next(up) + lane_prior(down))
            total -= all6 * x
            if c:
                total += viscous[c]
            if not cgrid:
                total = jnp.where(mask_ref[b] == 1, total, 0.0)
            out_ref[c, b] = total
        return 0

    lax.fori_loop(0, step_planes, one, 0)


def rate(q, majors, subs, extras, metric, mask, *, cgrid, step_planes, components, metric_rows):
    _, planes, rows, lanes = q.shape
    anywhere = pl.BlockSpec(memory_space=pl.ANY)
    block = lambda n: pl.BlockSpec((n, step_planes, rows, lanes), lambda i: (0, i, 0, 0))
    last_specs = [block(3)]
    last = (metric,)
    if mask is not None:
        last_specs = [pl.BlockSpec((step_planes, rows, lanes), lambda i: (i, 0, 0))] + last_specs
        last = (mask, metric)
    return pl.pallas_call(
        functools.partial(
            rate_kernel,
            cgrid=cgrid,
            step_planes=step_planes,
            components=components,
            metric_rows=metric_rows,
        ),
        grid=(planes // step_planes,),
        in_specs=[anywhere] + [IN_VMEM] * (4 + len(extras)) + last_specs,
        out_specs=block(5),
        out_shape=jax.ShapeDtypeStruct(q.shape, f32),
        scratch_shapes=[
            pltpu.VMEM((5, planes + 4, rows, lanes), f32),
            pltpu.VMEM((3, 10, rows, lanes), f32),
            pltpu.VMEM((2, 14, planes, lanes), f32),
        ]
        + [pltpu.VMEM((9, rows, 128), f32), pltpu.VMEM((6 * lanes, lanes), bf16)] * cgrid
        + [pltpu.SemaphoreType.DMA((planes // step_planes + 2,))],
        compiler_params=params(),
        cost_estimate=pl.CostEstimate(
            flops=300 * planes * rows * lanes, bytes_accessed=60 * planes * rows * lanes, transcendentals=0
        ),
        name="cgrid_rate" if cgrid else "flap_rate",
    )(q, *majors, *subs, *extras, *last)


def split_two(x):
    high = x.astype(bf16)
    return high, (x - high.astype(f32)).astype(bf16)


def lookup(both, at):
    width = at.shape[1]
    highs = 32
    components = both.shape[0] // (2 * highs)
    cells = lax.broadcasted_iota(i32, (256, width), 0).astype(f32).astype(bf16)
    sub = lax.broadcasted_iota(i32, (8, width), 0)
    pick = jnp.where(
        cells == (at & 255).astype(f32).astype(bf16), jnp.ones((), bf16), jnp.zeros((), bf16)
    )
    high = at // 256
    found = jnp.dot(both, pick, preferred_element_type=f32)
    masks = [sub + 8 * g == high for g in range(highs // 8)]
    values = []
    for c in range(components):
        value = None
        for g, mask in enumerate(masks):
            r = c * highs + 8 * g
            remainder = components * highs + r
            piece = found[r : r + 8] + found[remainder : remainder + 8]
            value = jnp.where(mask, piece, 0.0 if value is None else value)
        values.append(jnp.sum(value, axis=0, keepdims=True))
    return values


def take_lanes(values, lanes):
    return lax.gather(
        values,
        lanes[..., None],
        lax.GatherDimensionNumbers(
            offset_dims=(),
            collapsed_slice_dims=(1,),
            start_index_map=(1,),
            operand_batching_dims=(0,),
            start_indices_batching_dims=(0,),
        ),
        slice_sizes=(1, 1),
        mode=lax.GatherScatterMode.PROMISE_IN_BOUNDS,
    )


def add_remainders(table):
    half = table.shape[0] // 2
    for r in range(0, half, 8):
        value = table[r : r + 8, :]
        table[half + r : half + r + 8, :] = value - value.astype(bf16).astype(f32)


def donor_kernel(
    cell_ref,
    frac_ref,
    q_hbm,
    out_ref,
    wrap_lo,
    wrap_hi,
    span_lo,
    span_hi,
    wall,
    q_ref,
    planes,
    pieces,
    rank_ref,
    ordered,
    where_ref,
    first,
    partial,
    table,
    sems,
):
    spans, rows, lanes = q_ref.shape[1:]
    count, slots = cell_ref.shape
    tile = 256
    tiles = count * slots // tile
    wide = slots // 128
    one, zero = jnp.ones((), bf16), jnp.zeros((), bf16)
    fetch = pltpu.make_async_copy(q_hbm, q_ref, sems.at[0])
    fetch.start()

    cell = cell_ref[...]
    upper = jnp.floor((cell.astype(f32) + 0.5) * (1.0 / (lanes - 1)))
    span = jnp.floor((upper + 0.5) * (1.0 / (rows - 1)))
    pieces[0] = span
    pieces[1] = upper - span * (rows - 1)
    pieces[2] = cell.astype(f32) - upper * (lanes - 1)
    for d in range(3):
        f = frac_ref[d]
        high = f.astype(bf16).astype(f32)
        pieces[3 + 2 * d] = high
        pieces[4 + 2 * d] = f - high

    lines = jnp.concatenate([span[:, 128 * t : 128 * t + 128] for t in range(wide)], axis=0)
    depth = lines.shape[0]
    hits = [jnp.where(lines == b, 1.0, 0.0).astype(bf16) for b in range(spans)]
    into = lax.broadcasted_iota(i32, (128, 256), 0)
    onto = lax.broadcasted_iota(i32, (128, 256), 1)
    before = jnp.where((into < onto) | (onto >= 128), 1.0, 0.0).astype(bf16)
    inside = jnp.dot(jnp.concatenate(hits, axis=0), before, preferred_element_type=f32)
    sums = [inside[b * depth : (b + 1) * depth, 128:256] for b in range(spans)]
    lower = lax.broadcasted_iota(i32, (depth, depth), 1) < lax.broadcasted_iota(i32, (depth, depth), 0)
    above = jnp.dot(
        jnp.where(lower, 1.0, 0.0).astype(bf16),
        jnp.concatenate([x.astype(bf16) for x in sums], axis=1),
        preferred_element_type=f32,
    )
    start = jnp.zeros((1, 128), f32)
    rank = jnp.zeros((depth, 128), f32)
    for b in range(spans):
        over = above[:, b * 128 : (b + 1) * 128]
        rank = jnp.where(lines == b, inside[b * depth : (b + 1) * depth, 0:128] + over + start, rank)
        start = start + over[depth - 1 :] + sums[b][depth - 1 :]
    rank = rank.astype(i32)
    for t in range(wide):
        rank_ref[:, 128 * t : 128 * t + 128] = rank[8 * t : 8 * t + 8]

    tile_at = lax.broadcasted_iota(i32, (tiles, slots), 0).astype(f32).astype(bf16)
    place_at = lax.broadcasted_iota(i32, (tile, slots), 0).astype(f32).astype(bf16)
    ordered[...] = jnp.zeros_like(ordered)

    def order(w, _):
        to = rank_ref[pl.ds(w, 1), :]
        in_tile = jnp.where(tile_at == (to // tile).astype(f32).astype(bf16), one, zero)
        at_place = jnp.where(place_at == (to & (tile - 1)).astype(f32).astype(bf16), one, zero)
        parts = [in_tile * pieces[p, pl.ds(w, 1), :].astype(bf16) for p in range(9)]
        ordered[...] += lax.dot_general(
            jnp.concatenate(parts, axis=0),
            at_place,
            (((1,), (1,)), ((), ())),
            preferred_element_type=f32,
        )
        return 0

    lax.fori_loop(0, count, order, 0, unroll=4)
    where_ref[...] = ordered[0:tiles, :].astype(i32)
    copy = pltpu.make_async_copy(where_ref, first, sems.at[1])
    copy.start()

    fetch.wait()
    pack(q_ref, wrap_lo, wrap_hi, span_lo, span_hi, wall)

    def prepare(k, _):
        for c in range(5):
            high, low = split_two(q_ref[c, k])
            here = pl.ds(pl.multiple_of(k * 5 * rows + c * rows, 16), rows)
            planes[here, 0:lanes] = high
            planes[here, lanes : 2 * lanes] = low
            planes[here, 2 * lanes : 3 * lanes] = high
        return 0

    lax.fori_loop(0, spans, prepare, 0)
    copy.wait()

    def weights(cells, at, frac):
        here = lax.broadcasted_iota(i32, (cells, tile), 0)
        return jnp.where(here == at, 1.0 - frac, jnp.where(here == at + 1, frac, 0.0))

    def tile_of(i):
        def piece(p):
            return ordered[pl.ds(p * tiles + i, 1), :]

        span, wrap, normal = piece(0).astype(i32), piece(1).astype(i32), piece(2).astype(i32)
        f0, f1, f2 = [piece(3 + 2 * d) + piece(4 + 2 * d) for d in range(3)]
        cells = lax.broadcasted_iota(i32, (lanes, tile), 0).astype(f32).astype(bf16)
        at_lower, at_upper = [cells == (normal + n).astype(f32).astype(bf16) for n in range(2)]
        (lower_high, lower_low), (upper_high, upper_low) = split_two(1.0 - f2), split_two(f2)
        high = jnp.where(at_lower, lower_high, jnp.where(at_upper, upper_high, zero))
        low = jnp.where(at_lower, lower_low, jnp.where(at_upper, upper_low, zero))
        return span, f0, jnp.concatenate([high, high, low], axis=0), weights(rows, wrap, f1)

    def add_planes(k, number, made, sums):
        span, f0, along, across = made
        from_row = pl.ds(pl.multiple_of(k * 5 * rows, 16), number * 5 * rows)
        mixed = jnp.dot(planes[from_row, :], along, preferred_element_type=f32)
        new = list(sums)
        for n in range(number):
            ws = jnp.where(span == k + n, 1.0 - f0, jnp.where(span + 1 == k + n, f0, 0.0))
            for c in range(5):
                r0 = (5 * n + c) * rows
                total = mixed[r0 : r0 + 8] * across[0:8]
                for r in range(8, rows, 8):
                    total += mixed[r0 + r : r0 + r + 8] * across[r : r + 8]
                new[c] = ws * total if new[c] is None else new[c] + ws * total
        return tuple(new)

    def lowest_of(i):
        return jnp.minimum(first[i, 0], spans - 3)

    def step(g, _):
        for n in range(GROUP):
            i = g * GROUP + n
            for c, x in enumerate(add_planes(lowest_of(i), 3, tile_of(i), (None,) * 5)):
                partial[n, c] = x
        for n in range(GROUP):
            i = g * GROUP + n
            lowest = lowest_of(i)
            more = first[i, tile - 1] - 1 - lowest

            @pl.when(more > 0)
            def _():
                made = tile_of(i)

                def again(m, _):
                    sums = add_planes(lowest + 3 + m, 1, made, tuple(partial[n, c] for c in range(5)))
                    for c in range(5):
                        partial[n, c] = sums[c]
                    return 0

                lax.fori_loop(0, more, again, 0)

        for n in range(GROUP):
            i = g * GROUP + n
            for c in range(5):
                table[pl.ds(c * tiles + i, 1), :] = jnp.sum(partial[n, c], axis=0, keepdims=True)
        return 0

    lax.fori_loop(0, tiles // GROUP, step, 0)

    add_remainders(table)
    both = table[...].astype(bf16)

    def put_back(w, _):
        for t in range(0, slots, 512):
            for c, value in enumerate(lookup(both, rank_ref[pl.ds(w, 1), t : t + 512])):
                out_ref[w, c : c + 1, t : t + 512] = value
        return 0

    lax.fori_loop(0, count, put_back, 0, unroll=8)


def donors(cell, frac, state):
    _, spans, rows, lanes = state.shape
    count, slots = cell.shape
    tiles = count * slots // 256
    shapes = [(count, 5, slots)]
    shapes += [(5, 2, spans, lanes)] * 2 + [(5, 2, rows, lanes)] * 2 + [(5, rows, 2 * spans)]
    return pl.pallas_call(
        donor_kernel,
        grid=(1,),
        in_specs=[IN_VMEM, IN_VMEM, IN_HBM],
        out_specs=[whole(x) for x in shapes],
        out_shape=[jax.ShapeDtypeStruct(x, f32) for x in shapes],
        scratch_shapes=[
            pltpu.VMEM(state.shape, f32),
            pltpu.VMEM((spans * 5 * rows, 3 * lanes), bf16),
            pltpu.VMEM((9, count, slots), f32),
            pltpu.VMEM((count, slots), i32),
            pltpu.VMEM((9 * tiles, 256), f32),
            pltpu.VMEM((tiles, 256), i32),
            pltpu.SMEM((tiles, 256), i32),
            pltpu.VMEM((GROUP, 5, 8, 256), f32),
            pltpu.VMEM((10 * tiles, 256), f32),
            pltpu.SemaphoreType.DMA((2,)),
        ],
        compiler_params=params(60 * 1024 * 1024),
        name="donors",
    )(cell, frac, state)


def fill_kernel(
    from_ref,
    mask_ref,
    q_hbm,
    slot_ref,
    out_ref,
    norm_lo,
    norm_hi,
    span_lo,
    span_hi,
    table,
    spread,
    q_ref,
    sems,
):
    planes = pl.num_programs(0)
    rows, lanes = from_ref.shape[1:]
    count, _, slots = slot_ref.shape
    j = pl.program_id(0)

    def fetch(n):
        return pltpu.make_async_copy(q_hbm.at[:, n], q_ref.at[:, n], sems.at[n])

    @pl.when(j == 0)
    def _():
        for n in range(q_ref.shape[1]):
            fetch(n).start()
        per = slots // 256
        for c in range(4):
            for w in range(count):
                for r in range(per):
                    at = c * count * per + w * per + r
                    table[at : at + 1, :] = slot_ref[w, c : c + 1, r * 256 : (r + 1) * 256]
        add_remainders(table)
        for w in range(count):
            for r in range(slots // 128):
                value = slot_ref[w, 4:5, r * 128 : (r + 1) * 128]
                spread[w * (slots // 128) + r] = jnp.broadcast_to(value, (8, 128))

    fetch(j).wait()
    both = table[...].astype(bf16)
    lines = spread.shape[0]
    share = (rows // 8) * (lanes // 128) * lines // rows
    value = None
    for s in range(rows):
        keep = mask_ref[0, s : s + 1, :] == 1
        for c, found in enumerate(lookup(both, from_ref[0, s : s + 1, :])):
            out_ref[c, 0, s : s + 1, :] = jnp.where(keep, q_ref[c, j, s : s + 1, :], found)
        for n in range(s * share, (s + 1) * share):
            line = n % lines
            if line == 0:
                row, lane = divmod(n // lines, lanes // 128)
                here = (slice(8 * row, 8 * row + 8), slice(128 * lane, 128 * lane + 128))
                at = from_ref[0, here[0], here[1]]
                low, high = at & 127, at // 128
                value = jnp.zeros((8, 128), f32)
            value = jnp.where(high == line, take_lanes(spread[line], low), value)
            if line == lines - 1:
                keep = mask_ref[0, here[0], here[1]] == 1
                out_ref[4, 0, here[0], here[1]] = jnp.where(keep, q_ref[4, j, here[0], here[1]], value)

    for c in range(5):
        for l in range(2):
            span_lo[c, l, pl.ds(j, 1), :] = out_ref[c, 0, l : l + 1, :]
            span_hi[c, l, pl.ds(j, 1), :] = out_ref[c, 0, rows - 2 + l : rows - 1 + l, :]

    @pl.when(j < 2)
    def _():
        for c in range(5):
            norm_lo[c, j] = out_ref[c, 0]

    @pl.when(j >= planes - 2)
    def _():
        for c in range(5):
            norm_hi[c, j - (planes - 2)] = out_ref[c, 0]


def fill(source, mask, state, slot):
    _, planes, rows, lanes = state.shape
    count, _, slots = slot.shape
    plane = pl.BlockSpec((1, rows, lanes), lambda j: (j, 0, 0))
    state_plane = pl.BlockSpec((5, 1, rows, lanes), lambda j: (0, j, 0, 0))
    edges = [(5, 2, rows, lanes)] * 2 + [(5, 2, planes, lanes)] * 2
    return pl.pallas_call(
        fill_kernel,
        grid=(planes,),
        in_specs=[plane, plane, IN_HBM, IN_VMEM],
        out_specs=[state_plane] + [whole(s) for s in edges],
        out_shape=[jax.ShapeDtypeStruct(s, f32) for s in [state.shape] + edges],
        scratch_shapes=[
            pltpu.VMEM((8 * count * slots // 256, 256), f32),
            pltpu.VMEM((count * slots // 128, 8, 128), f32),
            pltpu.VMEM(state.shape, f32),
            pltpu.SemaphoreType.DMA((planes,)),
        ],
        compiler_params=params(49 * 1024 * 1024),
        cost_estimate=pl.CostEstimate(flops=24 * 10**9, bytes_accessed=6 * 10**6, transcendentals=0),
        name="fill",
    )(source, mask, state, slot)


def body(
    cgrid_state, cgrid_metric, flap_state, flap_metric, iblank, fringe_from, donor_cell, donor_frac
):
    wrap_count = lax.axis_size("wrap")

    def ring(axis):
        size = lax.axis_size(axis)
        return [(i, (i + 1) % size) for i in range(size)]

    def onward(value, axis):
        return lax.ppermute(value, axis, ring(axis))

    def back(value, axis):
        return lax.ppermute(value, axis, [(j, i) for i, j in ring(axis)])

    slot, wrap_lo, wrap_hi, span_lo, span_hi, wall = donors(
        donor_cell[0], jnp.transpose(donor_frac[0], (1, 0, 2)), cgrid_state
    )
    far = lax.ppermute(
        wall,
        "wrap",
        [(i, wrap_count - 1 - i if wrapped(i, wrap_count) else i) for i in range(wrap_count)],
    )
    majors = (onward(span_hi, "span"), back(span_lo, "span"))
    subs = (onward(wrap_hi, "wrap"), back(wrap_lo, "wrap"))

    slot = lax.all_to_all(slot, "wrap", split_axis=0, concat_axis=0, tiled=True)

    turned = lambda x: jnp.swapaxes(x, -3, -2)
    mask = turned(iblank)
    filled, norm_lo, norm_hi, edge_lo, edge_hi = fill(turned(fringe_from), mask, turned(flap_state), slot)
    flap_majors = (onward(norm_hi, "wrap"), back(norm_lo, "wrap"))
    flap_subs = (onward(edge_hi, "span"), back(edge_lo, "span"))

    cgrid_rate = rate(
        cgrid_state,
        majors,
        subs,
        (wrap_lo, wrap_hi, wall, far),
        cgrid_metric,
        None,
        cgrid=True,
        step_planes=4,
        components=(3, 1, 2),
        metric_rows=(0, 1, 2),
    )
    flap_rate = rate(
        filled,
        flap_majors,
        flap_subs,
        (),
        turned(flap_metric),
        mask,
        cgrid=False,
        step_planes=3,
        components=(2, 3, 1),
        metric_rows=(1, 0, 2),
    )
    return (cgrid_rate, turned(flap_rate))


def solution(mesh):
    return jax.shard_map(
        body,
        mesh=mesh,
        in_specs=(
            P(None, "span", "wrap", None),
            P(None, "span", "wrap", None),
            P(None, "span", "wrap", None),
            P(None, "span", "wrap", None),
            P("span", "wrap", None),
            P("span", "wrap", None),
            P(("wrap", "span"), None, None),
            P(("wrap", "span"), None, None, None),
        ),
        out_specs=(P(None, "span", "wrap", None), P(None, "span", "wrap", None)),
        check_vma=False,
    )
```

```python
import functools

import jax
import jax.numpy as jnp
from jax import lax
from jax.experimental import pallas as pl
from jax.experimental.pallas import tpu as pltpu
from jax.sharding import PartitionSpec as P

viscosity = 0.05
conduction = 0.07
damping = 1.0 / 32.0
VMEM_LIMIT = 40 * 1024 * 1024
IN_HBM = pl.BlockSpec(memory_space=pltpu.HBM)
IN_VMEM = pl.BlockSpec(memory_space=pltpu.VMEM)
GROUP = 8

f32, bf16, i32 = jnp.float32, jnp.bfloat16, jnp.int32


def whole(shape):
    return pl.BlockSpec(shape, lambda *_: (0,) * len(shape))


def params(limit=VMEM_LIMIT):
    return pltpu.CompilerParams(vmem_limit_bytes=limit)


def primitives(q):
    inverse = 1.0 / q[0]
    v = [q[m] * inverse for m in (1, 2, 3)]
    kinetic = 0.5 * (v[0] * v[0] + v[1] * v[1] + v[2] * v[2])
    pressure = 0.4 * (q[4] - q[0] * kinetic)
    return v + [pressure, kinetic + (conduction / viscosity) * (pressure * inverse)]


def wrapped(place, count):
    return (place < count // 4) | (place >= count - count // 4)


def flux(q, prims, m):
    u = (0.5 / damping) * prims[m - 1]
    f = [q[0] * u]
    for c in (1, 2, 3):
        f.append(q[c] * u + (0.5 / damping) * prims[3] if c == m else q[c] * u)
    f.append((q[4] + prims[3]) * u)
    return f


def pack(q_ref, wrap_lo, wrap_hi, span_lo, span_hi, wall):
    spans, rows = q_ref.shape[1], q_ref.shape[2]
    lane = lax.broadcasted_iota(i32, (rows, 128), 1)
    for c in range(5):
        for l in range(2):
            span_lo[c, l] = q_ref[c, l]
            span_hi[c, l] = q_ref[c, spans - 2 + l]
        cells = jnp.zeros((rows, 128), f32)
        for k in range(spans):
            for l in range(2):
                wrap_lo[c, l, k : k + 1, :] = q_ref[c, k, l : l + 1, :]
                wrap_hi[c, l, k : k + 1, :] = q_ref[c, k, rows - 2 + l : rows - 1 + l, :]
            near = q_ref[c, k, :, 0:128]
            if k:
                near = pltpu.roll(near, 2 * k, 1)
            cells = jnp.where(lane // 2 == k, near, cells)
        wall[c] = cells[:, 0 : 2 * spans]


def rate_kernel(
    q_hbm,
    major_lo,
    major_hi,
    sub_lo,
    sub_hi,
    *refs,
    cgrid,
    step_planes,
    components,
    metric_rows,
):
    if cgrid:
        own_lo, own_hi, wall_own, wall_far, metric_ref, out_ref, qe, prim, sub_edge, lane_edge, mix, sems = refs
    else:
        own_lo = own_hi = None
        mask_ref, metric_ref, out_ref, qe, prim, sub_edge, mix, sems = refs
    planes, rows, lanes = qe.shape[1] - 4, qe.shape[2], qe.shape[3]
    step = pl.program_id(0)
    place, count = lax.axis_index("wrap"), lax.axis_size("wrap")
    at_start = place == 0
    at_end = place == count - 1
    major_m, sub_m, lane_m = components
    width = mix.shape[1]

    def edge_fields(q1, q2, m, side):
        prims = primitives(q1)
        fl = flux(q1, prims, m)
        lead = [4.0 * q1[c] - side * fl[c] - q2[c] for c in range(5)]
        return lead + q1 + prims[:3] + prims[4:]

    def store_prims(k, slot):
        q = [qe[c, k] for c in range(5)]
        prims = primitives(q)
        for i, x in enumerate(prims + flux(q, prims, major_m)):
            prim[slot, i] = x

    steps = planes // step_planes

    def part(n):
        n = n * step_planes
        return pltpu.make_async_copy(
            q_hbm.at[:, pl.ds(n, step_planes)], qe.at[:, pl.ds(n + 2, step_planes)], sems.at[n // step_planes]
        )

    @pl.when(step == 0)
    def _():
        copies = [
            pltpu.make_async_copy(major_lo, qe.at[:, pl.ds(0, 2)], sems.at[steps]),
            pltpu.make_async_copy(major_hi, qe.at[:, pl.ds(planes + 2, 2)], sems.at[steps + 1]),
        ]
        copies[0].start()
        for n in range(steps):
            part(n).start()
        copies[1].start()
        for side, ref, own in ((-1, sub_lo, own_lo), (1, sub_hi, own_hi)):
            near, far = (1, 0) if side < 0 else (0, 1)
            q1 = [ref[c, near] for c in range(5)]
            q2 = [ref[c, far] for c in range(5)]
            if cgrid:
                edge = at_start if side < 0 else at_end
                clamp = 0 if side < 0 else 1
                q1 = [jnp.where(edge, own[c, clamp], q1[c]) for c in range(5)]
                q2 = [jnp.where(edge, own[c, clamp], q2[c]) for c in range(5)]
            for i, x in enumerate(edge_fields(q1, q2, sub_m, side)):
                sub_edge[(side + 1) // 2, i] = x
        if cgrid:
            in_wake = wrapped(place, count)
            turn = 7 - lax.broadcasted_iota(i32, (8, 128), 0)
            ghosts = []
            for c in range(5):
                sign = -1.0 if c in (1, 2, 3) else 1.0
                parts = []
                for r in range(rows // 8):
                    far = wall_far[c, rows - 8 - 8 * r : rows - 8 * r, :]
                    own = wall_own[c, 8 * r : 8 * r + 8, :]
                    own = jnp.concatenate([own, jnp.zeros((8, 128 - own.shape[1]), f32)], axis=1)
                    far = jnp.concatenate([far, jnp.zeros((8, 128 - far.shape[1]), f32)], axis=1)
                    far = jnp.take_along_axis(far, turn, axis=0, mode="promise_in_bounds")
                    parts.append(jnp.where(in_wake, far, sign * own))
                ghosts.append(jnp.concatenate(parts, axis=0))
            second = [pltpu.roll(x, 127, 1) for x in ghosts]
            fields = edge_fields(ghosts, second, lane_m, -1)
            even = lax.broadcasted_iota(i32, (rows, 128), 1) % 2 == 0
            for c in range(5):
                lane_edge[c] = jnp.where(even, fields[c], -pltpu.roll(ghosts[c], 1, 1))
            for i in range(4):
                lane_edge[5 + i] = jnp.where(even, fields[10 + i], 0.0)

        source = lax.broadcasted_iota(i32, (lanes, width), 0)
        target = lax.broadcasted_iota(i32, (lanes, width), 1)
        apart = source - target
        apart = jnp.where(apart > lanes - 3, apart - lanes, apart)

        def band(*pairs):
            total = jnp.zeros((lanes, width), f32)
            for distance, factor in pairs:
                if cgrid:
                    total += jnp.where(source == jnp.minimum(target + distance, lanes - 1), factor, 0.0)
                else:
                    total = jnp.where(apart == distance, factor, total)
            return total.astype(bf16)

        bands = [band((1, -1.0), (-1, 1.0))] * 2
        bands += [band((1, 4.0), (-1, 4.0), (2, -1.0), (-2, -1.0))] * 2
        bands += [band((1, 1.0), (-1, 1.0))] * 2
        for i, x in enumerate(bands):
            mix[i * lanes : (i + 1) * lanes, :] = x

        copies[0].wait()
        part(0).wait()
        part(1).wait()
        copies[1].wait()
        if not cgrid:

            @pl.when(at_start)
            def _():
                for c in range(5):
                    sign = -1.0 if c in (1, 2, 3) else 1.0
                    qe[c, 1] = sign * qe[c, 2]
                    qe[c, 0] = sign * qe[c, 3]

        store_prims(1, 0)
        store_prims(2, 1)

    @pl.when((step > 0) & (step < steps - 1))
    def _():
        part(step + 1).wait()

    if not cgrid:

        @pl.when((step == steps - 1) & at_end)
        def _():
            for c in range(5):
                qe[c, planes + 2] = qe[c, planes + 1]
                qe[c, planes + 3] = qe[c, planes + 1]

    row_at = lax.broadcasted_iota(i32, (8, lanes), 0)
    lane_at = lax.broadcasted_iota(i32, (rows, 128), 1)
    row_first, row_last = row_at == 0, row_at == 7

    def one(b, _):
        k = step * step_planes + b
        here, below, above = lax.rem(k + 1, 3), lax.rem(k, 3), lax.rem(k + 2, 3)
        store_prims(k + 3, above)

        def sub_next(x, i):
            moved = [pltpu.roll(x[r : r + 8], 7, 0) for r in range(0, rows, 8)]
            moved.append(sub_edge[1, i, pl.ds(k, 1), :])
            return jnp.concatenate(
                [jnp.where(row_last, moved[r + 1], moved[r]) for r in range(rows // 8)], axis=0
            )

        def sub_prior(x, i):
            moved = [sub_edge[0, i, pl.ds(k, 1), :]]
            moved += [pltpu.roll(x[r : r + 8], 1, 0) for r in range(0, rows, 8)]
            return jnp.concatenate(
                [jnp.where(row_first, moved[r], moved[r + 1]) for r in range(rows // 8)], axis=0
            )

        gm = metric_ref[metric_rows[0], b]
        gs = metric_ref[metric_rows[1], b]
        gl = metric_ref[metric_rows[2], b]
        gm2, gs2, gl2 = viscosity * gm * gm, viscosity * gs * gs, viscosity * gl * gl
        gm, gs, gl = damping * gm, damping * gs, damping * gl
        all2 = 2.0 * (gm2 + gs2 + gl2)
        all6 = 6.0 * (gm + gs + gl)
        mine = [prim[here, i] for i in range(5)]
        q = [qe[c, k + 2] for c in range(5)]
        lane_flux = flux(q, mine, lane_m)

        def lane_mixed(groups, mixer, edge):
            parts = [[part for x in group for part in split_two(x)] for group in groups]
            lines = []
            for t in range(0, lanes, width):
                for row in parts:
                    turned = [jnp.concatenate([x[:, t:], x[:, :t]], axis=1) if t else x for x in row]
                    lines.append(jnp.concatenate(turned, axis=1))
            mixed = jnp.dot(jnp.concatenate(lines, axis=0), mixer, preferred_element_type=f32)
            results = []
            for i in range(len(groups)):
                at = [(i + n * len(groups)) * rows for n in range(lanes // width)]
                x = jnp.concatenate([mixed[r : r + rows] for r in at], axis=1)
                if cgrid:
                    ghost = pltpu.roll(lane_edge[edge + i], lax.rem(128 - 2 * k, 128), 1)
                    ghost = jnp.where(lane_at < 2, ghost, 0.0)
                    x = jnp.concatenate([x[:, 0:128] + ghost, x[:, 128:]], axis=1)
                results.append(x)
            return results

        lane_damped = lane_mixed([(lane_flux[c], q[c]) for c in range(5)], mix[0 : 4 * lanes, :], 0)
        lane_curved = lane_mixed([(mine[i],) for i in (0, 1, 2, 4)], mix[4 * lanes :, :], 5)
        viscous = {}
        for i, c, e in ((0, 1, 10), (1, 2, 11), (2, 3, 12), (4, 4, 13)):
            x = mine[i]
            total = gm2 * (prim[above, i] + prim[below, i])
            total += gs2 * (sub_next(x, e) + sub_prior(x, e))
            total += gl2 * lane_curved[c - 1]
            viscous[c] = total - all2 * x
        sub_flux = flux(q, mine, sub_m)
        for c in range(5):
            x = q[c]
            four = 4.0 * x
            total = gm * (
                4.0 * (qe[c, k + 3] + qe[c, k + 1])
                - (qe[c, k + 4] + qe[c, k])
                - (prim[above, 5 + c] - prim[below, 5 + c])
            )
            up = four - sub_flux[c] - sub_next(x, 5 + c)
            down = four + sub_flux[c] - sub_prior(x, 5 + c)
            total += gs * (sub_next(up, c) + sub_prior(down, c))
            total += gl * lane_damped[c]
            total -= all6 * x
            if c:
                total += viscous[c]
            if not cgrid:
                total = jnp.where(mask_ref[b] == 1, total, 0.0)
            out_ref[c, b] = total
        return 0

    lax.fori_loop(0, step_planes, one, 0)


def rate(q, majors, subs, extras, metric, mask, *, cgrid, step_planes, components, metric_rows):
    _, planes, rows, lanes = q.shape
    anywhere = pl.BlockSpec(memory_space=pl.ANY)
    block = lambda n: pl.BlockSpec((n, step_planes, rows, lanes), lambda i: (0, i, 0, 0))
    last_specs = [block(3)]
    last = (metric,)
    if mask is not None:
        last_specs = [pl.BlockSpec((step_planes, rows, lanes), lambda i: (i, 0, 0))] + last_specs
        last = (mask, metric)
    return pl.pallas_call(
        functools.partial(
            rate_kernel,
            cgrid=cgrid,
            step_planes=step_planes,
            components=components,
            metric_rows=metric_rows,
        ),
        grid=(planes // step_planes,),
        in_specs=[anywhere] + [IN_VMEM] * (4 + len(extras)) + last_specs,
        out_specs=block(5),
        out_shape=jax.ShapeDtypeStruct(q.shape, f32),
        scratch_shapes=[
            pltpu.VMEM((5, planes + 4, rows, lanes), f32),
            pltpu.VMEM((3, 10, rows, lanes), f32),
            pltpu.VMEM((2, 14, planes, lanes), f32),
        ]
        + [pltpu.VMEM((9, rows, 128), f32)] * cgrid
        + [pltpu.VMEM((6 * lanes, 256), bf16)]
        + [pltpu.SemaphoreType.DMA((planes // step_planes + 2,))],
        compiler_params=params(),
        cost_estimate=pl.CostEstimate(
            flops=300 * planes * rows * lanes, bytes_accessed=60 * planes * rows * lanes, transcendentals=0
        ),
        name="cgrid_rate" if cgrid else "flap_rate",
    )(q, *majors, *subs, *extras, *last)


def split_two(x):
    high = x.astype(bf16)
    return high, (x - high.astype(f32)).astype(bf16)


def lookup(both, at):
    width = at.shape[1]
    highs = 32
    components = both.shape[0] // (2 * highs)
    cells = lax.broadcasted_iota(i32, (256, width), 0).astype(f32).astype(bf16)
    sub = lax.broadcasted_iota(i32, (8, width), 0)
    pick = jnp.where(
        cells == (at & 255).astype(f32).astype(bf16), jnp.ones((), bf16), jnp.zeros((), bf16)
    )
    high = at // 256
    found = jnp.dot(both, pick, preferred_element_type=f32)
    masks = [sub + 8 * g == high for g in range(highs // 8)]
    values = []
    for c in range(components):
        value = None
        for g, mask in enumerate(masks):
            r = c * highs + 8 * g
            remainder = components * highs + r
            piece = found[r : r + 8] + found[remainder : remainder + 8]
            value = jnp.where(mask, piece, 0.0 if value is None else value)
        values.append(jnp.sum(value, axis=0, keepdims=True))
    return values


def take_lanes(values, lanes):
    return lax.gather(
        values,
        lanes[..., None],
        lax.GatherDimensionNumbers(
            offset_dims=(),
            collapsed_slice_dims=(1,),
            start_index_map=(1,),
            operand_batching_dims=(0,),
            start_indices_batching_dims=(0,),
        ),
        slice_sizes=(1, 1),
        mode=lax.GatherScatterMode.PROMISE_IN_BOUNDS,
    )


def add_remainders(table):
    half = table.shape[0] // 2
    for r in range(0, half, 8):
        value = table[r : r + 8, :]
        table[half + r : half + r + 8, :] = value - value.astype(bf16).astype(f32)


def donor_kernel(
    cell_ref,
    frac_ref,
    q_hbm,
    out_ref,
    wrap_lo,
    wrap_hi,
    span_lo,
    span_hi,
    wall,
    q_ref,
    planes,
    pieces,
    rank_ref,
    ordered,
    where_ref,
    first,
    partial,
    table,
    sems,
):
    spans, rows, lanes = q_ref.shape[1:]
    count, slots = cell_ref.shape
    tile = 256
    tiles = count * slots // tile
    wide = slots // 128
    one, zero = jnp.ones((), bf16), jnp.zeros((), bf16)
    fetch = pltpu.make_async_copy(q_hbm, q_ref, sems.at[0])
    fetch.start()

    cell = cell_ref[...]
    upper = jnp.floor((cell.astype(f32) + 0.5) * (1.0 / (lanes - 1)))
    span = jnp.floor((upper + 0.5) * (1.0 / (rows - 1)))
    pieces[0] = span
    pieces[1] = upper - span * (rows - 1)
    pieces[2] = cell.astype(f32) - upper * (lanes - 1)
    for d in range(3):
        f = frac_ref[d]
        high = f.astype(bf16).astype(f32)
        pieces[3 + 2 * d] = high
        pieces[4 + 2 * d] = f - high

    lines = jnp.concatenate([span[:, 128 * t : 128 * t + 128] for t in range(wide)], axis=0)
    depth = lines.shape[0]
    hits = [jnp.where(lines == b, 1.0, 0.0).astype(bf16) for b in range(spans)]
    into = lax.broadcasted_iota(i32, (128, 256), 0)
    onto = lax.broadcasted_iota(i32, (128, 256), 1)
    before = jnp.where((into < onto) | (onto >= 128), 1.0, 0.0).astype(bf16)
    inside = jnp.dot(jnp.concatenate(hits, axis=0), before, preferred_element_type=f32)
    sums = [inside[b * depth : (b + 1) * depth, 128:256] for b in range(spans)]
    lower = lax.broadcasted_iota(i32, (depth, depth), 1) < lax.broadcasted_iota(i32, (depth, depth), 0)
    above = jnp.dot(
        jnp.where(lower, 1.0, 0.0).astype(bf16),
        jnp.concatenate([x.astype(bf16) for x in sums], axis=1),
        preferred_element_type=f32,
    )
    start = jnp.zeros((1, 128), f32)
    rank = jnp.zeros((depth, 128), f32)
    for b in range(spans):
        over = above[:, b * 128 : (b + 1) * 128]
        rank = jnp.where(lines == b, inside[b * depth : (b + 1) * depth, 0:128] + over + start, rank)
        start = start + over[depth - 1 :] + sums[b][depth - 1 :]
    rank = rank.astype(i32)
    for t in range(wide):
        rank_ref[:, 128 * t : 128 * t + 128] = rank[8 * t : 8 * t + 8]

    tile_at = lax.broadcasted_iota(i32, (tiles, slots), 0).astype(f32).astype(bf16)
    place_at = lax.broadcasted_iota(i32, (tile, slots), 0).astype(f32).astype(bf16)
    ordered[...] = jnp.zeros_like(ordered)

    def order(w, _):
        to = rank_ref[pl.ds(w, 1), :]
        in_tile = jnp.where(tile_at == (to // tile).astype(f32).astype(bf16), one, zero)
        at_place = jnp.where(place_at == (to & (tile - 1)).astype(f32).astype(bf16), one, zero)
        parts = [in_tile * pieces[p, pl.ds(w, 1), :].astype(bf16) for p in range(9)]
        ordered[...] += lax.dot_general(
            jnp.concatenate(parts, axis=0),
            at_place,
            (((1,), (1,)), ((), ())),
            preferred_element_type=f32,
        )
        return 0

    lax.fori_loop(0, count, order, 0, unroll=4)
    where_ref[...] = ordered[0:tiles, :].astype(i32)
    copy = pltpu.make_async_copy(where_ref, first, sems.at[1])
    copy.start()

    fetch.wait()
    pack(q_ref, wrap_lo, wrap_hi, span_lo, span_hi, wall)

    def prepare(k, _):
        for c in range(5):
            high, low = split_two(q_ref[c, k])
            here = pl.ds(pl.multiple_of(k * 5 * rows + c * rows, 16), rows)
            planes[here, 0:lanes] = high
            planes[here, lanes : 2 * lanes] = low
            planes[here, 2 * lanes : 3 * lanes] = high
        return 0

    lax.fori_loop(0, spans, prepare, 0)
    copy.wait()

    def weights(cells, at, frac):
        here = lax.broadcasted_iota(i32, (cells, tile), 0)
        return jnp.where(here == at, 1.0 - frac, jnp.where(here == at + 1, frac, 0.0))

    def tile_of(i):
        def piece(p):
            return ordered[pl.ds(p * tiles + i, 1), :]

        span, wrap, normal = piece(0).astype(i32), piece(1).astype(i32), piece(2).astype(i32)
        f0, f1, f2 = [piece(3 + 2 * d) + piece(4 + 2 * d) for d in range(3)]
        cells = lax.broadcasted_iota(i32, (lanes, tile), 0).astype(f32).astype(bf16)
        at_lower, at_upper = [cells == (normal + n).astype(f32).astype(bf16) for n in range(2)]
        (lower_high, lower_low), (upper_high, upper_low) = split_two(1.0 - f2), split_two(f2)
        high = jnp.where(at_lower, lower_high, jnp.where(at_upper, upper_high, zero))
        low = jnp.where(at_lower, lower_low, jnp.where(at_upper, upper_low, zero))
        return span, f0, jnp.concatenate([high, high, low], axis=0), weights(rows, wrap, f1)

    def add_planes(k, number, made, sums):
        span, f0, along, across = made
        from_row = pl.ds(pl.multiple_of(k * 5 * rows, 16), number * 5 * rows)
        mixed = jnp.dot(planes[from_row, :], along, preferred_element_type=f32)
        new = list(sums)
        for n in range(number):
            ws = jnp.where(span == k + n, 1.0 - f0, jnp.where(span + 1 == k + n, f0, 0.0))
            for c in range(5):
                r0 = (5 * n + c) * rows
                total = mixed[r0 : r0 + 8] * across[0:8]
                for r in range(8, rows, 8):
                    total += mixed[r0 + r : r0 + r + 8] * across[r : r + 8]
                new[c] = ws * total if new[c] is None else new[c] + ws * total
        return tuple(new)

    def lowest_of(i):
        return jnp.minimum(first[i, 0], spans - 3)

    def step(g, _):
        for n in range(GROUP):
            i = g * GROUP + n
            for c, x in enumerate(add_planes(lowest_of(i), 3, tile_of(i), (None,) * 5)):
                partial[n, c] = x
        for n in range(GROUP):
            i = g * GROUP + n
            lowest = lowest_of(i)
            more = first[i, tile - 1] - 1 - lowest

            @pl.when(more > 0)
            def _():
                made = tile_of(i)

                def again(m, _):
                    sums = add_planes(lowest + 3 + m, 1, made, tuple(partial[n, c] for c in range(5)))
                    for c in range(5):
                        partial[n, c] = sums[c]
                    return 0

                lax.fori_loop(0, more, again, 0)

        for n in range(GROUP):
            i = g * GROUP + n
            for c in range(5):
                table[pl.ds(c * tiles + i, 1), :] = jnp.sum(partial[n, c], axis=0, keepdims=True)
        return 0

    lax.fori_loop(0, tiles // GROUP, step, 0)

    add_remainders(table)
    both = table[...].astype(bf16)

    def put_back(w, _):
        for t in range(0, slots, 512):
            for c, value in enumerate(lookup(both, rank_ref[pl.ds(w, 1), t : t + 512])):
                out_ref[w, c : c + 1, t : t + 512] = value
        return 0

    lax.fori_loop(0, count, put_back, 0, unroll=8)


def donors(cell, frac, state):
    _, spans, rows, lanes = state.shape
    count, slots = cell.shape
    tiles = count * slots // 256
    shapes = [(count, 5, slots)]
    shapes += [(5, 2, spans, lanes)] * 2 + [(5, 2, rows, lanes)] * 2 + [(5, rows, 2 * spans)]
    return pl.pallas_call(
        donor_kernel,
        grid=(1,),
        in_specs=[IN_VMEM, IN_VMEM, IN_HBM],
        out_specs=[whole(x) for x in shapes],
        out_shape=[jax.ShapeDtypeStruct(x, f32) for x in shapes],
        scratch_shapes=[
            pltpu.VMEM(state.shape, f32),
            pltpu.VMEM((spans * 5 * rows, 3 * lanes), bf16),
            pltpu.VMEM((9, count, slots), f32),
            pltpu.VMEM((count, slots), i32),
            pltpu.VMEM((9 * tiles, 256), f32),
            pltpu.VMEM((tiles, 256), i32),
            pltpu.SMEM((tiles, 256), i32),
            pltpu.VMEM((GROUP, 5, 8, 256), f32),
            pltpu.VMEM((10 * tiles, 256), f32),
            pltpu.SemaphoreType.DMA((2,)),
        ],
        compiler_params=params(60 * 1024 * 1024),
        name="donors",
    )(cell, frac, state)


def fill_kernel(
    from_ref,
    mask_ref,
    q_hbm,
    slot_ref,
    out_ref,
    norm_lo,
    norm_hi,
    span_lo,
    span_hi,
    table,
    spread,
    q_ref,
    sems,
):
    planes = pl.num_programs(0)
    rows, lanes = from_ref.shape[1:]
    count, _, slots = slot_ref.shape
    j = pl.program_id(0)

    def fetch(n):
        return pltpu.make_async_copy(q_hbm.at[:, n], q_ref.at[:, n], sems.at[n])

    @pl.when(j == 0)
    def _():
        for n in range(q_ref.shape[1]):
            fetch(n).start()
        per = slots // 256
        for c in range(4):
            for w in range(count):
                for r in range(per):
                    at = c * count * per + w * per + r
                    table[at : at + 1, :] = slot_ref[w, c : c + 1, r * 256 : (r + 1) * 256]
        add_remainders(table)
        for w in range(count):
            for r in range(slots // 128):
                value = slot_ref[w, 4:5, r * 128 : (r + 1) * 128]
                spread[w * (slots // 128) + r] = jnp.broadcast_to(value, (8, 128))

    fetch(j).wait()
    both = table[...].astype(bf16)
    lines = spread.shape[0]
    share = (rows // 8) * (lanes // 128) * lines // rows
    value = None
    for s in range(rows):
        keep = mask_ref[0, s : s + 1, :] == 1
        for c, found in enumerate(lookup(both, from_ref[0, s : s + 1, :])):
            out_ref[c, 0, s : s + 1, :] = jnp.where(keep, q_ref[c, j, s : s + 1, :], found)
        for n in range(s * share, (s + 1) * share):
            line = n % lines
            if line == 0:
                row, lane = divmod(n // lines, lanes // 128)
                here = (slice(8 * row, 8 * row + 8), slice(128 * lane, 128 * lane + 128))
                at = from_ref[0, here[0], here[1]]
                low, high = at & 127, at // 128
                value = jnp.zeros((8, 128), f32)
            value = jnp.where(high == line, take_lanes(spread[line], low), value)
            if line == lines - 1:
                keep = mask_ref[0, here[0], here[1]] == 1
                out_ref[4, 0, here[0], here[1]] = jnp.where(keep, q_ref[4, j, here[0], here[1]], value)

    for c in range(5):
        for l in range(2):
            span_lo[c, l, pl.ds(j, 1), :] = out_ref[c, 0, l : l + 1, :]
            span_hi[c, l, pl.ds(j, 1), :] = out_ref[c, 0, rows - 2 + l : rows - 1 + l, :]

    @pl.when(j < 2)
    def _():
        for c in range(5):
            norm_lo[c, j] = out_ref[c, 0]

    @pl.when(j >= planes - 2)
    def _():
        for c in range(5):
            norm_hi[c, j - (planes - 2)] = out_ref[c, 0]


def fill(source, mask, state, slot):
    _, planes, rows, lanes = state.shape
    count, _, slots = slot.shape
    plane = pl.BlockSpec((1, rows, lanes), lambda j: (j, 0, 0))
    state_plane = pl.BlockSpec((5, 1, rows, lanes), lambda j: (0, j, 0, 0))
    edges = [(5, 2, rows, lanes)] * 2 + [(5, 2, planes, lanes)] * 2
    return pl.pallas_call(
        fill_kernel,
        grid=(planes,),
        in_specs=[plane, plane, IN_HBM, IN_VMEM],
        out_specs=[state_plane] + [whole(s) for s in edges],
        out_shape=[jax.ShapeDtypeStruct(s, f32) for s in [state.shape] + edges],
        scratch_shapes=[
            pltpu.VMEM((8 * count * slots // 256, 256), f32),
            pltpu.VMEM((count * slots // 128, 8, 128), f32),
            pltpu.VMEM(state.shape, f32),
            pltpu.SemaphoreType.DMA((planes,)),
        ],
        compiler_params=params(49 * 1024 * 1024),
        cost_estimate=pl.CostEstimate(flops=24 * 10**9, bytes_accessed=6 * 10**6, transcendentals=0),
        name="fill",
    )(source, mask, state, slot)


def body(
    cgrid_state, cgrid_metric, flap_state, flap_metric, iblank, fringe_from, donor_cell, donor_frac
):
    wrap_count = lax.axis_size("wrap")

    def ring(axis):
        size = lax.axis_size(axis)
        return [(i, (i + 1) % size) for i in range(size)]

    def onward(value, axis):
        return lax.ppermute(value, axis, ring(axis))

    def back(value, axis):
        return lax.ppermute(value, axis, [(j, i) for i, j in ring(axis)])

    slot, wrap_lo, wrap_hi, span_lo, span_hi, wall = donors(
        donor_cell[0], jnp.transpose(donor_frac[0], (1, 0, 2)), cgrid_state
    )
    far = lax.ppermute(
        wall,
        "wrap",
        [(i, wrap_count - 1 - i if wrapped(i, wrap_count) else i) for i in range(wrap_count)],
    )
    majors = (onward(span_hi, "span"), back(span_lo, "span"))
    subs = (onward(wrap_hi, "wrap"), back(wrap_lo, "wrap"))

    slot = lax.all_to_all(slot, "wrap", split_axis=0, concat_axis=0, tiled=True)

    turned = lambda x: jnp.swapaxes(x, -3, -2)
    mask = turned(iblank)
    filled, norm_lo, norm_hi, edge_lo, edge_hi = fill(turned(fringe_from), mask, turned(flap_state), slot)
    flap_majors = (onward(norm_hi, "wrap"), back(norm_lo, "wrap"))
    flap_subs = (onward(edge_hi, "span"), back(edge_lo, "span"))

    cgrid_rate = rate(
        cgrid_state,
        majors,
        subs,
        (wrap_lo, wrap_hi, wall, far),
        cgrid_metric,
        None,
        cgrid=True,
        step_planes=4,
        components=(3, 1, 2),
        metric_rows=(0, 1, 2),
    )
    flap_rate = rate(
        filled,
        flap_majors,
        flap_subs,
        (),
        turned(flap_metric),
        mask,
        cgrid=False,
        step_planes=3,
        components=(2, 3, 1),
        metric_rows=(1, 0, 2),
    )
    return (cgrid_rate, turned(flap_rate))


def solution(mesh):
    return jax.shard_map(
        body,
        mesh=mesh,
        in_specs=(
            P(None, "span", "wrap", None),
            P(None, "span", "wrap", None),
            P(None, "span", "wrap", None),
            P(None, "span", "wrap", None),
            P("span", "wrap", None),
            P("span", "wrap", None),
            P(("wrap", "span"), None, None),
            P(("wrap", "span"), None, None, None),
        ),
        out_specs=(P(None, "span", "wrap", None), P(None, "span", "wrap", None)),
        check_vma=False,
    )
```

```python
import functools

import jax
import jax.numpy as jnp
from jax import lax
from jax.experimental import pallas as pl
from jax.experimental.pallas import tpu as pltpu
from jax.sharding import PartitionSpec as P

viscosity = 0.05
conduction = 0.07
damping = 1.0 / 32.0
VMEM_LIMIT = 40 * 1024 * 1024
IN_HBM = pl.BlockSpec(memory_space=pltpu.HBM)
IN_VMEM = pl.BlockSpec(memory_space=pltpu.VMEM)
GROUP = 16

f32, bf16, i32 = jnp.float32, jnp.bfloat16, jnp.int32


def whole(shape):
    return pl.BlockSpec(shape, lambda *_: (0,) * len(shape))


def params(limit=VMEM_LIMIT):
    return pltpu.CompilerParams(vmem_limit_bytes=limit)


def primitives(q):
    inverse = 1.0 / q[0]
    v = [q[m] * inverse for m in (1, 2, 3)]
    kinetic = 0.5 * (v[0] * v[0] + v[1] * v[1] + v[2] * v[2])
    pressure = 0.4 * (q[4] - q[0] * kinetic)
    return v + [pressure, kinetic + (conduction / viscosity) * (pressure * inverse)]


def wrapped(place, count):
    return (place < count // 4) | (place >= count - count // 4)


def flux(q, prims, m):
    u = (0.5 / damping) * prims[m - 1]
    f = [q[0] * u]
    for c in (1, 2, 3):
        f.append(q[c] * u + (0.5 / damping) * prims[3] if c == m else q[c] * u)
    f.append((q[4] + prims[3]) * u)
    return f


def pack(q_ref, wrap_lo, wrap_hi, span_lo, span_hi, wall):
    spans, rows = q_ref.shape[1], q_ref.shape[2]
    lane = lax.broadcasted_iota(i32, (rows, 128), 1)
    for c in range(5):
        for l in range(2):
            span_lo[c, l] = q_ref[c, l]
            span_hi[c, l] = q_ref[c, spans - 2 + l]
        cells = jnp.zeros((rows, 128), f32)
        for k in range(spans):
            for l in range(2):
                wrap_lo[c, l, k : k + 1, :] = q_ref[c, k, l : l + 1, :]
                wrap_hi[c, l, k : k + 1, :] = q_ref[c, k, rows - 2 + l : rows - 1 + l, :]
            near = q_ref[c, k, :, 0:128]
            if k:
                near = pltpu.roll(near, 2 * k, 1)
            cells = jnp.where(lane // 2 == k, near, cells)
        wall[c] = cells[:, 0 : 2 * spans]


def rate_kernel(
    q_hbm,
    major_lo,
    major_hi,
    sub_lo,
    sub_hi,
    *refs,
    cgrid,
    step_planes,
    components,
    metric_rows,
):
    if cgrid:
        own_lo, own_hi, wall_own, wall_far, metric_ref, out_ref, qe, prim, sub_edge, lane_edge, mix, sems = refs
    else:
        own_lo = own_hi = None
        mask_ref, metric_ref, out_ref, qe, prim, sub_edge, mix, sems = refs
    planes, rows, lanes = qe.shape[1] - 4, qe.shape[2], qe.shape[3]
    step = pl.program_id(0)
    place, count = lax.axis_index("wrap"), lax.axis_size("wrap")
    at_start = place == 0
    at_end = place == count - 1
    major_m, sub_m, lane_m = components
    width = mix.shape[1]

    def edge_fields(q1, q2, m, side):
        prims = primitives(q1)
        fl = flux(q1, prims, m)
        lead = [4.0 * q1[c] - side * fl[c] - q2[c] for c in range(5)]
        return lead + q1 + prims[:3] + prims[4:]

    def store_prims(k, slot):
        q = [qe[c, k] for c in range(5)]
        prims = primitives(q)
        for i, x in enumerate(prims + flux(q, prims, major_m)):
            prim[slot, i] = x

    steps = planes // step_planes

    def part(n):
        n = n * step_planes
        return pltpu.make_async_copy(
            q_hbm.at[:, pl.ds(n, step_planes)], qe.at[:, pl.ds(n + 2, step_planes)], sems.at[n // step_planes]
        )

    @pl.when(step == 0)
    def _():
        copies = [
            pltpu.make_async_copy(major_lo, qe.at[:, pl.ds(0, 2)], sems.at[steps]),
            pltpu.make_async_copy(major_hi, qe.at[:, pl.ds(planes + 2, 2)], sems.at[steps + 1]),
        ]
        copies[0].start()
        for n in range(steps):
            part(n).start()
        copies[1].start()
        for side, ref, own in ((-1, sub_lo, own_lo), (1, sub_hi, own_hi)):
            near, far = (1, 0) if side < 0 else (0, 1)
            q1 = [ref[c, near] for c in range(5)]
            q2 = [ref[c, far] for c in range(5)]
            if cgrid:
                edge = at_start if side < 0 else at_end
                clamp = 0 if side < 0 else 1
                q1 = [jnp.where(edge, own[c, clamp], q1[c]) for c in range(5)]
                q2 = [jnp.where(edge, own[c, clamp], q2[c]) for c in range(5)]
            for i, x in enumerate(edge_fields(q1, q2, sub_m, side)):
                sub_edge[(side + 1) // 2, i] = x
        if cgrid:
            in_wake = wrapped(place, count)
            turn = 7 - lax.broadcasted_iota(i32, (8, 128), 0)
            ghosts = []
            for c in range(5):
                sign = -1.0 if c in (1, 2, 3) else 1.0
                parts = []
                for r in range(rows // 8):
                    far = wall_far[c, rows - 8 - 8 * r : rows - 8 * r, :]
                    own = wall_own[c, 8 * r : 8 * r + 8, :]
                    own = jnp.concatenate([own, jnp.zeros((8, 128 - own.shape[1]), f32)], axis=1)
                    far = jnp.concatenate([far, jnp.zeros((8, 128 - far.shape[1]), f32)], axis=1)
                    far = jnp.take_along_axis(far, turn, axis=0, mode="promise_in_bounds")
                    parts.append(jnp.where(in_wake, far, sign * own))
                ghosts.append(jnp.concatenate(parts, axis=0))
            second = [pltpu.roll(x, 127, 1) for x in ghosts]
            fields = edge_fields(ghosts, second, lane_m, -1)
            even = lax.broadcasted_iota(i32, (rows, 128), 1) % 2 == 0
            for c in range(5):
                lane_edge[c] = jnp.where(even, fields[c], -pltpu.roll(ghosts[c], 1, 1))
            for i in range(4):
                lane_edge[5 + i] = jnp.where(even, fields[10 + i], 0.0)

        source = lax.broadcasted_iota(i32, (lanes, width), 0)
        target = lax.broadcasted_iota(i32, (lanes, width), 1)
        apart = source - target
        apart = jnp.where(apart > lanes - 3, apart - lanes, apart)

        def band(*pairs):
            total = jnp.zeros((lanes, width), f32)
            for distance, factor in pairs:
                if cgrid:
                    total += jnp.where(source == jnp.minimum(target + distance, lanes - 1), factor, 0.0)
                else:
                    total = jnp.where(apart == distance, factor, total)
            return total.astype(bf16)

        bands = [band((1, -1.0), (-1, 1.0))] * 2
        bands += [band((1, 4.0), (-1, 4.0), (2, -1.0), (-2, -1.0))] * 2
        bands += [band((1, 1.0), (-1, 1.0))] * 2
        for i, x in enumerate(bands):
            mix[i * lanes : (i + 1) * lanes, :] = x

        copies[0].wait()
        part(0).wait()
        part(1).wait()
        copies[1].wait()
        if not cgrid:

            @pl.when(at_start)
            def _():
                for c in range(5):
                    sign = -1.0 if c in (1, 2, 3) else 1.0
                    qe[c, 1] = sign * qe[c, 2]
                    qe[c, 0] = sign * qe[c, 3]

        store_prims(1, 0)
        store_prims(2, 1)

    @pl.when((step > 0) & (step < steps - 1))
    def _():
        part(step + 1).wait()

    if not cgrid:

        @pl.when((step == steps - 1) & at_end)
        def _():
            for c in range(5):
                qe[c, planes + 2] = qe[c, planes + 1]
                qe[c, planes + 3] = qe[c, planes + 1]

    row_at = lax.broadcasted_iota(i32, (8, lanes), 0)
    lane_at = lax.broadcasted_iota(i32, (rows, 128), 1)
    row_first, row_last = row_at == 0, row_at == 7

    def one(b, _):
        k = step * step_planes + b
        here, below, above = lax.rem(k + 1, 3), lax.rem(k, 3), lax.rem(k + 2, 3)
        store_prims(k + 3, above)

        def sub_next(x, i):
            moved = [pltpu.roll(x[r : r + 8], 7, 0) for r in range(0, rows, 8)]
            moved.append(sub_edge[1, i, pl.ds(k, 1), :])
            return jnp.concatenate(
                [jnp.where(row_last, moved[r + 1], moved[r]) for r in range(rows // 8)], axis=0
            )

        def sub_prior(x, i):
            moved = [sub_edge[0, i, pl.ds(k, 1), :]]
            moved += [pltpu.roll(x[r : r + 8], 1, 0) for r in range(0, rows, 8)]
            return jnp.concatenate(
                [jnp.where(row_first, moved[r], moved[r + 1]) for r in range(rows // 8)], axis=0
            )

        gm = metric_ref[metric_rows[0], b]
        gs = metric_ref[metric_rows[1], b]
        gl = metric_ref[metric_rows[2], b]
        gm2, gs2, gl2 = viscosity * gm * gm, viscosity * gs * gs, viscosity * gl * gl
        gm, gs, gl = damping * gm, damping * gs, damping * gl
        all2 = 2.0 * (gm2 + gs2 + gl2)
        all6 = 6.0 * (gm + gs + gl)
        mine = [prim[here, i] for i in range(5)]
        q = [qe[c, k + 2] for c in range(5)]
        lane_flux = flux(q, mine, lane_m)

        def lane_mixed(groups, mixer, edge):
            parts = [[part for x in group for part in split_two(x)] for group in groups]
            lines = []
            for t in range(0, lanes, width):
                for row in parts:
                    turned = [jnp.concatenate([x[:, t:], x[:, :t]], axis=1) if t else x for x in row]
                    lines.append(jnp.concatenate(turned, axis=1))
            mixed = jnp.dot(jnp.concatenate(lines, axis=0), mixer, preferred_element_type=f32)
            results = []
            for i in range(len(groups)):
                at = [(i + n * len(groups)) * rows for n in range(lanes // width)]
                x = jnp.concatenate([mixed[r : r + rows] for r in at], axis=1)
                if cgrid:
                    ghost = pltpu.roll(lane_edge[edge + i], lax.rem(128 - 2 * k, 128), 1)
                    ghost = jnp.where(lane_at < 2, ghost, 0.0)
                    x = jnp.concatenate([x[:, 0:128] + ghost, x[:, 128:]], axis=1)
                results.append(x)
            return results

        lane_damped = lane_mixed([(lane_flux[c], q[c]) for c in range(5)], mix[0 : 4 * lanes, :], 0)
        lane_curved = lane_mixed([(mine[i],) for i in (0, 1, 2, 4)], mix[4 * lanes :, :], 5)
        viscous = {}
        for i, c, e in ((0, 1, 10), (1, 2, 11), (2, 3, 12), (4, 4, 13)):
            x = mine[i]
            total = gm2 * (prim[above, i] + prim[below, i])
            total += gs2 * (sub_next(x, e) + sub_prior(x, e))
            total += gl2 * lane_curved[c - 1]
            viscous[c] = total - all2 * x
        sub_flux = flux(q, mine, sub_m)
        for c in range(5):
            x = q[c]
            four = 4.0 * x
            total = gm * (
                4.0 * (qe[c, k + 3] + qe[c, k + 1])
                - (qe[c, k + 4] + qe[c, k])
                - (prim[above, 5 + c] - prim[below, 5 + c])
            )
            up = four - sub_flux[c] - sub_next(x, 5 + c)
            down = four + sub_flux[c] - sub_prior(x, 5 + c)
            total += gs * (sub_next(up, c) + sub_prior(down, c))
            total += gl * lane_damped[c]
            total -= all6 * x
            if c:
                total += viscous[c]
            if not cgrid:
                total = jnp.where(mask_ref[b] == 1, total, 0.0)
            out_ref[c, b] = total
        return 0

    lax.fori_loop(0, step_planes, one, 0)


def rate(q, majors, subs, extras, metric, mask, *, cgrid, step_planes, components, metric_rows):
    _, planes, rows, lanes = q.shape
    anywhere = pl.BlockSpec(memory_space=pl.ANY)
    block = lambda n: pl.BlockSpec((n, step_planes, rows, lanes), lambda i: (0, i, 0, 0))
    last_specs = [block(3)]
    last = (metric,)
    if mask is not None:
        last_specs = [pl.BlockSpec((step_planes, rows, lanes), lambda i: (i, 0, 0))] + last_specs
        last = (mask, metric)
    return pl.pallas_call(
        functools.partial(
            rate_kernel,
            cgrid=cgrid,
            step_planes=step_planes,
            components=components,
            metric_rows=metric_rows,
        ),
        grid=(planes // step_planes,),
        in_specs=[anywhere] + [IN_VMEM] * (4 + len(extras)) + last_specs,
        out_specs=block(5),
        out_shape=jax.ShapeDtypeStruct(q.shape, f32),
        scratch_shapes=[
            pltpu.VMEM((5, planes + 4, rows, lanes), f32),
            pltpu.VMEM((3, 10, rows, lanes), f32),
            pltpu.VMEM((2, 14, planes, lanes), f32),
        ]
        + [pltpu.VMEM((9, rows, 128), f32)] * cgrid
        + [pltpu.VMEM((6 * lanes, 256), bf16)]
        + [pltpu.SemaphoreType.DMA((planes // step_planes + 2,))],
        compiler_params=params(),
        cost_estimate=pl.CostEstimate(
            flops=300 * planes * rows * lanes, bytes_accessed=60 * planes * rows * lanes, transcendentals=0
        ),
        name="cgrid_rate" if cgrid else "flap_rate",
    )(q, *majors, *subs, *extras, *last)


def split_two(x):
    high = x.astype(bf16)
    return high, (x - high.astype(f32)).astype(bf16)


def lookup(both, at):
    width = at.shape[1]
    highs = 32
    components = both.shape[0] // (2 * highs)
    cells = lax.broadcasted_iota(i32, (256, width), 0).astype(f32).astype(bf16)
    sub = lax.broadcasted_iota(i32, (8, width), 0)
    pick = jnp.where(
        cells == (at & 255).astype(f32).astype(bf16), jnp.ones((), bf16), jnp.zeros((), bf16)
    )
    high = at // 256
    found = jnp.dot(both, pick, preferred_element_type=f32)
    masks = [sub + 8 * g == high for g in range(highs // 8)]
    values = []
    for c in range(components):
        value = None
        for g, mask in enumerate(masks):
            r = c * highs + 8 * g
            remainder = components * highs + r
            piece = found[r : r + 8] + found[remainder : remainder + 8]
            value = jnp.where(mask, piece, 0.0 if value is None else value)
        values.append(jnp.sum(value, axis=0, keepdims=True))
    return values


def take_lanes(values, lanes):
    return lax.gather(
        values,
        lanes[..., None],
        lax.GatherDimensionNumbers(
            offset_dims=(),
            collapsed_slice_dims=(1,),
            start_index_map=(1,),
            operand_batching_dims=(0,),
            start_indices_batching_dims=(0,),
        ),
        slice_sizes=(1, 1),
        mode=lax.GatherScatterMode.PROMISE_IN_BOUNDS,
    )


def add_remainders(table):
    half = table.shape[0] // 2
    for r in range(0, half, 8):
        value = table[r : r + 8, :]
        table[half + r : half + r + 8, :] = value - value.astype(bf16).astype(f32)


def donor_kernel(
    cell_ref,
    frac_ref,
    q_hbm,
    out_ref,
    wrap_lo,
    wrap_hi,
    span_lo,
    span_hi,
    wall,
    q_ref,
    planes,
    pieces,
    rank_ref,
    ordered,
    where_ref,
    first,
    partial,
    table,
    sems,
):
    spans, rows, lanes = q_ref.shape[1:]
    count, slots = cell_ref.shape
    tile = 256
    tiles = count * slots // tile
    wide = slots // 128
    one, zero = jnp.ones((), bf16), jnp.zeros((), bf16)
    fetch = pltpu.make_async_copy(q_hbm, q_ref, sems.at[0])
    fetch.start()

    cell = cell_ref[...]
    upper = jnp.floor((cell.astype(f32) + 0.5) * (1.0 / (lanes - 1)))
    span = jnp.floor((upper + 0.5) * (1.0 / (rows - 1)))
    pieces[0] = span
    pieces[1] = upper - span * (rows - 1)
    pieces[2] = cell.astype(f32) - upper * (lanes - 1)
    for d in range(3):
        f = frac_ref[d]
        high = f.astype(bf16).astype(f32)
        pieces[3 + 2 * d] = high
        pieces[4 + 2 * d] = f - high

    lines = jnp.concatenate([span[:, 128 * t : 128 * t + 128] for t in range(wide)], axis=0)
    depth = lines.shape[0]
    hits = [jnp.where(lines == b, 1.0, 0.0).astype(bf16) for b in range(spans)]
    into = lax.broadcasted_iota(i32, (128, 256), 0)
    onto = lax.broadcasted_iota(i32, (128, 256), 1)
    before = jnp.where((into < onto) | (onto >= 128), 1.0, 0.0).astype(bf16)
    inside = jnp.dot(jnp.concatenate(hits, axis=0), before, preferred_element_type=f32)
    sums = [inside[b * depth : (b + 1) * depth, 128:256] for b in range(spans)]
    lower = lax.broadcasted_iota(i32, (depth, depth), 1) < lax.broadcasted_iota(i32, (depth, depth), 0)
    above = jnp.dot(
        jnp.where(lower, 1.0, 0.0).astype(bf16),
        jnp.concatenate([x.astype(bf16) for x in sums], axis=1),
        preferred_element_type=f32,
    )
    start = jnp.zeros((1, 128), f32)
    rank = jnp.zeros((depth, 128), f32)
    for b in range(spans):
        over = above[:, b * 128 : (b + 1) * 128]
        rank = jnp.where(lines == b, inside[b * depth : (b + 1) * depth, 0:128] + over + start, rank)
        start = start + over[depth - 1 :] + sums[b][depth - 1 :]
    rank = rank.astype(i32)
    for t in range(wide):
        rank_ref[:, 128 * t : 128 * t + 128] = rank[8 * t : 8 * t + 8]

    tile_at = lax.broadcasted_iota(i32, (tiles, slots), 0).astype(f32).astype(bf16)
    place_at = lax.broadcasted_iota(i32, (tile, slots), 0).astype(f32).astype(bf16)
    ordered[...] = jnp.zeros_like(ordered)

    def order(w, _):
        to = rank_ref[pl.ds(w, 1), :]
        in_tile = jnp.where(tile_at == (to // tile).astype(f32).astype(bf16), one, zero)
        at_place = jnp.where(place_at == (to & (tile - 1)).astype(f32).astype(bf16), one, zero)
        parts = [in_tile * pieces[p, pl.ds(w, 1), :].astype(bf16) for p in range(9)]
        ordered[...] += lax.dot_general(
            jnp.concatenate(parts, axis=0),
            at_place,
            (((1,), (1,)), ((), ())),
            preferred_element_type=f32,
        )
        return 0

    lax.fori_loop(0, count, order, 0, unroll=4)
    where_ref[...] = ordered[0:tiles, :].astype(i32)
    copy = pltpu.make_async_copy(where_ref, first, sems.at[1])
    copy.start()

    fetch.wait()
    pack(q_ref, wrap_lo, wrap_hi, span_lo, span_hi, wall)

    def prepare(k, _):
        for c in range(5):
            high, low = split_two(q_ref[c, k])
            here = pl.ds(pl.multiple_of(k * 5 * rows + c * rows, 16), rows)
            planes[here, 0:lanes] = high
            planes[here, lanes : 2 * lanes] = low
            planes[here, 2 * lanes : 3 * lanes] = high
        return 0

    lax.fori_loop(0, spans, prepare, 0)
    copy.wait()

    def weights(cells, at, frac):
        here = lax.broadcasted_iota(i32, (cells, tile), 0)
        return jnp.where(here == at, 1.0 - frac, jnp.where(here == at + 1, frac, 0.0))

    def tile_of(i):
        def piece(p):
            return ordered[pl.ds(p * tiles + i, 1), :]

        span, wrap, normal = piece(0).astype(i32), piece(1).astype(i32), piece(2).astype(i32)
        f0, f1, f2 = [piece(3 + 2 * d) + piece(4 + 2 * d) for d in range(3)]
        cells = lax.broadcasted_iota(i32, (lanes, tile), 0).astype(f32).astype(bf16)
        at_lower, at_upper = [cells == (normal + n).astype(f32).astype(bf16) for n in range(2)]
        (lower_high, lower_low), (upper_high, upper_low) = split_two(1.0 - f2), split_two(f2)
        high = jnp.where(at_lower, lower_high, jnp.where(at_upper, upper_high, zero))
        low = jnp.where(at_lower, lower_low, jnp.where(at_upper, upper_low, zero))
        return span, f0, jnp.concatenate([high, high, low], axis=0), weights(rows, wrap, f1)

    def add_planes(k, number, made, sums):
        span, f0, along, across = made
        from_row = pl.ds(pl.multiple_of(k * 5 * rows, 16), number * 5 * rows)
        mixed = jnp.dot(planes[from_row, :], along, preferred_element_type=f32)
        new = list(sums)
        for n in range(number):
            ws = jnp.where(span == k + n, 1.0 - f0, jnp.where(span + 1 == k + n, f0, 0.0))
            for c in range(5):
                r0 = (5 * n + c) * rows
                total = mixed[r0 : r0 + 8] * across[0:8]
                for r in range(8, rows, 8):
                    total += mixed[r0 + r : r0 + r + 8] * across[r : r + 8]
                new[c] = ws * total if new[c] is None else new[c] + ws * total
        return tuple(new)

    def lowest_of(i):
        return jnp.minimum(first[i, 0], spans - 3)

    def step(g, _):
        for n in range(GROUP):
            i = g * GROUP + n
            for c, x in enumerate(add_planes(lowest_of(i), 3, tile_of(i), (None,) * 5)):
                partial[n, c] = x
        for n in range(GROUP):
            i = g * GROUP + n
            lowest = lowest_of(i)
            more = first[i, tile - 1] - 1 - lowest

            @pl.when(more > 0)
            def _():
                made = tile_of(i)

                def again(m, _):
                    sums = add_planes(lowest + 3 + m, 1, made, tuple(partial[n, c] for c in range(5)))
                    for c in range(5):
                        partial[n, c] = sums[c]
                    return 0

                lax.fori_loop(0, more, again, 0)

        for n in range(GROUP):
            i = g * GROUP + n
            for c in range(5):
                table[pl.ds(c * tiles + i, 1), :] = jnp.sum(partial[n, c], axis=0, keepdims=True)
        return 0

    lax.fori_loop(0, tiles // GROUP, step, 0)

    add_remainders(table)
    both = table[...].astype(bf16)

    def put_back(w, _):
        for t in range(0, slots, 512):
            for c, value in enumerate(lookup(both, rank_ref[pl.ds(w, 1), t : t + 512])):
                out_ref[w, c : c + 1, t : t + 512] = value
        return 0

    lax.fori_loop(0, count, put_back, 0, unroll=8)


def donors(cell, frac, state):
    _, spans, rows, lanes = state.shape
    count, slots = cell.shape
    tiles = count * slots // 256
    shapes = [(count, 5, slots)]
    shapes += [(5, 2, spans, lanes)] * 2 + [(5, 2, rows, lanes)] * 2 + [(5, rows, 2 * spans)]
    return pl.pallas_call(
        donor_kernel,
        grid=(1,),
        in_specs=[IN_VMEM, IN_VMEM, IN_HBM],
        out_specs=[whole(x) for x in shapes],
        out_shape=[jax.ShapeDtypeStruct(x, f32) for x in shapes],
        scratch_shapes=[
            pltpu.VMEM(state.shape, f32),
            pltpu.VMEM((spans * 5 * rows, 3 * lanes), bf16),
            pltpu.VMEM((9, count, slots), f32),
            pltpu.VMEM((count, slots), i32),
            pltpu.VMEM((9 * tiles, 256), f32),
            pltpu.VMEM((tiles, 256), i32),
            pltpu.SMEM((tiles, 256), i32),
            pltpu.VMEM((GROUP, 5, 8, 256), f32),
            pltpu.VMEM((10 * tiles, 256), f32),
            pltpu.SemaphoreType.DMA((2,)),
        ],
        compiler_params=params(60 * 1024 * 1024),
        name="donors",
    )(cell, frac, state)


def fill_kernel(
    from_ref,
    mask_ref,
    q_hbm,
    slot_ref,
    out_ref,
    norm_lo,
    norm_hi,
    span_lo,
    span_hi,
    table,
    spread,
    q_ref,
    sems,
):
    planes = pl.num_programs(0)
    rows, lanes = from_ref.shape[1:]
    count, _, slots = slot_ref.shape
    j = pl.program_id(0)

    def fetch(n):
        return pltpu.make_async_copy(q_hbm.at[:, n], q_ref.at[:, n], sems.at[n])

    @pl.when(j == 0)
    def _():
        for n in range(q_ref.shape[1]):
            fetch(n).start()
        per = slots // 256
        for c in range(4):
            for w in range(count):
                for r in range(per):
                    at = c * count * per + w * per + r
                    table[at : at + 1, :] = slot_ref[w, c : c + 1, r * 256 : (r + 1) * 256]
        add_remainders(table)
        for w in range(count):
            for r in range(slots // 128):
                value = slot_ref[w, 4:5, r * 128 : (r + 1) * 128]
                spread[w * (slots // 128) + r] = jnp.broadcast_to(value, (8, 128))

    fetch(j).wait()
    both = table[...].astype(bf16)
    lines = spread.shape[0]
    share = (rows // 8) * (lanes // 128) * lines // rows
    value = None
    for s in range(rows):
        keep = mask_ref[0, s : s + 1, :] == 1
        for c, found in enumerate(lookup(both, from_ref[0, s : s + 1, :])):
            out_ref[c, 0, s : s + 1, :] = jnp.where(keep, q_ref[c, j, s : s + 1, :], found)
        for n in range(s * share, (s + 1) * share):
            line = n % lines
            if line == 0:
                row, lane = divmod(n // lines, lanes // 128)
                here = (slice(8 * row, 8 * row + 8), slice(128 * lane, 128 * lane + 128))
                at = from_ref[0, here[0], here[1]]
                low, high = at & 127, at // 128
                value = jnp.zeros((8, 128), f32)
            value = jnp.where(high == line, take_lanes(spread[line], low), value)
            if line == lines - 1:
                keep = mask_ref[0, here[0], here[1]] == 1
                out_ref[4, 0, here[0], here[1]] = jnp.where(keep, q_ref[4, j, here[0], here[1]], value)

    for c in range(5):
        for l in range(2):
            span_lo[c, l, pl.ds(j, 1), :] = out_ref[c, 0, l : l + 1, :]
            span_hi[c, l, pl.ds(j, 1), :] = out_ref[c, 0, rows - 2 + l : rows - 1 + l, :]

    @pl.when(j < 2)
    def _():
        for c in range(5):
            norm_lo[c, j] = out_ref[c, 0]

    @pl.when(j >= planes - 2)
    def _():
        for c in range(5):
            norm_hi[c, j - (planes - 2)] = out_ref[c, 0]


def fill(source, mask, state, slot):
    _, planes, rows, lanes = state.shape
    count, _, slots = slot.shape
    plane = pl.BlockSpec((1, rows, lanes), lambda j: (j, 0, 0))
    state_plane = pl.BlockSpec((5, 1, rows, lanes), lambda j: (0, j, 0, 0))
    edges = [(5, 2, rows, lanes)] * 2 + [(5, 2, planes, lanes)] * 2
    return pl.pallas_call(
        fill_kernel,
        grid=(planes,),
        in_specs=[plane, plane, IN_HBM, IN_VMEM],
        out_specs=[state_plane] + [whole(s) for s in edges],
        out_shape=[jax.ShapeDtypeStruct(s, f32) for s in [state.shape] + edges],
        scratch_shapes=[
            pltpu.VMEM((8 * count * slots // 256, 256), f32),
            pltpu.VMEM((count * slots // 128, 8, 128), f32),
            pltpu.VMEM(state.shape, f32),
            pltpu.SemaphoreType.DMA((planes,)),
        ],
        compiler_params=params(49 * 1024 * 1024),
        cost_estimate=pl.CostEstimate(flops=24 * 10**9, bytes_accessed=6 * 10**6, transcendentals=0),
        name="fill",
    )(source, mask, state, slot)


def body(
    cgrid_state, cgrid_metric, flap_state, flap_metric, iblank, fringe_from, donor_cell, donor_frac
):
    wrap_count = lax.axis_size("wrap")

    def ring(axis):
        size = lax.axis_size(axis)
        return [(i, (i + 1) % size) for i in range(size)]

    def onward(value, axis):
        return lax.ppermute(value, axis, ring(axis))

    def back(value, axis):
        return lax.ppermute(value, axis, [(j, i) for i, j in ring(axis)])

    slot, wrap_lo, wrap_hi, span_lo, span_hi, wall = donors(
        donor_cell[0], jnp.transpose(donor_frac[0], (1, 0, 2)), cgrid_state
    )
    far = lax.ppermute(
        wall,
        "wrap",
        [(i, wrap_count - 1 - i if wrapped(i, wrap_count) else i) for i in range(wrap_count)],
    )
    majors = (onward(span_hi, "span"), back(span_lo, "span"))
    subs = (onward(wrap_hi, "wrap"), back(wrap_lo, "wrap"))

    slot = lax.all_to_all(slot, "wrap", split_axis=0, concat_axis=0, tiled=True)

    turned = lambda x: jnp.swapaxes(x, -3, -2)
    mask = turned(iblank)
    filled, norm_lo, norm_hi, edge_lo, edge_hi = fill(turned(fringe_from), mask, turned(flap_state), slot)
    flap_majors = (onward(norm_hi, "wrap"), back(norm_lo, "wrap"))
    flap_subs = (onward(edge_hi, "span"), back(edge_lo, "span"))

    cgrid_rate = rate(
        cgrid_state,
        majors,
        subs,
        (wrap_lo, wrap_hi, wall, far),
        cgrid_metric,
        None,
        cgrid=True,
        step_planes=4,
        components=(3, 1, 2),
        metric_rows=(0, 1, 2),
    )
    flap_rate = rate(
        filled,
        flap_majors,
        flap_subs,
        (),
        turned(flap_metric),
        mask,
        cgrid=False,
        step_planes=3,
        components=(2, 3, 1),
        metric_rows=(1, 0, 2),
    )
    return (cgrid_rate, turned(flap_rate))


def solution(mesh):
    return jax.shard_map(
        body,
        mesh=mesh,
        in_specs=(
            P(None, "span", "wrap", None),
            P(None, "span", "wrap", None),
            P(None, "span", "wrap", None),
            P(None, "span", "wrap", None),
            P("span", "wrap", None),
            P("span", "wrap", None),
            P(("wrap", "span"), None, None),
            P(("wrap", "span"), None, None, None),
        ),
        out_specs=(P(None, "span", "wrap", None), P(None, "span", "wrap", None)),
        check_vma=False,
    )
```

```python
import functools

import jax
import jax.numpy as jnp
from jax import lax
from jax.experimental import pallas as pl
from jax.experimental.pallas import tpu as pltpu
from jax.sharding import PartitionSpec as P

viscosity = 0.05
conduction = 0.07
damping = 1.0 / 32.0
VMEM_LIMIT = 40 * 1024 * 1024
IN_HBM = pl.BlockSpec(memory_space=pltpu.HBM)
IN_VMEM = pl.BlockSpec(memory_space=pltpu.VMEM)
GROUP = 16

f32, bf16, i32 = jnp.float32, jnp.bfloat16, jnp.int32


def whole(shape):
    return pl.BlockSpec(shape, lambda *_: (0,) * len(shape))


def params(limit=VMEM_LIMIT):
    return pltpu.CompilerParams(vmem_limit_bytes=limit)


def primitives(q):
    inverse = 1.0 / q[0]
    v = [q[m] * inverse for m in (1, 2, 3)]
    kinetic = 0.5 * (v[0] * v[0] + v[1] * v[1] + v[2] * v[2])
    pressure = 0.4 * (q[4] - q[0] * kinetic)
    return v + [pressure, kinetic + (conduction / viscosity) * (pressure * inverse)]


def wrapped(place, count):
    return (place < count // 4) | (place >= count - count // 4)


def flux(q, prims, m):
    u = (0.5 / damping) * prims[m - 1]
    f = [q[0] * u]
    for c in (1, 2, 3):
        f.append(q[c] * u + (0.5 / damping) * prims[3] if c == m else q[c] * u)
    f.append((q[4] + prims[3]) * u)
    return f


def pack(q_ref, wrap_lo, wrap_hi, span_lo, span_hi, wall):
    spans, rows = q_ref.shape[1], q_ref.shape[2]
    lane = lax.broadcasted_iota(i32, (rows, 128), 1)
    for c in range(5):
        for l in range(2):
            span_lo[c, l] = q_ref[c, l]
            span_hi[c, l] = q_ref[c, spans - 2 + l]
        cells = jnp.zeros((rows, 128), f32)
        for k in range(spans):
            for l in range(2):
                wrap_lo[c, l, k : k + 1, :] = q_ref[c, k, l : l + 1, :]
                wrap_hi[c, l, k : k + 1, :] = q_ref[c, k, rows - 2 + l : rows - 1 + l, :]
            near = q_ref[c, k, :, 0:128]
            if k:
                near = pltpu.roll(near, 2 * k, 1)
            cells = jnp.where(lane // 2 == k, near, cells)
        wall[c] = cells[:, 0 : 2 * spans]


def rate_kernel(
    q_hbm,
    major_lo,
    major_hi,
    sub_lo,
    sub_hi,
    *refs,
    cgrid,
    step_planes,
    components,
    metric_rows,
):
    if cgrid:
        own_lo, own_hi, wall_own, wall_far, metric_ref, out_ref, qe, prim, sub_edge, lane_edge, mix, sems = refs
    else:
        own_lo = own_hi = None
        mask_ref, metric_ref, out_ref, qe, prim, sub_edge, mix, sems = refs
    planes, rows, lanes = qe.shape[1] - 4, qe.shape[2], qe.shape[3]
    step = pl.program_id(0)
    place, count = lax.axis_index("wrap"), lax.axis_size("wrap")
    at_start = place == 0
    at_end = place == count - 1
    major_m, sub_m, lane_m = components
    width = mix.shape[1]

    def edge_fields(q1, q2, m, side):
        prims = primitives(q1)
        fl = flux(q1, prims, m)
        lead = [4.0 * q1[c] - side * fl[c] - q2[c] for c in range(5)]
        return lead + q1 + prims[:3] + prims[4:]

    def store_prims(k, slot):
        q = [qe[c, k] for c in range(5)]
        prims = primitives(q)
        for i, x in enumerate(prims + flux(q, prims, major_m)):
            prim[slot, i] = x

    steps = planes // step_planes

    def part(n):
        n = n * step_planes
        return pltpu.make_async_copy(
            q_hbm.at[:, pl.ds(n, step_planes)], qe.at[:, pl.ds(n + 2, step_planes)], sems.at[n // step_planes]
        )

    @pl.when(step == 0)
    def _():
        copies = [
            pltpu.make_async_copy(major_lo, qe.at[:, pl.ds(0, 2)], sems.at[steps]),
            pltpu.make_async_copy(major_hi, qe.at[:, pl.ds(planes + 2, 2)], sems.at[steps + 1]),
        ]
        copies[0].start()
        for n in range(steps):
            part(n).start()
        copies[1].start()
        for side, ref, own in ((-1, sub_lo, own_lo), (1, sub_hi, own_hi)):
            near, far = (1, 0) if side < 0 else (0, 1)
            q1 = [ref[c, near] for c in range(5)]
            q2 = [ref[c, far] for c in range(5)]
            if cgrid:
                edge = at_start if side < 0 else at_end
                clamp = 0 if side < 0 else 1
                q1 = [jnp.where(edge, own[c, clamp], q1[c]) for c in range(5)]
                q2 = [jnp.where(edge, own[c, clamp], q2[c]) for c in range(5)]
            for i, x in enumerate(edge_fields(q1, q2, sub_m, side)):
                sub_edge[(side + 1) // 2, i] = x
        if cgrid:
            in_wake = wrapped(place, count)
            turn = 7 - lax.broadcasted_iota(i32, (8, 128), 0)
            ghosts = []
            for c in range(5):
                sign = -1.0 if c in (1, 2, 3) else 1.0
                parts = []
                for r in range(rows // 8):
                    far = wall_far[c, rows - 8 - 8 * r : rows - 8 * r, :]
                    own = wall_own[c, 8 * r : 8 * r + 8, :]
                    own = jnp.concatenate([own, jnp.zeros((8, 128 - own.shape[1]), f32)], axis=1)
                    far = jnp.concatenate([far, jnp.zeros((8, 128 - far.shape[1]), f32)], axis=1)
                    far = jnp.take_along_axis(far, turn, axis=0, mode="promise_in_bounds")
                    parts.append(jnp.where(in_wake, far, sign * own))
                ghosts.append(jnp.concatenate(parts, axis=0))
            second = [pltpu.roll(x, 127, 1) for x in ghosts]
            fields = edge_fields(ghosts, second, lane_m, -1)
            even = lax.broadcasted_iota(i32, (rows, 128), 1) % 2 == 0
            for c in range(5):
                lane_edge[c] = jnp.where(even, fields[c], -pltpu.roll(ghosts[c], 1, 1))
            for i in range(4):
                lane_edge[5 + i] = jnp.where(even, fields[10 + i], 0.0)

        source = lax.broadcasted_iota(i32, (lanes, width), 0)
        target = lax.broadcasted_iota(i32, (lanes, width), 1)
        apart = source - target
        apart = jnp.where(apart > lanes - 3, apart - lanes, apart)

        def band(*pairs):
            total = jnp.zeros((lanes, width), f32)
            for distance, factor in pairs:
                if cgrid:
                    total += jnp.where(source == jnp.minimum(target + distance, lanes - 1), factor, 0.0)
                else:
                    total = jnp.where(apart == distance, factor, total)
            return total.astype(bf16)

        bands = [band((1, -1.0), (-1, 1.0))] * 2
        bands += [band((1, 4.0), (-1, 4.0), (2, -1.0), (-2, -1.0))] * 2
        bands += [band((1, 1.0), (-1, 1.0))] * 2
        for i, x in enumerate(bands):
            mix[i * lanes : (i + 1) * lanes, :] = x

        copies[0].wait()
        part(0).wait()
        part(1).wait()
        copies[1].wait()
        if not cgrid:

            @pl.when(at_start)
            def _():
                for c in range(5):
                    sign = -1.0 if c in (1, 2, 3) else 1.0
                    qe[c, 1] = sign * qe[c, 2]
                    qe[c, 0] = sign * qe[c, 3]

        store_prims(1, 0)
        store_prims(2, 1)

    @pl.when((step > 0) & (step < steps - 1))
    def _():
        part(step + 1).wait()

    if not cgrid:

        @pl.when((step == steps - 1) & at_end)
        def _():
            for c in range(5):
                qe[c, planes + 2] = qe[c, planes + 1]
                qe[c, planes + 3] = qe[c, planes + 1]

    row_at = lax.broadcasted_iota(i32, (8, lanes), 0)
    lane_at = lax.broadcasted_iota(i32, (rows, 128), 1)
    row_first, row_last = row_at == 0, row_at == 7

    def one(b, _):
        k = step * step_planes + b
        here, below, above = lax.rem(k + 1, 3), lax.rem(k, 3), lax.rem(k + 2, 3)
        store_prims(k + 3, above)

        def sub_next(x, i):
            moved = [pltpu.roll(x[r : r + 8], 7, 0) for r in range(0, rows, 8)]
            moved.append(sub_edge[1, i, pl.ds(k, 1), :])
            return jnp.concatenate(
                [jnp.where(row_last, moved[r + 1], moved[r]) for r in range(rows // 8)], axis=0
            )

        def sub_prior(x, i):
            moved = [sub_edge[0, i, pl.ds(k, 1), :]]
            moved += [pltpu.roll(x[r : r + 8], 1, 0) for r in range(0, rows, 8)]
            return jnp.concatenate(
                [jnp.where(row_first, moved[r], moved[r + 1]) for r in range(rows // 8)], axis=0
            )

        gm = metric_ref[metric_rows[0], b]
        gs = metric_ref[metric_rows[1], b]
        gl = metric_ref[metric_rows[2], b]
        gm2, gs2, gl2 = viscosity * gm * gm, viscosity * gs * gs, viscosity * gl * gl
        gm, gs, gl = damping * gm, damping * gs, damping * gl
        all2 = 2.0 * (gm2 + gs2 + gl2)
        all6 = 6.0 * (gm + gs + gl)
        mine = [prim[here, i] for i in range(5)]
        q = [qe[c, k + 2] for c in range(5)]
        lane_flux = flux(q, mine, lane_m)

        def lane_mixed(groups, mixer, edge):
            parts = [[part for x in group for part in split_two(x)] for group in groups]
            lines = []
            for t in range(0, lanes, width):
                for row in parts:
                    turned = [jnp.concatenate([x[:, t:], x[:, :t]], axis=1) if t else x for x in row]
                    lines.append(jnp.concatenate(turned, axis=1))
            mixed = jnp.dot(jnp.concatenate(lines, axis=0), mixer, preferred_element_type=f32)
            results = []
            for i in range(len(groups)):
                at = [(i + n * len(groups)) * rows for n in range(lanes // width)]
                x = jnp.concatenate([mixed[r : r + rows] for r in at], axis=1)
                if cgrid:
                    ghost = pltpu.roll(lane_edge[edge + i], lax.rem(128 - 2 * k, 128), 1)
                    ghost = jnp.where(lane_at < 2, ghost, 0.0)
                    x = jnp.concatenate([x[:, 0:128] + ghost, x[:, 128:]], axis=1)
                results.append(x)
            return results

        lane_damped = lane_mixed([(lane_flux[c], q[c]) for c in range(5)], mix[0 : 4 * lanes, :], 0)
        lane_curved = lane_mixed([(mine[i],) for i in (0, 1, 2, 4)], mix[4 * lanes :, :], 5)
        viscous = {}
        for i, c, e in ((0, 1, 10), (1, 2, 11), (2, 3, 12), (4, 4, 13)):
            x = mine[i]
            total = gm2 * (prim[above, i] + prim[below, i])
            total += gs2 * (sub_next(x, e) + sub_prior(x, e))
            total += gl2 * lane_curved[c - 1]
            viscous[c] = total - all2 * x
        sub_flux = flux(q, mine, sub_m)
        for c in range(5):
            x = q[c]
            four = 4.0 * x
            total = gm * (
                4.0 * (qe[c, k + 3] + qe[c, k + 1])
                - (qe[c, k + 4] + qe[c, k])
                - (prim[above, 5 + c] - prim[below, 5 + c])
            )
            up = four - sub_flux[c] - sub_next(x, 5 + c)
            down = four + sub_flux[c] - sub_prior(x, 5 + c)
            total += gs * (sub_next(up, c) + sub_prior(down, c))
            total += gl * lane_damped[c]
            total -= all6 * x
            if c:
                total += viscous[c]
            if not cgrid:
                total = jnp.where(mask_ref[b] == 1, total, 0.0)
            out_ref[c, b] = total
        return 0

    lax.fori_loop(0, step_planes, one, 0)


def rate(q, majors, subs, extras, metric, mask, *, cgrid, step_planes, components, metric_rows):
    _, planes, rows, lanes = q.shape
    anywhere = pl.BlockSpec(memory_space=pl.ANY)
    block = lambda n: pl.BlockSpec((n, step_planes, rows, lanes), lambda i: (0, i, 0, 0))
    last_specs = [block(3)]
    last = (metric,)
    if mask is not None:
        last_specs = [pl.BlockSpec((step_planes, rows, lanes), lambda i: (i, 0, 0))] + last_specs
        last = (mask, metric)
    return pl.pallas_call(
        functools.partial(
            rate_kernel,
            cgrid=cgrid,
            step_planes=step_planes,
            components=components,
            metric_rows=metric_rows,
        ),
        grid=(planes // step_planes,),
        in_specs=[anywhere] + [IN_VMEM] * (4 + len(extras)) + last_specs,
        out_specs=block(5),
        out_shape=jax.ShapeDtypeStruct(q.shape, f32),
        scratch_shapes=[
            pltpu.VMEM((5, planes + 4, rows, lanes), f32),
            pltpu.VMEM((3, 10, rows, lanes), f32),
            pltpu.VMEM((2, 14, planes, lanes), f32),
        ]
        + [pltpu.VMEM((9, rows, 128), f32)] * cgrid
        + [pltpu.VMEM((6 * lanes, 256), bf16)]
        + [pltpu.SemaphoreType.DMA((planes // step_planes + 2,))],
        compiler_params=params(),
        cost_estimate=pl.CostEstimate(
            flops=300 * planes * rows * lanes, bytes_accessed=60 * planes * rows * lanes, transcendentals=0
        ),
        name="cgrid_rate" if cgrid else "flap_rate",
    )(q, *majors, *subs, *extras, *last)


def split_two(x):
    high = x.astype(bf16)
    return high, (x - high.astype(f32)).astype(bf16)


def lookup(both, at):
    width = at.shape[1]
    highs = 32
    components = both.shape[0] // (2 * highs)
    cells = lax.broadcasted_iota(i32, (256, width), 0).astype(f32).astype(bf16)
    sub = lax.broadcasted_iota(i32, (8, width), 0)
    pick = jnp.where(
        cells == (at & 255).astype(f32).astype(bf16), jnp.ones((), bf16), jnp.zeros((), bf16)
    )
    high = at // 256
    found = jnp.dot(both, pick, preferred_element_type=f32)
    masks = [sub + 8 * g == high for g in range(highs // 8)]
    values = []
    for c in range(components):
        value = None
        for g, mask in enumerate(masks):
            r = c * highs + 8 * g
            remainder = components * highs + r
            piece = found[r : r + 8] + found[remainder : remainder + 8]
            value = jnp.where(mask, piece, 0.0 if value is None else value)
        values.append(jnp.sum(value, axis=0, keepdims=True))
    return values


def take_lanes(values, lanes):
    return lax.gather(
        values,
        lanes[..., None],
        lax.GatherDimensionNumbers(
            offset_dims=(),
            collapsed_slice_dims=(1,),
            start_index_map=(1,),
            operand_batching_dims=(0,),
            start_indices_batching_dims=(0,),
        ),
        slice_sizes=(1, 1),
        mode=lax.GatherScatterMode.PROMISE_IN_BOUNDS,
    )


def add_remainders(table):
    half = table.shape[0] // 2
    for r in range(0, half, 8):
        value = table[r : r + 8, :]
        table[half + r : half + r + 8, :] = value - value.astype(bf16).astype(f32)


def donor_kernel(
    cell_ref,
    frac_ref,
    q_hbm,
    out_ref,
    wrap_lo,
    wrap_hi,
    span_lo,
    span_hi,
    wall,
    q_ref,
    planes,
    pieces,
    rank_ref,
    ordered,
    where_ref,
    first,
    partial,
    table,
    sems,
):
    spans, rows, lanes = q_ref.shape[1:]
    count, slots = cell_ref.shape
    tile = 256
    tiles = count * slots // tile
    wide = slots // 128
    one, zero = jnp.ones((), bf16), jnp.zeros((), bf16)
    fetch = pltpu.make_async_copy(q_hbm, q_ref, sems.at[0])
    fetch.start()

    cell = cell_ref[...]
    upper = jnp.floor((cell.astype(f32) + 0.5) * (1.0 / (lanes - 1)))
    span = jnp.floor((upper + 0.5) * (1.0 / (rows - 1)))
    pieces[0] = span
    pieces[1] = upper - span * (rows - 1)
    pieces[2] = cell.astype(f32) - upper * (lanes - 1)
    for d in range(3):
        f = frac_ref[d]
        high = f.astype(bf16).astype(f32)
        pieces[3 + 2 * d] = high
        pieces[4 + 2 * d] = f - high

    lines = jnp.concatenate([span[:, 128 * t : 128 * t + 128] for t in range(wide)], axis=0)
    depth = lines.shape[0]
    hits = [jnp.where(lines == b, 1.0, 0.0).astype(bf16) for b in range(spans)]
    into = lax.broadcasted_iota(i32, (128, 256), 0)
    onto = lax.broadcasted_iota(i32, (128, 256), 1)
    before = jnp.where((into < onto) | (onto >= 128), 1.0, 0.0).astype(bf16)
    inside = jnp.dot(jnp.concatenate(hits, axis=0), before, preferred_element_type=f32)
    sums = [inside[b * depth : (b + 1) * depth, 128:256] for b in range(spans)]
    lower = lax.broadcasted_iota(i32, (depth, depth), 1) < lax.broadcasted_iota(i32, (depth, depth), 0)
    above = jnp.dot(
        jnp.where(lower, 1.0, 0.0).astype(bf16),
        jnp.concatenate([x.astype(bf16) for x in sums], axis=1),
        preferred_element_type=f32,
    )
    start = jnp.zeros((1, 128), f32)
    rank = jnp.zeros((depth, 128), f32)
    for b in range(spans):
        over = above[:, b * 128 : (b + 1) * 128]
        rank = jnp.where(lines == b, inside[b * depth : (b + 1) * depth, 0:128] + over + start, rank)
        start = start + over[depth - 1 :] + sums[b][depth - 1 :]
    rank = rank.astype(i32)
    for t in range(wide):
        rank_ref[:, 128 * t : 128 * t + 128] = rank[8 * t : 8 * t + 8]

    tile_at = lax.broadcasted_iota(i32, (tiles, slots), 0).astype(f32).astype(bf16)
    place_at = lax.broadcasted_iota(i32, (tile, slots), 0).astype(f32).astype(bf16)
    ordered[...] = jnp.zeros_like(ordered)

    def order(w, _):
        to = rank_ref[pl.ds(w, 1), :]
        in_tile = jnp.where(tile_at == (to // tile).astype(f32).astype(bf16), one, zero)
        at_place = jnp.where(place_at == (to & (tile - 1)).astype(f32).astype(bf16), one, zero)
        parts = [in_tile * pieces[p, pl.ds(w, 1), :].astype(bf16) for p in range(9)]
        ordered[...] += lax.dot_general(
            jnp.concatenate(parts, axis=0),
            at_place,
            (((1,), (1,)), ((), ())),
            preferred_element_type=f32,
        )
        return 0

    lax.fori_loop(0, count, order, 0, unroll=4)
    where_ref[...] = ordered[0:tiles, :].astype(i32)
    copy = pltpu.make_async_copy(where_ref, first, sems.at[1])
    copy.start()

    fetch.wait()
    pack(q_ref, wrap_lo, wrap_hi, span_lo, span_hi, wall)

    def prepare(k, _):
        for c in range(5):
            high, low = split_two(q_ref[c, k])
            here = pl.ds(pl.multiple_of(k * 5 * rows + c * rows, 16), rows)
            planes[here, 0:lanes] = high
            planes[here, lanes : 2 * lanes] = low
            planes[here, 2 * lanes : 3 * lanes] = high
        return 0

    lax.fori_loop(0, spans, prepare, 0)
    copy.wait()

    def weights(cells, at, frac):
        here = lax.broadcasted_iota(i32, (cells, tile), 0)
        return jnp.where(here == at, 1.0 - frac, jnp.where(here == at + 1, frac, 0.0))

    def tile_of(i):
        def piece(p):
            return ordered[pl.ds(p * tiles + i, 1), :]

        span, wrap, normal = piece(0).astype(i32), piece(1).astype(i32), piece(2).astype(i32)
        f0, f1, f2 = [piece(3 + 2 * d) + piece(4 + 2 * d) for d in range(3)]
        cells = lax.broadcasted_iota(i32, (lanes, tile), 0).astype(f32).astype(bf16)
        at_lower, at_upper = [cells == (normal + n).astype(f32).astype(bf16) for n in range(2)]
        (lower_high, lower_low), (upper_high, upper_low) = split_two(1.0 - f2), split_two(f2)
        high = jnp.where(at_lower, lower_high, jnp.where(at_upper, upper_high, zero))
        low = jnp.where(at_lower, lower_low, jnp.where(at_upper, upper_low, zero))
        return span, f0, jnp.concatenate([high, high, low], axis=0), weights(rows, wrap, f1)

    def add_planes(k, number, made, sums):
        span, f0, along, across = made
        from_row = pl.ds(pl.multiple_of(k * 5 * rows, 16), number * 5 * rows)
        mixed = jnp.dot(planes[from_row, :], along, preferred_element_type=f32)
        new = list(sums)
        for n in range(number):
            ws = jnp.where(span == k + n, 1.0 - f0, jnp.where(span + 1 == k + n, f0, 0.0))
            for c in range(5):
                r0 = (5 * n + c) * rows
                total = mixed[r0 : r0 + 8] * across[0:8]
                for r in range(8, rows, 8):
                    total += mixed[r0 + r : r0 + r + 8] * across[r : r + 8]
                new[c] = ws * total if new[c] is None else new[c] + ws * total
        return tuple(new)

    def lowest_of(i):
        return jnp.minimum(first[i, 0], spans - 3)

    def step(g, _):
        for n in range(GROUP):
            i = g * GROUP + n
            for c, x in enumerate(add_planes(lowest_of(i), 3, tile_of(i), (None,) * 5)):
                partial[n, c] = x
        for n in range(GROUP):
            i = g * GROUP + n
            lowest = lowest_of(i)
            more = first[i, tile - 1] - 1 - lowest

            @pl.when(more > 0)
            def _():
                made = tile_of(i)

                def again(m, _):
                    sums = add_planes(lowest + 3 + m, 1, made, tuple(partial[n, c] for c in range(5)))
                    for c in range(5):
                        partial[n, c] = sums[c]
                    return 0

                lax.fori_loop(0, more, again, 0)

        for n in range(GROUP):
            i = g * GROUP + n
            for c in range(5):
                table[pl.ds(c * tiles + i, 1), :] = jnp.sum(partial[n, c], axis=0, keepdims=True)
        return 0

    lax.fori_loop(0, tiles // GROUP, step, 0)

    add_remainders(table)
    both = table[...].astype(bf16)

    def put_back(w, _):
        for t in range(0, slots, 512):
            for c, value in enumerate(lookup(both, rank_ref[pl.ds(w, 1), t : t + 512])):
                out_ref[w, c : c + 1, t : t + 512] = value
        return 0

    lax.fori_loop(0, count, put_back, 0, unroll=8)


def donors(cell, frac, state):
    _, spans, rows, lanes = state.shape
    count, slots = cell.shape
    tiles = count * slots // 256
    shapes = [(count, 5, slots)]
    shapes += [(5, 2, spans, lanes)] * 2 + [(5, 2, rows, lanes)] * 2 + [(5, rows, 2 * spans)]
    return pl.pallas_call(
        donor_kernel,
        grid=(1,),
        in_specs=[IN_VMEM, IN_VMEM, IN_HBM],
        out_specs=[whole(x) for x in shapes],
        out_shape=[jax.ShapeDtypeStruct(x, f32) for x in shapes],
        scratch_shapes=[
            pltpu.VMEM(state.shape, f32),
            pltpu.VMEM((spans * 5 * rows, 3 * lanes), bf16),
            pltpu.VMEM((9, count, slots), f32),
            pltpu.VMEM((count, slots), i32),
            pltpu.VMEM((9 * tiles, 256), f32),
            pltpu.VMEM((tiles, 256), i32),
            pltpu.SMEM((tiles, 256), i32),
            pltpu.VMEM((GROUP, 5, 8, 256), f32),
            pltpu.VMEM((10 * tiles, 256), f32),
            pltpu.SemaphoreType.DMA((2,)),
        ],
        compiler_params=params(60 * 1024 * 1024),
        name="donors",
    )(cell, frac, state)


def fill_kernel(
    from_ref,
    mask_ref,
    q_hbm,
    slot_ref,
    out_ref,
    norm_lo,
    norm_hi,
    span_lo,
    span_hi,
    table,
    spread,
    q_ref,
    sems,
):
    planes = pl.num_programs(0)
    rows, lanes = from_ref.shape[1:]
    count, _, slots = slot_ref.shape
    j = pl.program_id(0)

    def fetch(n):
        return pltpu.make_async_copy(q_hbm.at[:, n], q_ref.at[:, n], sems.at[n])

    @pl.when(j == 0)
    def _():
        for n in range(q_ref.shape[1]):
            fetch(n).start()
        per = slots // 256
        for c in range(4):
            for w in range(count):
                for r in range(per):
                    at = c * count * per + w * per + r
                    table[at : at + 1, :] = slot_ref[w, c : c + 1, r * 256 : (r + 1) * 256]
        add_remainders(table)
        for w in range(count):
            for r in range(slots // 128):
                value = slot_ref[w, 4:5, r * 128 : (r + 1) * 128]
                spread[w * (slots // 128) + r] = jnp.broadcast_to(value, (8, 128))

    fetch(j).wait()
    both = table[...].astype(bf16)
    lines = spread.shape[0]
    share = (rows // 8) * (lanes // 128) * lines // rows
    value = None
    for s in range(rows):
        keep = mask_ref[0, s : s + 1, :] == 1
        for c, found in enumerate(lookup(both, from_ref[0, s : s + 1, :])):
            out_ref[c, 0, s : s + 1, :] = jnp.where(keep, q_ref[c, j, s : s + 1, :], found)
        for n in range(s * share, (s + 1) * share):
            line = n % lines
            if line == 0:
                row, lane = divmod(n // lines, lanes // 128)
                here = (slice(8 * row, 8 * row + 8), slice(128 * lane, 128 * lane + 128))
                at = from_ref[0, here[0], here[1]]
                low, high = at & 127, at // 128
                value = jnp.zeros((8, 128), f32)
            value = jnp.where(high == line, take_lanes(spread[line], low), value)
            if line == lines - 1:
                keep = mask_ref[0, here[0], here[1]] == 1
                out_ref[4, 0, here[0], here[1]] = jnp.where(keep, q_ref[4, j, here[0], here[1]], value)

    for c in range(5):
        for l in range(2):
            span_lo[c, l, pl.ds(j, 1), :] = out_ref[c, 0, l : l + 1, :]
            span_hi[c, l, pl.ds(j, 1), :] = out_ref[c, 0, rows - 2 + l : rows - 1 + l, :]

    @pl.when(j < 2)
    def _():
        for c in range(5):
            norm_lo[c, j] = out_ref[c, 0]

    @pl.when(j >= planes - 2)
    def _():
        for c in range(5):
            norm_hi[c, j - (planes - 2)] = out_ref[c, 0]


def fill(source, mask, state, slot):
    _, planes, rows, lanes = state.shape
    count, _, slots = slot.shape
    plane = pl.BlockSpec((1, rows, lanes), lambda j: (j, 0, 0))
    state_plane = pl.BlockSpec((5, 1, rows, lanes), lambda j: (0, j, 0, 0))
    edges = [(5, 2, rows, lanes)] * 2 + [(5, 2, planes, lanes)] * 2
    return pl.pallas_call(
        fill_kernel,
        grid=(planes,),
        in_specs=[plane, plane, IN_HBM, IN_VMEM],
        out_specs=[state_plane] + [whole(s) for s in edges],
        out_shape=[jax.ShapeDtypeStruct(s, f32) for s in [state.shape] + edges],
        scratch_shapes=[
            pltpu.VMEM((8 * count * slots // 256, 256), f32),
            pltpu.VMEM((count * slots // 128, 8, 128), f32),
            pltpu.VMEM(state.shape, f32),
            pltpu.SemaphoreType.DMA((planes,)),
        ],
        compiler_params=params(49 * 1024 * 1024),
        cost_estimate=pl.CostEstimate(flops=24 * 10**9, bytes_accessed=6 * 10**6, transcendentals=0),
        name="fill",
    )(source, mask, state, slot)


def body(
    cgrid_state, cgrid_metric, flap_state, flap_metric, iblank, fringe_from, donor_cell, donor_frac
):
    wrap_count = lax.axis_size("wrap")

    def ring(axis):
        size = lax.axis_size(axis)
        return [(i, (i + 1) % size) for i in range(size)]

    def onward(value, axis):
        return lax.ppermute(value, axis, ring(axis))

    def back(value, axis):
        return lax.ppermute(value, axis, [(j, i) for i, j in ring(axis)])

    slot, wrap_lo, wrap_hi, span_lo, span_hi, wall = donors(
        donor_cell[0], jnp.transpose(donor_frac[0], (1, 0, 2)), cgrid_state
    )
    far = lax.ppermute(
        wall,
        "wrap",
        [(i, wrap_count - 1 - i if wrapped(i, wrap_count) else i) for i in range(wrap_count)],
    )
    majors = (onward(span_hi, "span"), back(span_lo, "span"))
    subs = (onward(wrap_hi, "wrap"), back(wrap_lo, "wrap"))

    slot = lax.all_to_all(slot, "wrap", split_axis=0, concat_axis=0, tiled=True)

    turned = lambda x: jnp.swapaxes(x, -3, -2)
    mask = turned(iblank)
    filled, norm_lo, norm_hi, edge_lo, edge_hi = fill(turned(fringe_from), mask, turned(flap_state), slot)
    flap_majors = (onward(norm_hi, "wrap"), back(norm_lo, "wrap"))
    flap_subs = (onward(edge_hi, "span"), back(edge_lo, "span"))

    cgrid_rate = rate(
        cgrid_state,
        majors,
        subs,
        (wrap_lo, wrap_hi, wall, far),
        cgrid_metric,
        None,
        cgrid=True,
        step_planes=4,
        components=(3, 1, 2),
        metric_rows=(0, 1, 2),
    )
    flap_rate = rate(
        filled,
        flap_majors,
        flap_subs,
        (),
        turned(flap_metric),
        mask,
        cgrid=False,
        step_planes=4,
        components=(2, 3, 1),
        metric_rows=(1, 0, 2),
    )
    return (cgrid_rate, turned(flap_rate))


def solution(mesh):
    return jax.shard_map(
        body,
        mesh=mesh,
        in_specs=(
            P(None, "span", "wrap", None),
            P(None, "span", "wrap", None),
            P(None, "span", "wrap", None),
            P(None, "span", "wrap", None),
            P("span", "wrap", None),
            P("span", "wrap", None),
            P(("wrap", "span"), None, None),
            P(("wrap", "span"), None, None, None),
        ),
        out_specs=(P(None, "span", "wrap", None), P(None, "span", "wrap", None)),
        check_vma=False,
    )
```
